128 devices in a mesh: seg: 32 (over z, x, y_hi), span: 4 (over y_lo, core).
Axes of the slice: x: 4, y: 4 (y_hi: 2, y_lo: 2; y = y_hi * 2 + y_lo), z: 4, core: 2. Of those that a mesh axis runs over, the one named last changes fastest.
Arguments:
- inputs: bfloat16 [16384, 2048], P(('seg', 'span')), may hold values from -6 to 6
- cotangent: bfloat16 [16384, 2048], P(('seg', 'span')), may hold values from -6 to 6
- states: float32 [32, 32, 64, 64], P('seg', 'span'), may hold values from -4 to 4
- vectors: bfloat16 [16, 2048], P(None, ('seg', 'span')), may hold values from -7.5 to 1.3, as said below
- time_mix_weight: bfloat16 [4, 2048, 2048], P(None, 'seg', 'span'), may hold values from -0.125 to 0.125
- output_weight: bfloat16 [2048, 2048], P('span', 'seg'), may hold values from -0.125 to 0.125
- channel_receptance_weight: bfloat16 [2048, 2048], P(('seg', 'span')), may hold values from -0.125 to 0.125
- rank_down_weight: bfloat16 [2048, 224], P(('seg', 'span')), may hold values from -0.125 to 0.125
- rank_up_weight: bfloat16 [224, 2048], P(None, ('seg', 'span')), may hold values from -0.35 to 0.35
- channel_key_weight: bfloat16 [2048, 7168], P('seg', 'span'), may hold values from -0.125 to 0.125
- channel_value_weight: bfloat16 [7168, 2048], P('span', 'seg'), may hold values from -0.0625 to 0.0625
Outputs:
- output: bfloat16 [16384, 2048], P(('seg', 'span'))
- x_grad: float32 [16384, 2048], P(('seg', 'span'))
- state_grad: float32 [32, 32, 64, 64], P('seg', 'span')
- vectors_grad: float32 [16, 2048], P(None, ('seg', 'span'))
- time_proj_grad: float32 [4, 2048, 2048], P(None, 'seg', 'span')
- out_proj_grad: float32 [2048, 2048], P('span', 'seg')
- cm_recept_grad: float32 [2048, 2048], P(('seg', 'span'))
- lora_down_grad: float32 [2048, 224], P(('seg', 'span'))
- lora_up_grad: float32 [224, 2048], P(None, ('seg', 'span'))
- cm_key_grad: float32 [2048, 7168], P('seg', 'span')
- cm_value_grad: float32 [7168, 2048], P('span', 'seg')
The draws below stay inside these ranges and needn't reach their ends.
Inputs may be any that keep to these rules, and one draw needn't show every extreme that they name: `vectors`: rows 0, 10, 12 are gains in [0.7, 1.3]; rows 1, 11, 13 offsets in [-0.2, 0.2]; rows 2 to 7, 14, 15 blend weights in [0, 1]; row 8 decay exponents of at most -1; row 9 bonuses in [-1, 1].
All inputs are finite; a program needn't handle non-finite values.
Results may differ from the reference program's by a relative error of at most 0.033.
Values may be sent and summed in bfloat16 or wider, within the bound.
No kernel may reach another device: no remote copies, remote signals or barrier semaphores. Data moves between devices by JAX's collectives and lax.ppermute only.
A program may use at most 384 MiB of HBM per device.

```python
from functools import partial
import jax
import jax.numpy as jnp
from jax import lax

MODEL_WIDTH = 2048
FF = 7168
GROUP_DIMENSION = 64
SHIFT_RANK = 32
DECAY_RANK = 64
H = 32
NSEG = 32
TOKENS = 16384


def draw_vectors(key, part):
    group_count = MODEL_WIDTH // GROUP_DIMENSION
    key_list = jax.random.split(key, 3)
    starting_amount = jax.random.uniform(key_list[0], (16, MODEL_WIDTH), jnp.float32)
    normalizer_scales = 0.7 + 0.6 * starting_amount
    piece_starts = -0.2 + 0.4 * starting_amount
    head_rate = jax.random.uniform(key_list[1], (group_count, 1), jnp.float32, -7.0, -1.5)
    channel_rate = jax.random.uniform(key_list[2], (group_count, GROUP_DIMENSION), jnp.float32, -0.5, 0.5)
    fading_default_line = (head_rate + channel_rate).reshape(MODEL_WIDTH)
    reward_coefficient_line = -1.0 + 2.0 * starting_amount[9]
    emitted_lines = [normalizer_scales[0], piece_starts[1], starting_amount[2], starting_amount[3], starting_amount[4], starting_amount[5], starting_amount[6], starting_amount[7], fading_default_line, reward_coefficient_line, normalizer_scales[10], piece_starts[11], normalizer_scales[12], piece_starts[13], starting_amount[14], starting_amount[15]]
    return jnp.stack(emitted_lines).astype(jnp.bfloat16)


def draw_rank_up_weight(key, part):
    key_list = jax.random.split(key, 2)
    shift_rows = jax.random.uniform(key_list[0], (5 * SHIFT_RANK, MODEL_WIDTH), jnp.float32, -0.03, 0.03)
    decay_rows = jax.random.uniform(key_list[1], (DECAY_RANK, MODEL_WIDTH), jnp.float32, -0.35, 0.35)
    return jnp.concatenate([shift_rows, decay_rows], axis=0).astype(jnp.bfloat16)


def block_scale(own_key, shape, shards, smallest, largest):
    level, own = 1.0, jax.random.fold_in(own_key, 6)
    for dim, blocks in shards:
        heights = jnp.exp(jax.random.uniform(jax.random.fold_in(own, dim), (blocks,), jnp.float32, smallest / len(shards), largest / len(shards)))
        level = level * jnp.repeat(heights, shape[dim] // blocks).reshape([-1 if axis == dim else 1 for axis in range(len(shape))])
    return level


def scatter_about(rng, dims, scale, reach, shards=(), dtype=jnp.bfloat16):
    entries = scale * jax.random.normal(rng, dims, jnp.float32)
    if shards:
        entries = entries * block_scale(rng, dims, shards, -0.22, 0.18)
    return jnp.clip(entries, -reach, reach).astype(dtype)


def setup_inputs(seed: int = 0) -> dict:
    arg_keys = jax.random.split(jax.random.key(seed), 12)
    inputs = scatter_about(arg_keys[0], (TOKENS, MODEL_WIDTH), 1.0, 6.0, ((0, 128),))
    cotangent = scatter_about(arg_keys[1], (TOKENS, MODEL_WIDTH), 1.0, 6.0, ((0, 128),))
    states = scatter_about(arg_keys[2], (NSEG, H, GROUP_DIMENSION, GROUP_DIMENSION), 0.5, 4.0, ((0, 32), (1, 4)), jnp.float32)
    vectors = draw_vectors(jax.random.fold_in(arg_keys[11], 71), 0)
    time_mix_weight = scatter_about(arg_keys[4], (4, MODEL_WIDTH, MODEL_WIDTH), MODEL_WIDTH ** -0.5, 0.125, ((1, 32), (2, 4)))
    output_weight = scatter_about(arg_keys[5], (MODEL_WIDTH, MODEL_WIDTH), MODEL_WIDTH ** -0.5, 0.125, ((0, 4), (1, 32)))
    channel_receptance_weight = scatter_about(arg_keys[6], (MODEL_WIDTH, MODEL_WIDTH), MODEL_WIDTH ** -0.5, 0.125, ((0, 128),))
    rank_down_weight = scatter_about(arg_keys[7], (MODEL_WIDTH, 5 * SHIFT_RANK + DECAY_RANK), MODEL_WIDTH ** -0.5, 0.125, ((0, 128),))
    rank_up_weight = draw_rank_up_weight(jax.random.fold_in(arg_keys[11], 71), 0)
    channel_key_weight = scatter_about(arg_keys[9], (MODEL_WIDTH, FF), MODEL_WIDTH ** -0.5, 0.125, ((0, 32), (1, 4)))
    channel_value_weight = scatter_about(arg_keys[10], (FF, MODEL_WIDTH), FF ** -0.5, 0.0625, ((0, 4), (1, 32)))
    return dict(inputs=inputs, cotangent=cotangent, states=states, vectors=vectors, time_mix_weight=time_mix_weight, output_weight=output_weight, channel_receptance_weight=channel_receptance_weight, rank_down_weight=rank_down_weight, rank_up_weight=rank_up_weight, channel_key_weight=channel_key_weight, channel_value_weight=channel_value_weight)


@jax.custom_vjp
def low(v):
    return lax.optimization_barrier(v.astype(jnp.bfloat16)).astype(jnp.float32)

@jax.custom_vjp
def low_back(v):
    return v

def low_keep(v):
    return (low(v), None)

def low_pass(kept, grad):
    return (grad,)

def back_keep(v):
    return (v, None)

def back_low(kept, grad):
    return (low(grad),)
low.defvjp(low_keep, low_pass)
low_back.defvjp(back_keep, back_low)
maximal_accuracy = lax.Precision.HIGHEST
ln_eps = 1e-05
gn_eps = 0.00064

def product_highest(left_arg, right_arg):
    return jnp.dot(left_arg, right_arg, precision=maximal_accuracy, preferred_element_type=jnp.float32)

def layer_norm(values, gain_vec, offset):
    centre = values - lax.optimization_barrier(jnp.mean(values, -1, keepdims=True))
    return centre * lax.rsqrt(lax.optimization_barrier(jnp.mean(centre * centre, -1, keepdims=True)) + ln_eps) * gain_vec + offset

def shift_tokens(values, segments):
    token_rows, embedding_dimension = values.shape
    grid = values.reshape(segments, token_rows // segments, embedding_dimension)
    prior = jnp.concatenate([jnp.zeros((segments, 1, embedding_dimension), jnp.float32), grid[:, :-1]], axis=1)
    return prior.reshape(token_rows, embedding_dimension) - values

def attention_sum_tile(reward_array, transported_memory, argument_tile):

    def token_step(present_memory, block_item):
        acceptance_each_moment, key_t, val_t, dec_t = block_item
        address_content_dyad = key_t[:, :, None] * val_t[:, None, :]
        emitted_each_moment = jnp.einsum('fr,frz->fz', acceptance_each_moment, present_memory + reward_array[:, :, None] * address_content_dyad, precision=maximal_accuracy)
        return (dec_t[:, :, None] * present_memory + address_content_dyad, emitted_each_moment)
    return lax.scan(token_step, transported_memory, argument_tile)

def attention_sum_piece(acceptance_lines, address_mapped, content_mapped, fading_multiplier, starting_memory, reward_array):
    block_count = acceptance_lines.shape[0] // 32
    blocks = tuple((input_tensor.reshape(block_count, 32, input_tensor.shape[1], input_tensor.shape[2]) for input_tensor in (acceptance_lines, address_mapped, content_mapped, fading_multiplier)))
    recurrence_update = jax.checkpoint(partial(attention_sum_tile, reward_array))
    final_state, outs = lax.scan(recurrence_update, starting_memory, blocks)
    return outs.reshape(acceptance_lines.shape)

def forward_block(inputs, states, vectors, time_mix_weight, output_weight, channel_receptance_weight, rank_down_weight, rank_up_weight, channel_key_weight, channel_value_weight):
    token_rows, embedding_dimension = inputs.shape
    segments = states.shape[0]
    group_count = embedding_dimension // GROUP_DIMENSION
    rank_columns = 5 * SHIFT_RANK
    normed = layer_norm(inputs, vectors[0], vectors[1])
    shifted = shift_tokens(normed, segments)
    mixed_input = low(normed + shifted * vectors[2])
    hidden_rows = low_back(product_highest(mixed_input, rank_down_weight[:, :rank_columns]))
    squash_values = low(jnp.tanh(hidden_rows)).reshape(token_rows, 5, SHIFT_RANK)
    modulation_terms = low_back(jnp.einsum('spi,pif->psf', squash_values, rank_up_weight[:rank_columns].reshape(5, SHIFT_RANK, embedding_dimension), precision=maximal_accuracy))
    shift_mixes = [low(normed + shifted * (vectors[3 + group_id] + modulation_terms[group_id])) for group_id in range(5)]
    acceptance_lines = low_back(product_highest(shift_mixes[3], time_mix_weight[0]))
    address_mapped = low_back(product_highest(shift_mixes[1], time_mix_weight[1]))
    content_mapped = low_back(product_highest(shift_mixes[2], time_mix_weight[2]))
    gate_act = jax.nn.silu(low_back(product_highest(shift_mixes[4], time_mix_weight[3])))
    decay_low_rank = low(jnp.tanh(low_back(product_highest(shift_mixes[0], rank_down_weight[:, rank_columns:]))))
    logged_fading = -jnp.exp(vectors[8] + low_back(product_highest(decay_low_rank, rank_up_weight[rank_columns:])))

    def per_segment(input_tensor):
        return input_tensor.reshape(segments, token_rows // segments, group_count, GROUP_DIMENSION)
    weighted_kv = jax.vmap(attention_sum_piece, in_axes=(0, 0, 0, 0, 0, None))(per_segment(acceptance_lines), per_segment(address_mapped), per_segment(content_mapped), per_segment(jnp.exp(logged_fading)), states, vectors[9].reshape(group_count, GROUP_DIMENSION))
    weighted_kv = weighted_kv.reshape(token_rows, group_count, GROUP_DIMENSION)
    centre = weighted_kv - lax.optimization_barrier(jnp.mean(weighted_kv, -1, keepdims=True))
    unit_gn = centre * lax.rsqrt(lax.optimization_barrier(jnp.mean(centre * centre, -1, keepdims=True)) + gn_eps)
    grouped = unit_gn.reshape(token_rows, embedding_dimension) * vectors[10] + vectors[11]
    mixed = low(grouped * gate_act)
    resid = inputs + low_back(product_highest(mixed, output_weight))
    normed_two = layer_norm(resid, vectors[12], vectors[13])
    shifted_two = shift_tokens(normed_two, segments)
    key_in = low(normed_two + shifted_two * vectors[14])
    rec_in = low(normed_two + shifted_two * vectors[15])
    hidden_two = low_back(product_highest(key_in, channel_key_weight))
    squared = low(jnp.square(jax.nn.relu(hidden_two)))
    value_out = low_back(product_highest(squared, channel_value_weight))
    return resid + jax.nn.sigmoid(low_back(product_highest(rec_in, channel_receptance_weight))) * value_out

def reference(inputs, cotangent, states, vectors, time_mix_weight, output_weight, channel_receptance_weight, rank_down_weight, rank_up_weight, channel_key_weight, channel_value_weight):
    primal_inputs = tuple((input_tensor.astype(jnp.float32) for input_tensor in (inputs, states, vectors, time_mix_weight, output_weight, channel_receptance_weight, rank_down_weight, rank_up_weight, channel_key_weight, channel_value_weight)))
    final_result, pullback_function = jax.vjp(forward_block, *primal_inputs)
    grads = pullback_function(cotangent.astype(jnp.float32))
    return (final_result.astype(jnp.bfloat16), grads[0], grads[1], grads[2], grads[3], grads[4], grads[5], grads[6], grads[7], grads[8], grads[9])
```

```python
import jax
import jax.numpy as jnp
from jax import lax
from jax.sharding import PartitionSpec as P

GROUP_DIMENSION = 64
SHIFT_RANK = 32
ALL = ("seg", "span")

maximal_accuracy = lax.Precision.HIGHEST
ln_eps = 1e-05
gn_eps = 0.00064


def swap(block, bit):
    count = lax.axis_size("seg") * lax.axis_size("span")
    return lax.ppermute(block, ALL, [(i, i ^ bit) for i in range(count)])


def swap_core(block):
    return swap(block, 1)


def swap_low(block):
    return swap(block, 2)


def swap_high(block):
    return swap(block, 4)


def plane_groups():
    half = lax.axis_size("seg") // 2
    return [[2 * j + h for j in range(half)] for h in range(2)]


def in_order(own, other, second):
    return jnp.where(second, other, own), jnp.where(second, own, other)


def span_gather(block):
    place = lax.axis_index("span")
    low, core = place // 2, place % 2
    p0, p1 = in_order(block, swap_low(block), low == 1)
    q = swap_core(jnp.stack([p0, p1]))
    a0, a1 = in_order(p0, q[0], core == 1)
    b0, b1 = in_order(p1, q[1], core == 1)
    return jnp.concatenate([a0, a1, b0, b1], axis=0)


def span_reduce(part):
    place = lax.axis_index("span")
    low, core = place // 2, place % 2
    rows = part.shape[0] // 4
    b = part.reshape(2, 2, rows, part.shape[1])
    keep = jnp.where(core == 1, b[:, 1], b[:, 0])
    send = jnp.where(core == 1, b[:, 0], b[:, 1]).astype(jnp.bfloat16)
    got = swap_core(send)
    both = keep.astype(jnp.float32) + got.astype(jnp.float32)
    mine = jnp.where(low == 1, both[1], both[0])
    send = jnp.where(low == 1, both[0], both[1]).astype(jnp.bfloat16)
    return mine + swap_low(send).astype(jnp.float32)


def plane_gather(block):
    high = lax.axis_index("seg") % 2
    first, second = in_order(block, swap_high(block), high == 1)
    return lax.all_gather(
        jnp.concatenate([first, second], axis=0),
        "seg",
        axis=0,
        tiled=True,
        axis_index_groups=plane_groups(),
    )


def plane_reduce(part):
    high = lax.axis_index("seg") % 2
    pair = lax.psum_scatter(
        part, "seg", scatter_dimension=0, tiled=True, axis_index_groups=plane_groups()
    )
    rows = pair.shape[0] // 2
    mine = jnp.where(high == 1, pair[rows:], pair[:rows])
    send = jnp.where(high == 1, pair[:rows], pair[rows:])
    return mine.astype(jnp.float32) + swap_high(send).astype(jnp.float32)


def split_columns(block):
    place = lax.axis_index("span")
    n = block.shape[1] // 4

    def columns(at):
        return lax.dynamic_slice_in_dim(block, at * n, n, 1)

    pieces = [columns(place)] + [swap(columns(place ^ bit), bit) for bit in (1, 2, 3)]
    result = jnp.zeros((4, block.shape[0], n), block.dtype)
    for bit, piece in enumerate(pieces):
        result = lax.dynamic_update_index_in_dim(result, piece, place ^ bit, 0)
    return result.reshape(4 * block.shape[0], n)


def join_columns(block):
    place = lax.axis_index("span")
    r, n = block.shape[0] // 4, block.shape[1]

    def rows(at):
        return lax.dynamic_slice_in_dim(block, at * r, r, 0)

    result = jnp.zeros((r, 4 * n), block.dtype)
    for bit in range(4):
        piece = rows(place ^ bit)
        if bit:
            piece = swap(piece, bit)
        result = lax.dynamic_update_slice_in_dim(result, piece, (place ^ bit) * n, 1)
    return result


def product_lower(left_arg, right_arg):
    return jnp.dot(left_arg, right_arg, preferred_element_type=jnp.float32)


def outer_sum(left_arg, right_arg):
    return jnp.einsum("td,te->de", left_arg, right_arg, preferred_element_type=jnp.float32)


def backward_product(gradient, weights):
    return jnp.einsum("te,de->td", gradient, weights, preferred_element_type=jnp.float32)


def norm_rows(values, gain_vec, offset):
    centre = values - jnp.mean(values, -1, keepdims=True)
    row_rstd = lax.rsqrt(jnp.mean(centre * centre, -1, keepdims=True) + ln_eps)
    unit_rows = centre * row_rstd
    return (unit_rows * gain_vec + offset, unit_rows, row_rstd)


def norm_back(gradient, unit_rows, row_rstd, gain_vec):
    scaled = gradient * gain_vec
    return row_rstd * (
        scaled
        - jnp.mean(scaled, -1, keepdims=True)
        - unit_rows * jnp.mean(scaled * unit_rows, -1, keepdims=True)
    )


def prior_rows(values):
    return jnp.concatenate([jnp.zeros_like(values[:1]), values[:-1]], axis=0)


def next_rows(values):
    return jnp.concatenate([values[1:], jnp.zeros_like(values[:1])], axis=0)


def gather_small(block):
    return lax.all_gather(block, ALL, axis=0, tiled=True)


def reduce_small(part):
    count = lax.axis_size("seg") * lax.axis_size("span")
    rows, width = part.shape[0] // count, part.shape[1]
    pieces = part.astype(jnp.bfloat16).reshape(count, rows, width)
    arrived = lax.all_to_all(pieces, ALL, split_axis=0, concat_axis=0, tiled=True)
    return arrived.astype(jnp.float32).sum(axis=0)


def weighted_kv_local(
    acceptance_lines, address_mapped, content_mapped, logged_fading, reward_array, start_state
):
    token_rows, group_count, head_size = acceptance_lines.shape
    block_len = min(64, token_rows)
    block_count = token_rows // block_len

    def to_blocks(input_tensor):
        return input_tensor.reshape(block_count, block_len, group_count, head_size)

    acceptance_tile = to_blocks(acceptance_lines)
    address_tile = to_blocks(address_mapped)
    content_tile = to_blocks(content_mapped)
    dec_blk = to_blocks(logged_fading)
    running = jnp.cumsum(dec_blk, axis=1)
    rec_scaled = acceptance_tile * jnp.exp(running - dec_blk)
    key_scaled = address_tile * jnp.exp(-running)
    scores = jnp.einsum("bthk,bihk->bhti", rec_scaled, key_scaled, precision=maximal_accuracy)
    lower_mask = jnp.arange(block_len)[:, None] > jnp.arange(block_len)[None, :]
    scores = jnp.where(lower_mask, scores, 0.0)
    intra_out = jnp.einsum("bhti,bihv->bthv", scores, content_tile, precision=maximal_accuracy)
    diagonal_term = (
        jnp.sum(acceptance_tile * reward_array * address_tile, axis=-1, keepdims=True)
        * content_tile
    )
    block_total = running[:, -1]
    key_end = address_tile * jnp.exp(block_total[:, None] - running)
    block_state = jnp.einsum("bihk,bihv->bhkv", key_end, content_tile, precision=maximal_accuracy)

    def pass_state(transported_memory, block_item):
        return (
            jnp.exp(block_item[0])[..., None] * transported_memory + block_item[1],
            transported_memory,
        )

    final_state, start_states = lax.scan(pass_state, start_state, (block_total, block_state))
    inter_out = jnp.einsum("bthk,bhkv->bthv", rec_scaled, start_states, precision=maximal_accuracy)
    return (intra_out + diagonal_term + inter_out).reshape(token_rows, group_count, head_size)


def shards(
    inputs,
    cotangent,
    states,
    vectors,
    time_mix_weight,
    output_weight,
    channel_receptance_weight,
    rank_down_weight,
    rank_up_weight,
    channel_key_weight,
    channel_value_weight,
):
    token_rows, width = inputs.shape
    ranks = 5 * SHIFT_RANK
    own_width = time_mix_weight.shape[2]
    hidden = channel_key_weight.shape[1]
    local_heads = own_width // GROUP_DIMENSION
    col_start = lax.axis_index("span") * own_width
    position = lax.axis_index("span") * token_rows

    proj_w = plane_gather(jnp.moveaxis(time_mix_weight, 0, 1).reshape(-1, 4 * own_width))
    key_all = plane_gather(jnp.concatenate([output_weight.T, channel_key_weight], axis=1))
    value_all = plane_gather(
        jnp.concatenate([split_columns(channel_receptance_weight), channel_value_weight.T], axis=1)
    )
    down_weight = gather_small(rank_down_weight)
    up_turned = gather_small(jnp.concatenate([rank_up_weight.T, vectors.T], axis=1))
    up_weight = up_turned[:, : ranks + 64].T
    vec = up_turned[:, ranks + 64 :].T.astype(jnp.float32)

    def own_cols(line):
        return lax.dynamic_slice_in_dim(line, col_start, own_width, line.ndim - 1)

    def own_rows(values):
        return lax.dynamic_slice_in_dim(values, position, token_rows, 0)

    def place_cols(values):
        blank = jnp.zeros(values.shape[:-1] + (width,), jnp.float32)
        return lax.dynamic_update_slice_in_dim(blank, values, col_start, values.ndim - 1)

    def w_proj(g):
        return proj_w[:, g * own_width : (g + 1) * own_width]

    out_w, key_w = key_all[:, :own_width], key_all[:, own_width:]
    recept_w, value_w = value_all[:, :own_width], value_all[:, own_width:]

    x_in = inputs.astype(jnp.float32)
    x_seg = span_gather(inputs).astype(jnp.float32)
    normed, unit_one, _ = norm_rows(x_seg, vec[0], vec[1])
    seg_rows = normed.shape[0]
    head_shape = (seg_rows, local_heads, GROUP_DIMENSION)
    shifted = prior_rows(normed) - normed
    mix_in = (normed + shifted * vec[2]).astype(jnp.bfloat16)
    squash = jnp.tanh(product_lower(mix_in, down_weight[:, :ranks]))
    squash_low = squash.astype(jnp.bfloat16).reshape(seg_rows, 5, SHIFT_RANK)
    up_mods = up_weight[:ranks].reshape(5, SHIFT_RANK, width)
    mods = jnp.einsum("spi,pif->psf", squash_low, up_mods, preferred_element_type=jnp.float32)
    coeffs = [vec[3 + g] + mods[g] for g in range(5)]
    mixes = [(normed + shifted * coeffs[g]).astype(jnp.bfloat16) for g in range(5)]
    recept = product_lower(mixes[3], w_proj(0))
    key_proj = product_lower(mixes[1], w_proj(1))
    val_proj = product_lower(mixes[2], w_proj(2))
    gate_pre = product_lower(mixes[4], w_proj(3))
    gate_act = jax.nn.silu(gate_pre)
    decay_tanh = jnp.tanh(product_lower(mixes[0], down_weight[:, ranks:]))
    decay_low = decay_tanh.astype(jnp.bfloat16)
    up_decay_own = own_cols(up_weight[ranks:])
    log_decay = -jnp.exp(own_cols(vec[8]) + product_lower(decay_low, up_decay_own))
    reward = own_cols(vec[9]).reshape(local_heads, GROUP_DIMENSION)
    wkv, wkv_pullback = jax.vjp(
        weighted_kv_local,
        recept.reshape(head_shape),
        key_proj.reshape(head_shape),
        val_proj.reshape(head_shape),
        log_decay.reshape(head_shape),
        reward,
        states[0],
    )
    centre = wkv - jnp.mean(wkv, -1, keepdims=True)
    gn_rstd = lax.rsqrt(jnp.mean(centre * centre, -1, keepdims=True) + gn_eps)
    gn_unit = centre * gn_rstd
    grouped = gn_unit.reshape(seg_rows, own_width) * own_cols(vec[10]) + own_cols(vec[11])
    mixed = (grouped * gate_act).astype(jnp.bfloat16)
    resid = x_in + span_reduce(backward_product(mixed, out_w).astype(jnp.bfloat16))

    normed_two, unit_two, rstd_two = norm_rows(resid, vec[12], vec[13])
    n2 = span_gather(normed_two.astype(jnp.bfloat16)).astype(jnp.float32)
    shifted_two = prior_rows(n2) - n2
    key_in = (n2 + shifted_two * vec[14]).astype(jnp.bfloat16)
    rec_in = (n2 + shifted_two * vec[15]).astype(jnp.bfloat16)
    hidden_two = product_lower(key_in, key_w)
    active = jax.nn.relu(hidden_two)
    squared = (active * active).astype(jnp.bfloat16)
    value_out = span_reduce(backward_product(squared, value_w).astype(jnp.bfloat16))
    rec_pre = join_columns(product_lower(rec_in, recept_w).astype(jnp.bfloat16))
    rec_gate = jax.nn.sigmoid(rec_pre.astype(jnp.float32))
    output = (resid + rec_gate * value_out).astype(jnp.bfloat16)

    grad_out = cotangent.astype(jnp.float32)
    g_value = (grad_out * rec_gate).astype(jnp.bfloat16)
    g_rec = (grad_out * value_out * rec_gate * (1.0 - rec_gate)).astype(jnp.bfloat16)
    g_value_all = span_gather(g_value)
    g_rec_own = split_columns(g_rec)
    value_part = outer_sum(g_value_all, squared).astype(jnp.bfloat16)
    rec_part = outer_sum(rec_in, g_rec_own).astype(jnp.bfloat16)
    g_hid = (product_lower(g_value_all, value_w) * 2.0 * active).astype(jnp.bfloat16)
    key_part = outer_sum(key_in, g_hid).astype(jnp.bfloat16)
    cm_grad = plane_reduce(jnp.concatenate([rec_part, value_part, key_part], axis=1))
    g_key_in = backward_product(g_hid, key_w)
    g_rec_in = backward_product(g_rec_own, recept_w)
    vec_fourteen = jnp.sum(g_key_in * shifted_two, axis=0)
    vec_fifteen = jnp.sum(g_rec_in * shifted_two, axis=0)
    g_shift_two = g_key_in * vec[14] + g_rec_in * vec[15]
    g_n2_part = g_key_in + g_rec_in - g_shift_two + next_rows(g_shift_two)
    g_n2 = span_reduce(g_n2_part.astype(jnp.bfloat16))
    vec_twelve = jnp.sum(g_n2 * unit_two, axis=0)
    vec_thirteen = jnp.sum(g_n2, axis=0)
    g_resid = grad_out + norm_back(g_n2, unit_two, rstd_two, vec[12])

    g_att = span_gather(g_resid.astype(jnp.bfloat16))
    out_part = outer_sum(g_att, mixed).astype(jnp.bfloat16)
    g_mixed = product_lower(g_att, out_w)
    g_grouped = g_mixed * gate_act
    gate_sig = jax.nn.sigmoid(gate_pre)
    g_gate = (g_mixed * grouped * gate_sig * (1.0 + gate_pre * (1.0 - gate_sig))).astype(jnp.bfloat16)
    vec_ten = jnp.sum(g_grouped * gn_unit.reshape(seg_rows, own_width), axis=0)
    vec_eleven = jnp.sum(g_grouped, axis=0)
    g_unit = (g_grouped * own_cols(vec[10])).reshape(head_shape)
    g_wkv = gn_rstd * (
        g_unit
        - jnp.mean(g_unit, -1, keepdims=True)
        - gn_unit * jnp.mean(g_unit * gn_unit, -1, keepdims=True)
    )
    g_r, g_k, g_v, g_w, g_u, g_start = wkv_pullback(g_wkv)
    state_grad = g_start[None]
    g_recept = g_r.reshape(seg_rows, own_width).astype(jnp.bfloat16)
    g_key = g_k.reshape(seg_rows, own_width).astype(jnp.bfloat16)
    g_val = g_v.reshape(seg_rows, own_width).astype(jnp.bfloat16)
    g_expo = g_w.reshape(seg_rows, own_width) * log_decay
    vec_eight = jnp.sum(g_expo, axis=0)
    g_ww = g_expo.astype(jnp.bfloat16)
    proj_parts = [
        outer_sum(mixes[3], g_recept).astype(jnp.bfloat16),
        outer_sum(mixes[1], g_key).astype(jnp.bfloat16),
        outer_sum(mixes[2], g_val).astype(jnp.bfloat16),
        outer_sum(mixes[4], g_gate).astype(jnp.bfloat16),
    ]
    tm_grad = plane_reduce(jnp.concatenate([out_part] + proj_parts, axis=1))

    up_decay_grad = outer_sum(decay_low, g_ww)
    g_decay_hidden = (
        backward_product(g_ww, up_decay_own) * (1.0 - decay_tanh * decay_tanh)
    ).astype(jnp.bfloat16)
    down_decay_grad = outer_sum(mixes[0], g_decay_hidden)
    g_mix = [
        backward_product(g_decay_hidden, down_weight[:, ranks:]),
        backward_product(g_key, w_proj(1)),
        backward_product(g_val, w_proj(2)),
        backward_product(g_recept, w_proj(0)),
        backward_product(g_gate, w_proj(3)),
    ]
    g_times = [g * shifted for g in g_mix]
    vec_mixes = [jnp.sum(g, axis=0) for g in g_times]
    g_mods = jnp.stack(g_times).astype(jnp.bfloat16)
    up_mods_grad = jnp.einsum(
        "tgj,gtd->gjd", squash_low, g_mods, preferred_element_type=jnp.float32
    ).reshape(ranks, width)
    g_squash = jnp.einsum(
        "gtd,gjd->tgj", g_mods, up_mods, preferred_element_type=jnp.float32
    ).reshape(seg_rows, ranks)
    g_hidden = (g_squash * (1.0 - squash * squash)).astype(jnp.bfloat16)
    down_mods_grad = outer_sum(mix_in, g_hidden)
    g_mix_in = backward_product(g_hidden, down_weight[:, :ranks])
    vec_two = jnp.sum(g_mix_in * shifted, axis=0)
    g_shifted = g_mix_in * vec[2]
    g_normed = g_mix_in
    for g in range(5):
        g_shifted = g_shifted + g_mix[g] * coeffs[g]
        g_normed = g_normed + g_mix[g]
    g_normed = g_normed - g_shifted + next_rows(g_shifted)
    vec_zero = jnp.sum(g_normed * unit_one, axis=0)
    vec_one = jnp.sum(g_normed, axis=0)
    g_n1 = span_reduce(g_normed.astype(jnp.bfloat16))
    _, unit_own, rstd_own = norm_rows(x_in, vec[0], vec[1])
    x_grad = g_resid + norm_back(g_n1, unit_own, rstd_own, vec[0])
    vec_part = jnp.stack(
        [vec_zero, vec_one, vec_two]
        + vec_mixes
        + [
            place_cols(vec_eight),
            place_cols(g_u.reshape(own_width)),
            place_cols(vec_ten),
            place_cols(vec_eleven),
            vec_twelve,
            vec_thirteen,
            vec_fourteen,
            vec_fifteen,
        ]
    )
    up_part = jnp.concatenate([up_mods_grad, place_cols(up_decay_grad)], axis=0)
    small = reduce_small(
        jnp.concatenate([down_mods_grad, down_decay_grad, up_part.T, vec_part.T], axis=1)
    )
    rank_all = ranks + 64
    down_grad, up_grad, vec_grad = (
        small[:, :rank_all],
        small[:, rank_all : 2 * rank_all].T,
        small[:, 2 * rank_all :].T,
    )
    rec_grad = join_columns(cm_grad[:, :own_width])
    value_grad = cm_grad[:, own_width : own_width + hidden].T
    key_grad = cm_grad[:, own_width + hidden :]
    out_grad = tm_grad[:, :own_width].T
    proj_grad = jnp.moveaxis(tm_grad[:, own_width:].reshape(-1, 4, own_width), 1, 0)
    return (
        output,
        x_grad,
        state_grad,
        vec_grad,
        proj_grad,
        out_grad,
        rec_grad,
        down_grad,
        up_grad,
        key_grad,
        value_grad,
    )


def solution(mesh):
    rows, columns = P(ALL, None), P(None, ALL)
    state = P("seg", "span", None, None)
    time_mix = P(None, "seg", "span")
    turned, straight = P("span", "seg"), P("seg", "span")
    return jax.shard_map(
        shards,
        mesh=mesh,
        in_specs=(
            rows, rows, state, columns, time_mix, turned, rows, rows, columns, straight, turned
        ),
        out_specs=(
            rows, rows, state, columns, time_mix, turned, rows, rows, columns, straight, turned
        ),
        check_vma=False,
    )
```

```python
import jax
import jax.numpy as jnp
from jax import lax
from jax.experimental import pallas as pl
from jax.experimental.pallas import tpu as pltpu
from jax.experimental.layout import Layout, with_layout_constraint
from jax.sharding import PartitionSpec as P

GROUP_DIMENSION = 64
SHIFT_RANK = 32
ALL = ("seg", "span")

maximal_accuracy = lax.Precision.HIGHEST
ln_eps = 1e-05
gn_eps = 0.00064


def swap(block, bit):
    count = lax.axis_size("seg") * lax.axis_size("span")
    return lax.ppermute(block, ALL, [(i, i ^ bit) for i in range(count)])


def swap_core(block):
    return swap(block, 1)


def swap_low(block):
    return swap(block, 2)


def swap_high(block):
    return swap(block, 4)


def plane_groups():
    half = lax.axis_size("seg") // 2
    return [[2 * j + h for j in range(half)] for h in range(2)]


def in_order(own, other, second):
    return jnp.where(second, other, own), jnp.where(second, own, other)


def span_gather(block):
    place = lax.axis_index("span")
    low, core = place // 2, place % 2
    p0, p1 = in_order(block, swap_low(block), low == 1)
    q = swap_core(jnp.stack([p0, p1]))
    a0, a1 = in_order(p0, q[0], core == 1)
    b0, b1 = in_order(p1, q[1], core == 1)
    return jnp.concatenate([a0, a1, b0, b1], axis=0)


def span_reduce(part):
    place = lax.axis_index("span")
    low, core = place // 2, place % 2
    rows = part.shape[0] // 4
    b = part.reshape(2, 2, rows, part.shape[1])
    keep = jnp.where(core == 1, b[:, 1], b[:, 0])
    send = jnp.where(core == 1, b[:, 0], b[:, 1]).astype(jnp.bfloat16)
    got = swap_core(send)
    both = keep.astype(jnp.float32) + got.astype(jnp.float32)
    mine = jnp.where(low == 1, both[1], both[0])
    send = jnp.where(low == 1, both[0], both[1]).astype(jnp.bfloat16)
    return mine + swap_low(send).astype(jnp.float32)


def plane_gather(*blocks):
    high = lax.axis_index("seg") % 2
    pairs = [
        jnp.concatenate(in_order(block, swap_high(block), high == 1), axis=0) for block in blocks
    ]
    whole = lax.all_gather(
        jnp.concatenate(pairs, axis=1),
        "seg",
        axis=0,
        tiled=True,
        axis_index_groups=plane_groups(),
    )
    return with_layout_constraint(whole, Layout(major_to_minor=(0, 1)))


def plane_scatter(part):
    return lax.psum_scatter(
        part, "seg", scatter_dimension=0, tiled=True, axis_index_groups=plane_groups()
    )


def finish_scatter(pair):
    high = lax.axis_index("seg") % 2
    rows = pair.shape[0] // 2
    mine = jnp.where(high == 1, pair[rows:], pair[:rows])
    send = jnp.where(high == 1, pair[:rows], pair[rows:])
    return mine.astype(jnp.float32) + swap_high(send).astype(jnp.float32)


def split_columns(block):
    place = lax.axis_index("span")
    n = block.shape[1] // 4

    def columns(at):
        return lax.dynamic_slice_in_dim(block, at * n, n, 1)

    pieces = [columns(place)] + [swap(columns(place ^ bit), bit) for bit in (1, 2, 3)]
    result = jnp.zeros((4, block.shape[0], n), block.dtype)
    for bit, piece in enumerate(pieces):
        result = lax.dynamic_update_index_in_dim(result, piece, place ^ bit, 0)
    return result.reshape(4 * block.shape[0], n)


def join_columns(block):
    place = lax.axis_index("span")
    r, n = block.shape[0] // 4, block.shape[1]

    def rows(at):
        return lax.dynamic_slice_in_dim(block, at * r, r, 0)

    result = jnp.zeros((r, 4 * n), block.dtype)
    for bit in range(4):
        piece = rows(place ^ bit)
        if bit:
            piece = swap(piece, bit)
        result = lax.dynamic_update_slice_in_dim(result, piece, (place ^ bit) * n, 1)
    return result


def product_lower(left_arg, right_arg):
    return jnp.dot(left_arg, right_arg, preferred_element_type=jnp.float32)


def outer_sum(left_arg, right_arg):
    return jnp.einsum("td,te->de", left_arg, right_arg, preferred_element_type=jnp.float32)


def backward_product(gradient, weights):
    return jnp.einsum("te,de->td", gradient, weights, preferred_element_type=jnp.float32)


def norm_rows(values, gain_vec, offset):
    centre = values - jnp.mean(values, -1, keepdims=True)
    row_rstd = lax.rsqrt(jnp.mean(centre * centre, -1, keepdims=True) + ln_eps)
    unit_rows = centre * row_rstd
    return (unit_rows * gain_vec + offset, unit_rows, row_rstd)


def norm_back(gradient, unit_rows, row_rstd, gain_vec):
    scaled = gradient * gain_vec
    return row_rstd * (
        scaled
        - jnp.mean(scaled, -1, keepdims=True)
        - unit_rows * jnp.mean(scaled * unit_rows, -1, keepdims=True)
    )


def prior_rows(values):
    return jnp.concatenate([jnp.zeros_like(values[:1]), values[:-1]], axis=0)


def next_rows(values):
    return jnp.concatenate([values[1:], jnp.zeros_like(values[:1])], axis=0)


def reduce_small(part):
    place, high = lax.axis_index("span"), lax.axis_index("seg") % 2
    planes = lax.axis_size("seg") // 2
    width = part.shape[1]
    b = part.reshape(planes, 2, 2, 2, -1, width)
    for dim, bit, move in ((3, place % 2, swap_core), (2, place // 2, swap_low), (1, high, swap_high)):
        at0, at1 = (lax.index_in_dim(b, k, dim, keepdims=False) for k in (0, 1))
        mine, send = in_order(at0, at1, bit == 1)
        b = mine.astype(jnp.float32) + move(send.astype(jnp.bfloat16)).astype(jnp.float32)
    arrived = lax.all_to_all(
        b.astype(jnp.bfloat16), "seg", split_axis=0, concat_axis=0, tiled=True, axis_index_groups=plane_groups()
    )
    return arrived.astype(jnp.float32).sum(axis=0)


CHUNK = 64
PACK = 256


def mxu(a, b, contract):
    return lax.dot_general(
        a.astype(jnp.bfloat16),
        b.astype(jnp.bfloat16),
        (contract, ((), ())),
        preferred_element_type=jnp.float32,
    )


NN, NT, TN = ((1,), (0,)), ((1,), (1,)), ((0,), (0,))


def halves(values):
    high = values.astype(jnp.bfloat16)
    return high, (values - high.astype(jnp.float32)).astype(jnp.bfloat16)


def iota2(shape, dim):
    return lax.broadcasted_iota(jnp.int32, shape, dim)


def head_ones():
    shape = (PACK, PACK)
    same = iota2(shape, 0) // GROUP_DIMENSION == iota2(shape, 1) // GROUP_DIMENSION
    return jnp.where(same, 1.0, 0.0).astype(jnp.float32)


def spread(block, ones):
    return jnp.concatenate([block] * (PACK // CHUNK), axis=0) * ones


def fold(big, ones):
    kept = big * ones
    total = kept[:CHUNK]
    for h in range(1, PACK // CHUNK):
        total = total + kept[h * CHUNK : (h + 1) * CHUNK]
    return total


def head_sum(values, ones):
    high, rest = halves(values)
    return mxu(high, ones, NN) + mxu(rest, ones, NN)


def run_sum(which, values):
    high, rest = halves(values)
    return mxu(which, high, NN) + mxu(which, rest, NN)


def row_of(values, row):
    return values[row : row + 1]


def piece_factors(run, before):
    rows = iota2((CHUNK, PACK), 0)
    t, i = iota2((CHUNK, PACK), 0), iota2((CHUNK, PACK), 1) % CHUNK
    levels = []
    for half in (32, 16):
        upper = rows % (2 * half) >= half
        reference = jnp.broadcast_to(row_of(run, half - 1), run.shape)
        for start in range(2 * half, CHUNK, 2 * half):
            here = jnp.broadcast_to(row_of(run, start + half - 1), run.shape)
            reference = jnp.where(rows >= start, here, reference)
        scale = jnp.exp(jnp.where(upper, before - reference, reference - run))
        pairs = (t // (2 * half) == i // (2 * half)) & (t % (2 * half) >= half) & (i % (2 * half) < half)
        levels.append((jnp.where(upper, scale, 0.0), jnp.where(upper, 0.0, scale), pairs))
    reference = jnp.broadcast_to(row_of(run, 7), run.shape)
    for start in range(16, CHUNK, 16):
        here = jnp.broadcast_to(row_of(run, start + 7), run.shape)
        reference = jnp.where(rows >= start, here, reference)
    pairs = (t // 16 == i // 16) & (t > i)
    to_row = jnp.exp(jnp.minimum(before - reference, 80.0))
    to_prior = jnp.exp(jnp.minimum(reference - run, 80.0))
    levels.append((to_row, to_prior, pairs))
    return levels


def lower_ones():
    return jnp.where(iota2((CHUNK, CHUNK), 0) >= iota2((CHUNK, CHUNK), 1), 1.0, 0.0).astype(jnp.float32)


def decay_of(low_ref, up_ref, par_ref):
    log_decay = -jnp.exp(par_ref[0:1] + mxu(low_ref[...], up_ref[...], NT))
    run = run_sum(lower_ones(), log_decay)
    return log_decay, run, run - log_decay


def unit_heads(wkv, ones):
    centre = wkv - head_sum(wkv, ones) * (1.0 / GROUP_DIMENSION)
    rstd = lax.rsqrt(head_sum(centre * centre, ones) * (1.0 / GROUP_DIMENSION) + gn_eps)
    return centre * rstd, rstd


def lane_groups(refs, kinds):
    width = refs[0].shape[1]
    for g in range(width // PACK):
        lanes = pl.ds(g * PACK, PACK)
        part = {"c": lambda ref: ref.at[:, lanes], "r": lambda ref: ref.at[lanes], "s": lambda ref: ref.at[g]}
        yield [ref if kind == "w" else part[kind](ref) for ref, kind in zip(refs, kinds)]


def wkv_forward_kernel(*refs):
    for group in lane_groups(refs, "ccccwrcccccs"):
        forward_heads(*group)


def wkv_backward_kernel(*refs):
    for group in lane_groups(refs, "ccccwrccccccccccc" + "s"):
        backward_heads(*group)


def forward_heads(
    r_ref, k_ref, v_ref, gate_ref, low_ref, up_ref, par_ref, first_ref, mixed_ref, wkv_ref, held_ref, state
):
    ones = head_ones()

    @pl.when(pl.program_id(0) == 0)
    def _():
        state[...] = spread(first_ref[...], ones)

    r, k, v = r_ref[...], k_ref[...], v_ref[...]
    _, run, before = decay_of(low_ref, up_ref, par_ref)
    held_ref[...] = fold(state[...], ones)
    score = jnp.zeros((CHUNK, PACK), jnp.float32)
    for to_row, to_prior, pairs in piece_factors(run, before):
        score = jnp.where(pairs, mxu(r * to_row, spread(k * to_prior, ones), NT), score)
    out = mxu(score, spread(v, ones), NN) + mxu(r * jnp.exp(before), state[...], NT)
    out = out + head_sum(r * par_ref[1:2] * k, ones) * v
    wkv_ref[...] = out
    last = row_of(run, CHUNK - 1)
    state[...] = jnp.exp(last) * state[...] + mxu(v, k * jnp.exp(last - run), TN) * ones
    unit, _ = unit_heads(out, ones)
    gate = gate_ref[...]
    mixed_ref[...] = ((unit * par_ref[2:3] + par_ref[3:4]) * gate * jax.nn.sigmoid(gate)).astype(jnp.bfloat16)


def wkv_forward(r, k, v, gate, low, up, par, first):
    rows, columns = r.shape
    chunks = rows // CHUNK
    block = pl.BlockSpec((CHUNK, columns), lambda c: (c, 0))
    whole = lambda a: pl.BlockSpec(a.shape, lambda c: (0, 0))
    return pl.pallas_call(
        wkv_forward_kernel,
        grid=(chunks,),
        in_specs=[block] * 4
        + [
            pl.BlockSpec((CHUNK, low.shape[1]), lambda c: (c, 0)),
            whole(up),
            whole(par),
            whole(first),
        ],
        out_specs=[block, block, block],
        out_shape=[
            jax.ShapeDtypeStruct((rows, columns), jnp.bfloat16),
            jax.ShapeDtypeStruct((rows, columns), jnp.float32),
            jax.ShapeDtypeStruct((rows, columns), jnp.float32),
        ],
        scratch_shapes=[pltpu.VMEM((columns // PACK, PACK, PACK), jnp.float32)],
        compiler_params=pltpu.CompilerParams(
            dimension_semantics=("arbitrary",), vmem_limit_bytes=32 * 2**20
        ),
        cost_estimate=pl.CostEstimate(
            flops=2 * 9 * PACK * rows * columns, bytes_accessed=26 * rows * columns, transcendentals=8 * rows * columns
        ),
        name="wkv_forward",
    )(r, k, v, gate, low, up, par, first)


def backward_heads(
    r_ref, k_ref, v_ref, gate_ref, low_ref, up_ref, par_ref, wkv_ref, held_ref, gm_ref,
    gr_ref, gk_ref, gv_ref, gg_ref, gw_ref, sums_ref, first_ref, state,
):
    ones = head_ones()

    @pl.when(pl.program_id(0) == 0)
    def _():
        state[...] = jnp.zeros_like(state)
        sums_ref[...] = jnp.zeros_like(sums_ref)

    r, k, v, gate = r_ref[...], k_ref[...], v_ref[...], gate_ref[...]
    bonus, gain = par_ref[1:2], par_ref[2:3]

    def add_to(row, values):
        sums_ref[row : row + 1] = sums_ref[row : row + 1] + jnp.sum(values, axis=0, keepdims=True)

    unit, rstd = unit_heads(wkv_ref[...], ones)
    sig = jax.nn.sigmoid(gate)
    g_mixed = gm_ref[...].astype(jnp.float32)
    g_grouped = g_mixed * gate * sig
    grouped = unit * gain + par_ref[3:4]
    gg_ref[...] = (g_mixed * grouped * sig * (1.0 + gate * (1.0 - sig))).astype(jnp.bfloat16)
    add_to(2, g_grouped * unit)
    add_to(3, g_grouped)
    g_unit = g_grouped * gain
    scale = 1.0 / GROUP_DIMENSION
    g_out = rstd * (
        g_unit - head_sum(g_unit, ones) * scale - unit * (head_sum(g_unit * unit, ones) * scale)
    )

    log_decay, run, before = decay_of(low_ref, up_ref, par_ref)
    last = row_of(run, CHUNK - 1)
    start = spread(held_ref[...], ones)
    end_grad = state[...]
    v_wide = spread(v, ones)
    g_score = mxu(g_out, v_wide, NT)
    score = jnp.zeros((CHUNK, PACK), jnp.float32)
    from_start = jnp.exp(before)
    g_r = from_start * mxu(g_out, start, NN)
    to_end = jnp.exp(last - run)
    g_end = to_end * mxu(v, end_grad, NN)
    g_k = g_end
    for to_row, to_prior, pairs in piece_factors(run, before):
        r_level = (r * to_row).astype(jnp.bfloat16)
        k_level = spread(k * to_prior, ones).astype(jnp.bfloat16)
        score = jnp.where(pairs, mxu(r_level, k_level, NT), score)
        g_level = jnp.where(pairs, g_score, 0.0).astype(jnp.bfloat16)
        g_r = g_r + to_row * mxu(g_level, k_level, NN)
        g_k = g_k + to_prior * fold(mxu(g_level, r_level, TN), ones)
    g_v = fold(mxu(score, g_out, TN), ones) + mxu(k * to_end, end_grad, NT)
    g_before = r * g_r
    g_run = g_before - k * g_k
    g_last = jnp.sum(k * g_end, axis=0, keepdims=True) + jnp.exp(last) * jnp.sum(
        start * end_grad, axis=0, keepdims=True
    )
    upper = jnp.where(iota2((CHUNK, CHUNK), 0) <= iota2((CHUNK, CHUNK), 1), 1.0, 0.0).astype(jnp.float32)
    g_decay = run_sum(upper, g_run) - g_before + g_last
    g_expo = g_decay * log_decay
    gw_ref[...] = g_expo.astype(jnp.bfloat16)
    add_to(0, g_expo)
    g_diag = head_sum(g_out * v, ones)
    add_to(1, r * k * g_diag)
    gr_ref[...] = (g_r + bonus * k * g_diag).astype(jnp.bfloat16)
    gk_ref[...] = (g_k + bonus * r * g_diag).astype(jnp.bfloat16)
    gv_ref[...] = (g_v + head_sum(r * bonus * k, ones) * g_out).astype(jnp.bfloat16)
    state[...] = jnp.exp(last) * end_grad + mxu(g_out, r * from_start, TN) * ones

    @pl.when(pl.program_id(0) == pl.num_programs(0) - 1)
    def _():
        first_ref[...] = fold(state[...], ones)


def wkv_backward(r, k, v, gate, low, up, par, wkv, held, g_mixed):
    rows, columns = r.shape
    chunks = rows // CHUNK
    block = pl.BlockSpec((CHUNK, columns), lambda c: (chunks - 1 - c, 0))
    whole = lambda a: pl.BlockSpec(a.shape, lambda c: (0, 0))
    of_all = lambda n: pl.BlockSpec((n, columns), lambda c: (0, 0))
    low_type = jax.ShapeDtypeStruct((rows, columns), jnp.bfloat16)
    return pl.pallas_call(
        wkv_backward_kernel,
        grid=(chunks,),
        in_specs=[block] * 4
        + [
            pl.BlockSpec((CHUNK, low.shape[1]), lambda c: (chunks - 1 - c, 0)),
            whole(up),
            whole(par),
            block,
            block,
            block,
        ],
        out_specs=[block] * 5 + [of_all(8), of_all(GROUP_DIMENSION)],
        out_shape=[low_type] * 5
        + [
            jax.ShapeDtypeStruct((8, columns), jnp.float32),
            jax.ShapeDtypeStruct((GROUP_DIMENSION, columns), jnp.float32),
        ],
        scratch_shapes=[pltpu.VMEM((columns // PACK, PACK, PACK), jnp.float32)],
        compiler_params=pltpu.CompilerParams(
            dimension_semantics=("arbitrary",), vmem_limit_bytes=32 * 2**20
        ),
        cost_estimate=pl.CostEstimate(
            flops=2 * 24 * PACK * rows * columns, bytes_accessed=40 * rows * columns, transcendentals=12 * rows * columns
        ),
        name="wkv_backward",
    )(r, k, v, gate, low, up, par, wkv, held, g_mixed)


GRAD_COLUMNS = 256


def grad_kernel(left_ref, right_ref, *rest):
    out_ref, turned = rest[-2:]

    @pl.when(pl.program_id(0) == 0)
    def _():
        turned[...] = left_ref[...].T

    out_ref[...] = mxu(turned[...], right_ref[...], NN).astype(jnp.bfloat16)


def grad_into(left, right, total, at, into=None):
    rows, width = left.shape
    columns = right.shape[1]
    shift = at // GRAD_COLUMNS
    specs = [
        pl.BlockSpec((rows, width), lambda j: (0, 0)),
        pl.BlockSpec((rows, GRAD_COLUMNS), lambda j: (0, j)),
    ]
    operands = [left, right]
    alias = {}
    if into is not None:
        specs.append(pl.BlockSpec(memory_space=pltpu.HBM))
        operands.append(into)
        alias = {2: 0}
    return pl.pallas_call(
        grad_kernel,
        grid=(columns // GRAD_COLUMNS,),
        in_specs=specs,
        out_specs=pl.BlockSpec((width, GRAD_COLUMNS), lambda j: (0, j + shift)),
        out_shape=pltpu.HBM((width, total), jnp.bfloat16),
        scratch_shapes=[pltpu.VMEM((width, rows), jnp.bfloat16)],
        input_output_aliases=alias,
        compiler_params=pltpu.CompilerParams(
            dimension_semantics=("arbitrary",), vmem_limit_bytes=32 * 2**20
        ),
        cost_estimate=pl.CostEstimate(
            flops=2 * rows * width * columns,
            bytes_accessed=2 * (rows * (width + columns) + width * columns),
            transcendentals=0,
        ),
        name="weight_grad",
    )(*operands)


TILE = 256


def mixes_forward_kernel(
    unit_ref, w_ref, down_ref, up_ref, vec_ref,
    m0_ref, m1_ref, m2_ref, m3_ref, m4_ref, normed_ref, squash_ref, decay_ref, r_ref, k_ref, v_ref, g_ref,
    hidden, decay,
):
    phase, tile = pl.program_id(0), pl.program_id(1)
    rows, ranks = squash_ref.shape
    own = r_ref.shape[1]
    vec = vec_ref[...]
    normed = unit_ref[...] * vec[0:1] + vec[1:2]
    row = iota2(normed.shape, 0)
    shifted = jnp.where(row == 0, 0.0, pltpu.roll(normed, 1, 0)) - normed

    @pl.when((phase == 0) & (tile == 0))
    def _():
        hidden[...] = jnp.zeros_like(hidden)

    @pl.when(phase == 0)
    def _():
        hidden[...] = hidden[...] + mxu(normed + shifted * vec[2:3], down_ref[:, :ranks], NN)

    @pl.when((phase == 1) & (tile == 0))
    def _():
        squash_ref[...] = jnp.tanh(hidden[...])
        decay[...] = jnp.zeros_like(decay)
        for ref in (r_ref, k_ref, v_ref, g_ref):
            ref[...] = jnp.zeros_like(ref)

    @pl.when(phase == 1)
    def _():
        normed_ref[...] = normed
        group_col = iota2((rows, ranks), 1) // SHIFT_RANK
        squash_low = squash_ref[...].astype(jnp.bfloat16)
        up = up_ref[...]
        for g, mix_ref in enumerate((m0_ref, m1_ref, m2_ref, m3_ref, m4_ref)):
            squash_g = jnp.where(group_col == g, squash_low, 0)
            mix = (normed + shifted * (vec[3 + g : 4 + g] + mxu(squash_g, up, NT))).astype(jnp.bfloat16)
            mix_ref[...] = mix
            if g == 0:
                decay[...] = decay[...] + mxu(mix, down_ref[:, ranks:], NN)
            else:
                column = (None, 1, 2, 0, 3)[g] * own
                out = (None, k_ref, v_ref, r_ref, g_ref)[g]
                out[...] = out[...] + mxu(mix, w_ref[:, column : column + own], NN)

    @pl.when((phase == 1) & (tile == pl.num_programs(1) - 1))
    def _():
        decay_ref[...] = jnp.tanh(decay[...])


def mixes_forward(unit, proj_w, down, up_mods, vec, own):
    rows, width = unit.shape
    ranks = up_mods.shape[1]
    low = down.shape[1] - ranks
    tiles = width // TILE
    down_rows = lambda columns: pl.BlockSpec((TILE, columns), lambda p, n: (n, 0))
    across = lambda r: pl.BlockSpec((r, TILE), lambda p, n: (0, n))
    late = pl.BlockSpec((rows, TILE), lambda p, n: (0, n * p))
    whole = lambda columns: pl.BlockSpec((rows, columns), lambda p, n: (0, 0))
    kept = lambda columns, dtype: jax.ShapeDtypeStruct((rows, columns), dtype)
    return pl.pallas_call(
        mixes_forward_kernel,
        grid=(2, tiles),
        in_specs=[
            across(rows),
            pl.BlockSpec((TILE, 4 * own), lambda p, n: (n * p, 0)),
            down_rows(down.shape[1]),
            down_rows(ranks),
            across(vec.shape[0]),
        ],
        out_specs=[late] * 6 + [whole(ranks), whole(low)] + [whole(own)] * 4,
        out_shape=[kept(width, jnp.bfloat16)] * 5
        + [kept(width, jnp.float32), kept(ranks, jnp.float32), kept(low, jnp.float32)]
        + [kept(own, jnp.float32)] * 4,
        scratch_shapes=[pltpu.VMEM((rows, ranks), jnp.float32), pltpu.VMEM((rows, low), jnp.float32)],
        compiler_params=pltpu.CompilerParams(
            dimension_semantics=("arbitrary", "arbitrary"), vmem_limit_bytes=48 * 2**20
        ),
        cost_estimate=pl.CostEstimate(
            flops=2 * rows * width * (4 * own + 7 * ranks),
            bytes_accessed=2 * width * 4 * own + 22 * rows * width,
            transcendentals=0,
        ),
        name="mixes_forward",
    )(unit, proj_w, down, up_mods, vec)


def mixes_back_kernel(
    gk_ref, gv_ref, gr_ref, gg_ref, gd_ref, w_ref, down_ref, up_ref, vec_ref, squash_ref, normed_ref,
    out_ref, down_grad_ref, up_grad_ref, sums_ref,
    g_shift, g_norm, g_squash, g_hidden, g_up, g_sums,
):
    phase, tile = pl.program_id(0), pl.program_id(1)
    rows, ranks = squash_ref.shape
    own = gk_ref.shape[1]
    normed = normed_ref[...]
    row = iota2(normed.shape, 0)
    shifted = jnp.where(row == 0, 0.0, pltpu.roll(normed, 1, 0)) - normed
    squash = squash_ref[...]
    up = up_ref[...]
    vec = vec_ref[...]

    @pl.when((phase == 0) & (tile == 0))
    def _():
        g_squash[...] = jnp.zeros_like(g_squash)

    @pl.when(phase == 0)
    def _():
        group_col = iota2((rows, ranks), 1) // SHIFT_RANK
        group_wide = iota2((TILE, ranks), 1) // SHIFT_RANK
        squash_low = squash.astype(jnp.bfloat16)
        total_shift = jnp.zeros((rows, TILE), jnp.float32)
        total_norm = jnp.zeros((rows, TILE), jnp.float32)
        add_squash = jnp.zeros((rows, ranks), jnp.float32)
        add_up = jnp.zeros((TILE, ranks), jnp.float32)
        sums = []
        for g in range(5):
            squash_g = jnp.where(group_col == g, squash_low, 0)
            up_g = jnp.where(group_wide == g, up, 0)
            if g == 0:
                part = mxu(gd_ref[...], down_ref[:, ranks:], NT)
            else:
                column = (None, 1, 2, 0, 3)[g] * own
                grad = (None, gk_ref, gv_ref, gr_ref, gg_ref)[g]
                part = mxu(grad[...], w_ref[:, column : column + own], NT)
            coeff = vec[3 + g : 4 + g] + mxu(squash_g, up, NT)
            times = part * shifted
            times_low = times.astype(jnp.bfloat16)
            sums.append(jnp.sum(times, axis=0, keepdims=True))
            total_shift = total_shift + part * coeff
            total_norm = total_norm + part
            add_squash = add_squash + mxu(times_low, up_g, NN)
            add_up = add_up + mxu(times_low, squash_g, TN)
        g_shift[tile] = total_shift
        g_norm[tile] = total_norm
        g_squash[...] = g_squash[...] + add_squash
        g_up[tile] = add_up
        g_sums[tile] = jnp.concatenate(sums + [jnp.zeros((3, TILE), jnp.float32)], axis=0)

    @pl.when((phase == 1) & (tile == 0))
    def _():
        g_hidden[...] = (g_squash[...] * (1.0 - squash * squash)).astype(jnp.bfloat16)

    @pl.when(phase == 1)
    def _():
        blend = vec[2:3]
        mix_in = normed + shifted * blend
        part = mxu(g_hidden[...], down_ref[:, :ranks], NT)
        total_shift = g_shift[tile] + part * blend
        total = g_norm[tile] + part - total_shift
        total = total + jnp.where(row == rows - 1, 0.0, pltpu.roll(total_shift, rows - 1, 0))
        out_ref[...] = total.astype(jnp.bfloat16)
        unit = (normed - vec[1:2]) / vec[0:1]
        head = [
            jnp.sum(total * unit, axis=0, keepdims=True),
            jnp.sum(total, axis=0, keepdims=True),
            jnp.sum(part * shifted, axis=0, keepdims=True),
        ]
        sums_ref[...] = jnp.concatenate(head + [g_sums[tile][:5]], axis=0)
        down_grad_ref[...] = mxu(mix_in, g_hidden[...], TN)
        up_grad_ref[...] = g_up[tile]


def mixes_back(g_key, g_val, g_recept, g_gate, g_decay, proj_w, down, up_mods, vec, squash, normed):
    rows, width = normed.shape
    own, ranks = g_key.shape[1], squash.shape[1]
    tiles = width // TILE
    whole = lambda a: pl.BlockSpec(a.shape, lambda p, n: (0, 0))
    down_rows = lambda columns: pl.BlockSpec((TILE, columns), lambda p, n: (n, 0))
    first_only = pl.BlockSpec((TILE, 4 * own), lambda p, n: (n * (1 - p) + (tiles - 1) * p, 0))
    across = lambda r: pl.BlockSpec((r, TILE), lambda p, n: (0, n))
    late = lambda n_rows: pl.BlockSpec((n_rows, TILE), lambda p, n: (0, n * p))
    late_down = lambda columns: pl.BlockSpec((TILE, columns), lambda p, n: (n * p, 0))
    return pl.pallas_call(
        mixes_back_kernel,
        grid=(2, tiles),
        in_specs=[whole(g_key)] * 4
        + [
            whole(g_decay),
            first_only,
            down_rows(down.shape[1]),
            down_rows(ranks),
            across(vec.shape[0]),
            whole(squash),
            across(rows),
        ],
        out_specs=[late(rows), late_down(ranks), late_down(ranks), late(8)],
        out_shape=[
            jax.ShapeDtypeStruct((rows, width), jnp.bfloat16),
            jax.ShapeDtypeStruct((width, ranks), jnp.float32),
            jax.ShapeDtypeStruct((width, ranks), jnp.float32),
            jax.ShapeDtypeStruct((8, width), jnp.float32),
        ],
        scratch_shapes=[
            pltpu.VMEM((tiles, rows, TILE), jnp.float32),
            pltpu.VMEM((tiles, rows, TILE), jnp.float32),
            pltpu.VMEM((rows, ranks), jnp.float32),
            pltpu.VMEM((rows, ranks), jnp.bfloat16),
            pltpu.VMEM((tiles, TILE, ranks), jnp.float32),
            pltpu.VMEM((tiles, 8, TILE), jnp.float32),
        ],
        compiler_params=pltpu.CompilerParams(
            dimension_semantics=("arbitrary", "arbitrary"), vmem_limit_bytes=56 * 2**20
        ),
        cost_estimate=pl.CostEstimate(
            flops=2 * rows * width * (4 * own + 17 * ranks),
            bytes_accessed=2 * width * 4 * own + 10 * rows * width,
            transcendentals=0,
        ),
        name="mixes_back",
    )(g_key, g_val, g_recept, g_gate, g_decay, proj_w, down, up_mods, vec, squash, normed)


def shards(
    inputs,
    cotangent,
    states,
    vectors,
    time_mix_weight,
    output_weight,
    channel_receptance_weight,
    rank_down_weight,
    rank_up_weight,
    channel_key_weight,
    channel_value_weight,
):
    token_rows, width = inputs.shape
    ranks = 5 * SHIFT_RANK
    own_width = time_mix_weight.shape[2]
    hidden = channel_key_weight.shape[1]
    local_heads = own_width // GROUP_DIMENSION
    col_start = lax.axis_index("span") * own_width
    position = lax.axis_index("span") * token_rows

    x_seg = span_gather(inputs).astype(jnp.float32)
    small_rows = span_gather(
        jnp.concatenate([rank_down_weight, rank_up_weight.T, vectors.T], axis=1)
    )
    first = plane_gather(
        jnp.concatenate([time_mix_weight[g] for g in range(4)] + [output_weight.T], axis=1), small_rows
    )
    second = plane_gather(
        jnp.concatenate(
            [channel_key_weight, channel_value_weight.T, split_columns(channel_receptance_weight)], axis=1
        )
    )
    out_w = first[:, 4 * own_width : 5 * own_width]
    low_rank = first[:, 5 * own_width :]
    key_w, value_w, recept_w = second[:, :hidden], second[:, hidden : 2 * hidden], second[:, 2 * hidden :]
    rank_all = rank_down_weight.shape[1]
    down_weight = low_rank[:, :rank_all]
    up_mods, up_decay = low_rank[:, rank_all : rank_all + ranks], low_rank[:, rank_all + ranks : 2 * rank_all]
    vec = low_rank[:, 2 * rank_all :].T.astype(jnp.float32)

    def own_cols(line):
        return lax.dynamic_slice_in_dim(line, col_start, own_width, line.ndim - 1)

    def own_rows(values):
        return lax.dynamic_slice_in_dim(values, position, token_rows, 0)

    def place_rows(values):
        blank = jnp.zeros((width,) + values.shape[1:], jnp.float32)
        return lax.dynamic_update_slice_in_dim(blank, values, col_start, 0)

    x_in = inputs.astype(jnp.float32)
    _, unit_seg, _ = norm_rows(x_seg, 1.0, 0.0)
    *mixes, normed, squash, decay_tanh, recept, key_proj, val_proj, gate_pre = mixes_forward(
        unit_seg, first, down_weight, up_mods, vec, own_width
    )
    decay_low = decay_tanh.astype(jnp.bfloat16)
    up_decay_own = lax.dynamic_slice_in_dim(up_decay, col_start, own_width, 0)
    head_vec = jnp.concatenate([own_cols(vec[8:12]), jnp.zeros((4, own_width), jnp.float32)], axis=0)
    first_state = jnp.transpose(states[0], (2, 0, 1)).reshape(GROUP_DIMENSION, own_width)
    heads_in = (recept, key_proj, val_proj, gate_pre, decay_low, up_decay_own, head_vec)
    mixed, wkv, held = wkv_forward(*heads_in, first_state)
    resid = x_in + span_reduce(backward_product(mixed, out_w).astype(jnp.bfloat16))

    normed_two, unit_two, rstd_two = norm_rows(resid, vec[12], vec[13])
    n2 = span_gather(normed_two.astype(jnp.bfloat16)).astype(jnp.float32)
    shifted_two = prior_rows(n2) - n2
    key_in = (n2 + shifted_two * vec[14]).astype(jnp.bfloat16)
    rec_in = (n2 + shifted_two * vec[15]).astype(jnp.bfloat16)
    hidden_two = product_lower(key_in, key_w)
    active = jax.nn.relu(hidden_two)
    squared = (active * active).astype(jnp.bfloat16)
    rec_part = product_lower(rec_in, recept_w).astype(jnp.bfloat16)
    rec_pre = join_columns(rec_part)
    _, squared = lax.optimization_barrier((rec_part, squared))
    value_part, rec_pre = lax.optimization_barrier(
        (backward_product(squared, value_w).astype(jnp.bfloat16), rec_pre)
    )
    value_out = span_reduce(value_part)
    rec_gate = jax.nn.sigmoid(rec_pre.astype(jnp.float32))
    output = (resid + rec_gate * value_out).astype(jnp.bfloat16)

    grad_out = cotangent.astype(jnp.float32)
    g_value = (grad_out * rec_gate).astype(jnp.bfloat16)
    g_rec = (grad_out * value_out * rec_gate * (1.0 - rec_gate)).astype(jnp.bfloat16)
    g_value_all = span_gather(g_value)
    g_rec_own = split_columns(g_rec)
    cm_total = 2 * hidden
    cm_part = grad_into(g_value_all, squared, cm_total, hidden)
    g_value_all, cm_part = lax.optimization_barrier((g_value_all, cm_part))
    g_hid = (product_lower(g_value_all, value_w) * 2.0 * active).astype(jnp.bfloat16)
    cm_part = grad_into(key_in, g_hid, cm_total, 0, cm_part)
    cm_part, g_hid, g_rec_own = lax.optimization_barrier((cm_part, g_hid, g_rec_own))
    cm_pair = plane_scatter(cm_part)
    g_key_in = backward_product(g_hid, key_w)
    g_rec_in = backward_product(g_rec_own, recept_w)
    vec_fourteen = jnp.sum(g_key_in * shifted_two, axis=0)
    vec_fifteen = jnp.sum(g_rec_in * shifted_two, axis=0)
    g_shift_two = g_key_in * vec[14] + g_rec_in * vec[15]
    g_n2_part = g_key_in + g_rec_in - g_shift_two + next_rows(g_shift_two)
    g_n2 = span_reduce(g_n2_part.astype(jnp.bfloat16))
    vec_twelve = jnp.sum(g_n2 * unit_two, axis=0)
    vec_thirteen = jnp.sum(g_n2, axis=0)
    g_resid = grad_out + norm_back(g_n2, unit_two, rstd_two, vec[12])

    g_att = span_gather(g_resid.astype(jnp.bfloat16))
    g_mixed = product_lower(g_att, out_w)
    g_recept, g_key, g_val, g_gate, g_ww, head_sums, g_first = wkv_backward(
        *heads_in, wkv, held, g_mixed
    )
    state_grad = jnp.transpose(
        g_first.reshape(GROUP_DIMENSION, local_heads, GROUP_DIMENSION), (1, 2, 0)
    )[None]
    tm_total = 6 * own_width
    tm_part = grad_into(g_att, mixed, tm_total, 0)
    tm_part = grad_into(rec_in, g_rec_own, tm_total, 5 * own_width, tm_part)
    for at, mix, grad in ((1, 3, g_recept), (2, 1, g_key), (3, 2, g_val), (4, 4, g_gate)):
        tm_part = grad_into(mixes[mix], grad, tm_total, at * own_width, tm_part)
    g_key, g_ww, tm_part = lax.optimization_barrier((g_key, g_ww, tm_part))

    up_decay_grad = outer_sum(g_ww, decay_low)
    g_decay_hidden = (
        product_lower(g_ww, up_decay_own) * (1.0 - decay_tanh * decay_tanh)
    ).astype(jnp.bfloat16)
    down_decay_grad = outer_sum(mixes[0], g_decay_hidden)
    g_normed, down_mods_grad, up_mods_grad, width_sums = mixes_back(
        g_key, g_val, g_recept, g_gate, g_decay_hidden, first, down_weight, up_mods, vec, squash, normed
    )
    g_normed, cm_pair, tm_part = lax.optimization_barrier((g_normed, cm_pair, tm_part))
    tm_pair = plane_scatter(tm_part)
    cm_grad = finish_scatter(cm_pair)
    tm_grad = finish_scatter(tm_pair)
    g_n1 = span_reduce(g_normed)
    _, unit_own, rstd_own = norm_rows(x_in, vec[0], vec[1])
    x_grad = g_resid + norm_back(g_n1, unit_own, rstd_own, vec[0])
    vec_part = jnp.concatenate(
        [
            width_sums.T,
            place_rows(head_sums[:4].T),
            jnp.stack([vec_twelve, vec_thirteen, vec_fourteen, vec_fifteen]).T,
        ],
        axis=1,
    )
    small = reduce_small(
        jnp.concatenate(
            [down_mods_grad, down_decay_grad, up_mods_grad, place_rows(up_decay_grad), vec_part], axis=1
        )
    )
    down_grad, up_grad, vec_grad = (
        small[:, :rank_all],
        small[:, rank_all : 2 * rank_all].T,
        small[:, 2 * rank_all :].T,
    )
    rec_grad = join_columns(tm_grad[:, 5 * own_width :])
    value_grad = cm_grad[:, hidden:].T
    key_grad = cm_grad[:, :hidden]
    out_grad = tm_grad[:, :own_width].T
    proj_grad = jnp.moveaxis(tm_grad[:, own_width : 5 * own_width].reshape(-1, 4, own_width), 1, 0)
    return (
        output,
        x_grad,
        state_grad,
        vec_grad,
        proj_grad,
        out_grad,
        rec_grad,
        down_grad,
        up_grad,
        key_grad,
        value_grad,
    )


def solution(mesh):
    rows, columns = P(ALL, None), P(None, ALL)
    state = P("seg", "span", None, None)
    time_mix = P(None, "seg", "span")
    turned, straight = P("span", "seg"), P("seg", "span")
    return jax.shard_map(
        shards,
        mesh=mesh,
        in_specs=(
            rows, rows, state, columns, time_mix, turned, rows, rows, columns, straight, turned
        ),
        out_specs=(
            rows, rows, state, columns, time_mix, turned, rows, rows, columns, straight, turned
        ),
        check_vma=False,
    )
```

```python
import jax
import jax.numpy as jnp
from jax import lax
from jax.experimental import pallas as pl
from jax.experimental.pallas import tpu as pltpu
from jax.experimental.layout import Layout, with_layout_constraint
from jax.sharding import PartitionSpec as P

GROUP_DIMENSION = 64
SHIFT_RANK = 32
ALL = ("seg", "span")

maximal_accuracy = lax.Precision.HIGHEST
ln_eps = 1e-05
gn_eps = 0.00064


def swap(block, bit):
    count = lax.axis_size("seg") * lax.axis_size("span")
    return lax.ppermute(block, ALL, [(i, i ^ bit) for i in range(count)])


def swap_core(block):
    return swap(block, 1)


def swap_low(block):
    return swap(block, 2)


def swap_high(block):
    return swap(block, 4)


def plane_groups():
    half = lax.axis_size("seg") // 2
    return [[2 * j + h for j in range(half)] for h in range(2)]


def in_order(own, other, second):
    return jnp.where(second, other, own), jnp.where(second, own, other)


def span_gather(block):
    place = lax.axis_index("span")
    low, core = place // 2, place % 2
    p0, p1 = in_order(block, swap_low(block), low == 1)
    q = swap_core(jnp.stack([p0, p1]))
    a0, a1 = in_order(p0, q[0], core == 1)
    b0, b1 = in_order(p1, q[1], core == 1)
    return jnp.concatenate([a0, a1, b0, b1], axis=0)


def span_reduce(part):
    place = lax.axis_index("span")
    low, core = place // 2, place % 2
    rows = part.shape[0] // 4
    b = part.reshape(2, 2, rows, part.shape[1])
    keep = jnp.where(core == 1, b[:, 1], b[:, 0])
    send = jnp.where(core == 1, b[:, 0], b[:, 1]).astype(jnp.bfloat16)
    got = swap_core(send)
    both = keep.astype(jnp.float32) + got.astype(jnp.float32)
    mine = jnp.where(low == 1, both[1], both[0])
    send = jnp.where(low == 1, both[0], both[1]).astype(jnp.bfloat16)
    return mine + swap_low(send).astype(jnp.float32)


def both_planes(laid, *blocks):
    high = lax.axis_index("seg") % 2
    own, other = (
        jnp.concatenate(laid(*got), axis=1) for got in (blocks, [swap_high(block) for block in blocks])
    )
    return jnp.concatenate(in_order(own, other, high == 1), axis=0)


def plane_gather(pair):
    whole = lax.all_gather(
        pair,
        "seg",
        axis=0,
        tiled=True,
        axis_index_groups=plane_groups(),
    )
    return with_layout_constraint(whole, Layout(major_to_minor=(0, 1)))


def plane_scatter(part):
    return lax.psum_scatter(
        part, "seg", scatter_dimension=0, tiled=True, axis_index_groups=plane_groups()
    )


def plane_halves(pair):
    high = lax.axis_index("seg") % 2
    rows = pair.shape[0] // 2
    return in_order(pair[:rows], pair[rows:], high == 1)


def finish_scatter(mine, send):
    return mine.astype(jnp.float32) + swap_high(send).astype(jnp.float32)


def gather_and_split(small, wide):
    place = lax.axis_index("span")
    n = wide.shape[1] // 4
    messages = [
        jnp.concatenate([lax.dynamic_slice_in_dim(wide, (place ^ bit) * n, n, 1), small], axis=1)
        for bit in range(4)
    ]
    pieces = [m if bit == 0 else swap(m, bit) for bit, m in enumerate(messages)]
    result = jnp.zeros((4, *messages[0].shape), small.dtype)
    for bit, piece in enumerate(pieces):
        result = lax.dynamic_update_index_in_dim(result, piece, place ^ bit, 0)
    return pieces[1], result.reshape(4 * small.shape[0], -1)


def split_columns(block):
    place = lax.axis_index("span")
    n = block.shape[1] // 4

    def columns(at):
        return lax.dynamic_slice_in_dim(block, at * n, n, 1)

    pieces = [columns(place)] + [swap(columns(place ^ bit), bit) for bit in (1, 2, 3)]
    result = jnp.zeros((4, block.shape[0], n), block.dtype)
    for bit, piece in enumerate(pieces):
        result = lax.dynamic_update_index_in_dim(result, piece, place ^ bit, 0)
    return result.reshape(4 * block.shape[0], n)


def join_columns(block):
    place = lax.axis_index("span")
    r, n = block.shape[0] // 4, block.shape[1]

    def rows(at):
        return lax.dynamic_slice_in_dim(block, at * r, r, 0)

    result = jnp.zeros((r, 4 * n), block.dtype)
    for bit in range(4):
        piece = rows(place ^ bit)
        if bit:
            piece = swap(piece, bit)
        result = lax.dynamic_update_slice_in_dim(result, piece, (place ^ bit) * n, 1)
    return result


def product_lower(left_arg, right_arg):
    return jnp.dot(left_arg, right_arg, preferred_element_type=jnp.float32)


def outer_sum(left_arg, right_arg):
    return jnp.einsum("td,te->de", left_arg, right_arg, preferred_element_type=jnp.float32)


def backward_product(gradient, weights):
    return jnp.einsum("te,de->td", gradient, weights, preferred_element_type=jnp.float32)


def norm_rows(values, gain_vec, offset):
    centre = values - jnp.mean(values, -1, keepdims=True)
    row_rstd = lax.rsqrt(jnp.mean(centre * centre, -1, keepdims=True) + ln_eps)
    unit_rows = centre * row_rstd
    return (unit_rows * gain_vec + offset, unit_rows, row_rstd)


def norm_back(gradient, unit_rows, row_rstd, gain_vec):
    scaled = gradient * gain_vec
    return row_rstd * (
        scaled
        - jnp.mean(scaled, -1, keepdims=True)
        - unit_rows * jnp.mean(scaled * unit_rows, -1, keepdims=True)
    )


def prior_rows(values):
    return jnp.concatenate([jnp.zeros_like(values[:1]), values[:-1]], axis=0)


def next_rows(values):
    return jnp.concatenate([values[1:], jnp.zeros_like(values[:1])], axis=0)


def reduce_small(part, pair):
    place, high = lax.axis_index("span"), lax.axis_index("seg") % 2
    planes = lax.axis_size("seg") // 2
    width = part.shape[1]
    b = part.reshape(planes, 2, 2, 2, -1, width)

    def summed(b, dim, bit, move):
        at0, at1 = (lax.index_in_dim(b, k, dim, keepdims=False) for k in (0, 1))
        mine, send = in_order(at0, at1, bit == 1)
        return mine.astype(jnp.float32) + move(send.astype(jnp.bfloat16)).astype(jnp.float32)

    b = summed(summed(b, 3, place % 2, swap_core), 2, place // 2, swap_low)
    b, pair = lax.optimization_barrier((b, pair))
    finished = finish_scatter(*plane_halves(pair))
    arrived = lax.all_to_all(
        summed(b, 1, high, swap_high).astype(jnp.bfloat16),
        "seg",
        split_axis=0,
        concat_axis=0,
        tiled=True,
        axis_index_groups=plane_groups(),
    )
    return arrived.astype(jnp.float32).sum(axis=0), finished


CHUNK = 64
PACK = 256


def mxu(a, b, contract):
    return lax.dot_general(
        a.astype(jnp.bfloat16),
        b.astype(jnp.bfloat16),
        (contract, ((), ())),
        preferred_element_type=jnp.float32,
    )


NN, NT, TN = ((1,), (0,)), ((1,), (1,)), ((0,), (0,))


def halves(values):
    high = values.astype(jnp.bfloat16)
    return high, (values - high.astype(jnp.float32)).astype(jnp.bfloat16)


def iota2(shape, dim):
    return lax.broadcasted_iota(jnp.int32, shape, dim)


def head_ones():
    shape = (PACK, PACK)
    same = iota2(shape, 0) // GROUP_DIMENSION == iota2(shape, 1) // GROUP_DIMENSION
    return jnp.where(same, 1.0, 0.0).astype(jnp.float32)


def spread(block, ones):
    return jnp.concatenate([block] * (PACK // CHUNK), axis=0) * ones


def fold(big, ones):
    kept = big * ones
    total = kept[:CHUNK]
    for h in range(1, PACK // CHUNK):
        total = total + kept[h * CHUNK : (h + 1) * CHUNK]
    return total


def head_sum(values, ones):
    high, rest = halves(values)
    return mxu(high, ones, NN) + mxu(rest, ones, NN)


def run_sum(which, values):
    high, rest = halves(values)
    return mxu(which, high, NN) + mxu(which, rest, NN)


def row_of(values, row):
    return values[row : row + 1]


def piece_factors(run, before):
    rows = iota2((CHUNK, PACK), 0)
    t, i = iota2((CHUNK, PACK), 0), iota2((CHUNK, PACK), 1) % CHUNK
    levels = []
    for half in (32, 16):
        upper = rows % (2 * half) >= half
        reference = jnp.broadcast_to(row_of(run, half - 1), run.shape)
        for start in range(2 * half, CHUNK, 2 * half):
            here = jnp.broadcast_to(row_of(run, start + half - 1), run.shape)
            reference = jnp.where(rows >= start, here, reference)
        scale = jnp.exp(jnp.where(upper, before - reference, reference - run))
        pairs = (t // (2 * half) == i // (2 * half)) & (t % (2 * half) >= half) & (i % (2 * half) < half)
        levels.append((jnp.where(upper, scale, 0.0), jnp.where(upper, 0.0, scale), pairs))
    reference = jnp.broadcast_to(row_of(run, 7), run.shape)
    for start in range(16, CHUNK, 16):
        here = jnp.broadcast_to(row_of(run, start + 7), run.shape)
        reference = jnp.where(rows >= start, here, reference)
    pairs = (t // 16 == i // 16) & (t > i)
    to_row = jnp.exp(jnp.minimum(before - reference, 80.0))
    to_prior = jnp.exp(jnp.minimum(reference - run, 80.0))
    levels.append((to_row, to_prior, pairs))
    return levels


def lower_ones():
    return jnp.where(iota2((CHUNK, CHUNK), 0) >= iota2((CHUNK, CHUNK), 1), 1.0, 0.0).astype(jnp.float32)


def decay_of(low_ref, up_ref, par_ref):
    log_decay = -jnp.exp(par_ref[0:1] + mxu(low_ref[...], up_ref[...], NT))
    run = run_sum(lower_ones(), log_decay)
    return log_decay, run, run - log_decay


def unit_heads(wkv, ones):
    centre = wkv - head_sum(wkv, ones) * (1.0 / GROUP_DIMENSION)
    rstd = lax.rsqrt(head_sum(centre * centre, ones) * (1.0 / GROUP_DIMENSION) + gn_eps)
    return centre * rstd, rstd


def lane_groups(refs, kinds):
    width = refs[0].shape[1]
    for g in range(width // PACK):
        lanes = pl.ds(g * PACK, PACK)
        part = {"c": lambda ref: ref.at[:, lanes], "r": lambda ref: ref.at[lanes], "s": lambda ref: ref.at[g]}
        yield [ref if kind == "w" else part[kind](ref) for ref, kind in zip(refs, kinds)]


def wkv_forward_kernel(*refs):
    for group in lane_groups(refs, "ccccwrcccccs"):
        forward_heads(*group)


def wkv_backward_kernel(*refs):
    for group in lane_groups(refs, "ccccwrccccccccccc" + "s"):
        backward_heads(*group)


def forward_heads(
    r_ref, k_ref, v_ref, gate_ref, low_ref, up_ref, par_ref, first_ref, mixed_ref, wkv_ref, held_ref, state
):
    ones = head_ones()

    @pl.when(pl.program_id(0) == 0)
    def _():
        state[...] = spread(first_ref[...], ones)

    r, k, v = r_ref[...], k_ref[...], v_ref[...]
    _, run, before = decay_of(low_ref, up_ref, par_ref)
    held_ref[...] = fold(state[...], ones)
    score = jnp.zeros((CHUNK, PACK), jnp.float32)
    for to_row, to_prior, pairs in piece_factors(run, before):
        score = jnp.where(pairs, mxu(r * to_row, spread(k * to_prior, ones), NT), score)
    out = mxu(score, spread(v, ones), NN) + mxu(r * jnp.exp(before), state[...], NT)
    out = out + head_sum(r * par_ref[1:2] * k, ones) * v
    wkv_ref[...] = out
    last = row_of(run, CHUNK - 1)
    state[...] = jnp.exp(last) * state[...] + mxu(v, k * jnp.exp(last - run), TN) * ones
    unit, _ = unit_heads(out, ones)
    gate = gate_ref[...]
    mixed_ref[...] = ((unit * par_ref[2:3] + par_ref[3:4]) * gate * jax.nn.sigmoid(gate)).astype(jnp.bfloat16)


def wkv_forward(r, k, v, gate, low, up, par, first):
    rows, columns = r.shape
    chunks = rows // CHUNK
    block = pl.BlockSpec((CHUNK, columns), lambda c: (c, 0))
    whole = lambda a: pl.BlockSpec(a.shape, lambda c: (0, 0))
    return pl.pallas_call(
        wkv_forward_kernel,
        grid=(chunks,),
        in_specs=[block] * 4
        + [
            pl.BlockSpec((CHUNK, low.shape[1]), lambda c: (c, 0)),
            whole(up),
            whole(par),
            whole(first),
        ],
        out_specs=[block, block, block],
        out_shape=[
            jax.ShapeDtypeStruct((rows, columns), jnp.bfloat16),
            jax.ShapeDtypeStruct((rows, columns), jnp.float32),
            jax.ShapeDtypeStruct((rows, columns), jnp.float32),
        ],
        scratch_shapes=[pltpu.VMEM((columns // PACK, PACK, PACK), jnp.float32)],
        compiler_params=pltpu.CompilerParams(
            dimension_semantics=("arbitrary",), vmem_limit_bytes=32 * 2**20
        ),
        cost_estimate=pl.CostEstimate(
            flops=2 * 9 * PACK * rows * columns, bytes_accessed=26 * rows * columns, transcendentals=8 * rows * columns
        ),
        name="wkv_forward",
    )(r, k, v, gate, low, up, par, first)


def backward_heads(
    r_ref, k_ref, v_ref, gate_ref, low_ref, up_ref, par_ref, wkv_ref, held_ref, gm_ref,
    gr_ref, gk_ref, gv_ref, gg_ref, gw_ref, sums_ref, first_ref, state,
):
    ones = head_ones()

    @pl.when(pl.program_id(0) == 0)
    def _():
        state[...] = jnp.zeros_like(state)
        sums_ref[...] = jnp.zeros_like(sums_ref)

    r, k, v, gate = r_ref[...], k_ref[...], v_ref[...], gate_ref[...]
    bonus, gain = par_ref[1:2], par_ref[2:3]

    def add_to(row, values):
        sums_ref[row : row + 1] = sums_ref[row : row + 1] + jnp.sum(values, axis=0, keepdims=True)

    unit, rstd = unit_heads(wkv_ref[...], ones)
    sig = jax.nn.sigmoid(gate)
    g_mixed = gm_ref[...].astype(jnp.float32)
    g_grouped = g_mixed * gate * sig
    grouped = unit * gain + par_ref[3:4]
    gg_ref[...] = (g_mixed * grouped * sig * (1.0 + gate * (1.0 - sig))).astype(jnp.bfloat16)
    add_to(2, g_grouped * unit)
    add_to(3, g_grouped)
    g_unit = g_grouped * gain
    scale = 1.0 / GROUP_DIMENSION
    g_out = rstd * (
        g_unit - head_sum(g_unit, ones) * scale - unit * (head_sum(g_unit * unit, ones) * scale)
    )

    log_decay, run, before = decay_of(low_ref, up_ref, par_ref)
    last = row_of(run, CHUNK - 1)
    start = spread(held_ref[...], ones)
    end_grad = state[...]
    v_wide = spread(v, ones)
    g_score = mxu(g_out, v_wide, NT)
    score = jnp.zeros((CHUNK, PACK), jnp.float32)
    from_start = jnp.exp(before)
    g_r = from_start * mxu(g_out, start, NN)
    to_end = jnp.exp(last - run)
    g_end = to_end * mxu(v, end_grad, NN)
    g_k = g_end
    for to_row, to_prior, pairs in piece_factors(run, before):
        r_level = (r * to_row).astype(jnp.bfloat16)
        k_level = spread(k * to_prior, ones).astype(jnp.bfloat16)
        score = jnp.where(pairs, mxu(r_level, k_level, NT), score)
        g_level = jnp.where(pairs, g_score, 0.0).astype(jnp.bfloat16)
        g_r = g_r + to_row * mxu(g_level, k_level, NN)
        g_k = g_k + to_prior * fold(mxu(g_level, r_level, TN), ones)
    g_v = fold(mxu(score, g_out, TN), ones) + mxu(k * to_end, end_grad, NT)
    g_before = r * g_r
    g_run = g_before - k * g_k
    g_last = jnp.sum(k * g_end, axis=0, keepdims=True) + jnp.exp(last) * jnp.sum(
        start * end_grad, axis=0, keepdims=True
    )
    upper = jnp.where(iota2((CHUNK, CHUNK), 0) <= iota2((CHUNK, CHUNK), 1), 1.0, 0.0).astype(jnp.float32)
    g_decay = run_sum(upper, g_run) - g_before + g_last
    g_expo = g_decay * log_decay
    gw_ref[...] = g_expo.astype(jnp.bfloat16)
    add_to(0, g_expo)
    g_diag = head_sum(g_out * v, ones)
    add_to(1, r * k * g_diag)
    gr_ref[...] = (g_r + bonus * k * g_diag).astype(jnp.bfloat16)
    gk_ref[...] = (g_k + bonus * r * g_diag).astype(jnp.bfloat16)
    gv_ref[...] = (g_v + head_sum(r * bonus * k, ones) * g_out).astype(jnp.bfloat16)
    state[...] = jnp.exp(last) * end_grad + mxu(g_out, r * from_start, TN) * ones

    @pl.when(pl.program_id(0) == pl.num_programs(0) - 1)
    def _():
        first_ref[...] = fold(state[...], ones)


def wkv_backward(r, k, v, gate, low, up, par, wkv, held, g_mixed):
    rows, columns = r.shape
    chunks = rows // CHUNK
    block = pl.BlockSpec((CHUNK, columns), lambda c: (chunks - 1 - c, 0))
    whole = lambda a: pl.BlockSpec(a.shape, lambda c: (0, 0))
    of_all = lambda n: pl.BlockSpec((n, columns), lambda c: (0, 0))
    low_type = jax.ShapeDtypeStruct((rows, columns), jnp.bfloat16)
    return pl.pallas_call(
        wkv_backward_kernel,
        grid=(chunks,),
        in_specs=[block] * 4
        + [
            pl.BlockSpec((CHUNK, low.shape[1]), lambda c: (chunks - 1 - c, 0)),
            whole(up),
            whole(par),
            block,
            block,
            block,
        ],
        out_specs=[block] * 5 + [of_all(8), of_all(GROUP_DIMENSION)],
        out_shape=[low_type] * 5
        + [
            jax.ShapeDtypeStruct((8, columns), jnp.float32),
            jax.ShapeDtypeStruct((GROUP_DIMENSION, columns), jnp.float32),
        ],
        scratch_shapes=[pltpu.VMEM((columns // PACK, PACK, PACK), jnp.float32)],
        compiler_params=pltpu.CompilerParams(
            dimension_semantics=("arbitrary",), vmem_limit_bytes=32 * 2**20
        ),
        cost_estimate=pl.CostEstimate(
            flops=2 * 24 * PACK * rows * columns, bytes_accessed=40 * rows * columns, transcendentals=12 * rows * columns
        ),
        name="wkv_backward",
    )(r, k, v, gate, low, up, par, wkv, held, g_mixed)


GRAD_ROWS, GRAD_COLUMNS = 512, 256


def grad_kernel(left_ref, right_ref, *rest):
    out_ref = rest[-1]
    turned = left_ref[...].T
    for at in range(0, out_ref.shape[1], GRAD_COLUMNS):
        columns = slice(at, at + GRAD_COLUMNS)
        out_ref[:, columns] = mxu(turned, right_ref[:, columns], NN).astype(jnp.bfloat16)


def grad_into(left, right, total, at, into=None):
    rows, width = left.shape
    columns = right.shape[1]
    shift = at // columns
    specs = [
        pl.BlockSpec((rows, GRAD_ROWS), lambda i: (0, i)),
        pl.BlockSpec((rows, columns), lambda i: (0, 0)),
    ]
    operands = [left, right]
    alias = {}
    if into is not None:
        specs.append(pl.BlockSpec(memory_space=pltpu.HBM))
        operands.append(into)
        alias = {2: 0}
    return pl.pallas_call(
        grad_kernel,
        grid=(width // GRAD_ROWS,),
        in_specs=specs,
        out_specs=pl.BlockSpec((GRAD_ROWS, columns), lambda i: (i, shift)),
        out_shape=pltpu.HBM((width, total), jnp.bfloat16),
        input_output_aliases=alias,
        compiler_params=pltpu.CompilerParams(
            dimension_semantics=("arbitrary",), vmem_limit_bytes=32 * 2**20
        ),
        cost_estimate=pl.CostEstimate(
            flops=2 * rows * width * columns,
            bytes_accessed=2 * (rows * (width + columns) + width * columns),
            transcendentals=0,
        ),
        name="weight_grad",
    )(*operands)


LOW = 256
SHIFT_LANES = 5 * SHIFT_RANK
LANES = SHIFT_LANES + 64

TILE = 512


def lane_group(shape):
    return iota2(shape, 1) // SHIFT_RANK


def mixes_forward_kernel(
    unit_ref, w_ref, down_ref, up_ref, vec_ref,
    m0_ref, m1_ref, m2_ref, m3_ref, m4_ref, normed_ref, squash_ref, r_ref, k_ref, v_ref, g_ref,
    hidden, grouped,
):
    phase, tile = pl.program_id(0), pl.program_id(1)
    rows = unit_ref.shape[0]
    own = r_ref.shape[1]
    vec = vec_ref[...]
    normed = unit_ref[...] * vec[0:1] + vec[1:2]
    row = iota2(normed.shape, 0)
    shifted = jnp.where(row == 0, 0.0, pltpu.roll(normed, 1, 0)) - normed
    down = down_ref[...]
    of_shift = iota2(down.shape, 1) < SHIFT_LANES

    @pl.when((phase == 0) & (tile == 0))
    def _():
        hidden[...] = jnp.zeros_like(hidden)

    @pl.when(phase == 0)
    def _():
        hidden[...] = hidden[...] + mxu(normed + shifted * vec[2:3], jnp.where(of_shift, down, 0), NN)

    @pl.when((phase == 1) & (tile == 0))
    def _():
        squash = jnp.tanh(hidden[...])
        squash_ref[...] = squash
        group = lane_group(squash.shape)
        for g in range(5):
            grouped[g] = jnp.where(group == g, squash, 0.0).astype(jnp.bfloat16)
        hidden[...] = jnp.zeros_like(hidden)
        for ref in (r_ref, k_ref, v_ref, g_ref):
            ref[...] = jnp.zeros_like(ref)

    @pl.when(phase == 1)
    def _():
        normed_ref[...] = normed
        up = up_ref[...]
        for g, mix_ref in enumerate((m0_ref, m1_ref, m2_ref, m3_ref, m4_ref)):
            mix = (normed + shifted * (vec[3 + g : 4 + g] + mxu(grouped[g], up, NT))).astype(jnp.bfloat16)
            mix_ref[...] = mix
            if g == 0:
                hidden[...] = hidden[...] + mxu(mix, jnp.where(of_shift, 0, down), NN)
            else:
                column = (None, 1, 2, 0, 3)[g] * own
                out = (None, k_ref, v_ref, r_ref, g_ref)[g]
                out[...] = out[...] + mxu(mix, w_ref[:, column : column + own], NN)

    @pl.when((phase == 1) & (tile == pl.num_programs(1) - 1))
    def _():
        squash_ref[...] = squash_ref[...] + jnp.tanh(hidden[...])


def mixes_forward(unit, first, low_at, vec, own):
    rows, width = unit.shape
    tiles = width // TILE
    block = low_at // LOW
    across = lambda r: pl.BlockSpec((r, TILE), lambda p, n: (0, n))
    late = pl.BlockSpec((rows, TILE), lambda p, n: (0, n * p))
    whole = lambda columns: pl.BlockSpec((rows, columns), lambda p, n: (0, 0))
    kept = lambda columns, dtype: jax.ShapeDtypeStruct((rows, columns), dtype)
    return pl.pallas_call(
        mixes_forward_kernel,
        grid=(2, tiles),
        in_specs=[
            across(rows),
            pl.BlockSpec((TILE, 4 * own), lambda p, n: (n * p, 0)),
            pl.BlockSpec((TILE, LOW), lambda p, n: (n, block)),
            pl.BlockSpec((TILE, LOW), lambda p, n: (n, block + 1)),
            across(vec.shape[0]),
        ],
        out_specs=[late] * 6 + [whole(LOW)] + [whole(own)] * 4,
        out_shape=[kept(width, jnp.bfloat16)] * 5
        + [kept(width, jnp.float32), kept(LOW, jnp.float32)]
        + [kept(own, jnp.float32)] * 4,
        scratch_shapes=[pltpu.VMEM((rows, LOW), jnp.float32), pltpu.VMEM((5, rows, LOW), jnp.bfloat16)],
        compiler_params=pltpu.CompilerParams(
            dimension_semantics=("arbitrary", "arbitrary"), vmem_limit_bytes=48 * 2**20
        ),
        cost_estimate=pl.CostEstimate(
            flops=2 * rows * width * (4 * own + 7 * LOW),
            bytes_accessed=2 * width * 4 * own + 22 * rows * width,
            transcendentals=0,
        ),
        name="mixes_forward",
    )(unit, first, first, first, vec)


def mixes_back_kernel(
    gk_ref, gv_ref, gr_ref, gg_ref, gd_ref, w_ref, down_ref, up_ref, vec_ref, squash_ref, normed_ref,
    mix_ref, sums_ref, out_ref, small_ref,
    g_shift, g_norm, g_squash, g_hidden, g_up, g_sums, grouped, turned,
):
    phase, tile = pl.program_id(0), pl.program_id(1)
    rows = squash_ref.shape[0]
    own = gk_ref.shape[1]
    normed = normed_ref[...]
    row = iota2(normed.shape, 0)
    shifted = jnp.where(row == 0, 0.0, pltpu.roll(normed, 1, 0)) - normed
    squash = squash_ref[...]
    vec = vec_ref[...]

    @pl.when((phase == 0) & (tile == 0))
    def _():
        g_squash[...] = jnp.zeros_like(g_squash)
        group = lane_group(squash.shape)
        for g in range(5):
            grouped[g] = jnp.where(group == g, squash, 0.0).astype(jnp.bfloat16)
        turned[...] = squash.astype(jnp.bfloat16).T

    @pl.when(phase == 0)
    def _():
        up = up_ref[...]
        group_wide = lane_group(up.shape)
        total_shift = jnp.zeros((rows, TILE), jnp.float32)
        total_norm = jnp.zeros((rows, TILE), jnp.float32)
        add_squash = jnp.zeros((rows, LOW), jnp.float32)
        sums = []
        for g in range(5):
            if g == 0:
                part = mxu(gd_ref[...], down_ref[...], NT)
            else:
                column = (None, 1, 2, 0, 3)[g] * own
                grad = (None, gk_ref, gv_ref, gr_ref, gg_ref)[g]
                part = mxu(grad[...], w_ref[:, column : column + own], NT)
            coeff = vec[3 + g : 4 + g] + mxu(grouped[g], up, NT)
            times = part * shifted
            times_low = times.astype(jnp.bfloat16)
            sums.append(jnp.sum(times, axis=0, keepdims=True))
            total_shift = total_shift + part * coeff
            total_norm = total_norm + part
            add_squash = add_squash + mxu(times_low, jnp.where(group_wide == g, up, 0), NN)
            lanes = slice(g * SHIFT_RANK, (g + 1) * SHIFT_RANK)
            g_up[tile, lanes] = mxu(turned[lanes], times_low, NN)
        g_shift[tile] = total_shift
        g_norm[tile] = total_norm
        g_squash[...] = g_squash[...] + add_squash
        g_sums[tile] = jnp.concatenate(sums + [jnp.zeros((3, TILE), jnp.float32)], axis=0)

    @pl.when((phase == 1) & (tile == 0))
    def _():
        g_hidden[...] = (g_squash[...] * (1.0 - squash * squash)).astype(jnp.bfloat16)

    @pl.when(phase == 1)
    def _():
        blend = vec[2:3]
        part = mxu(g_hidden[...], down_ref[...], NT)
        total_shift = g_shift[tile] + part * blend
        total = g_norm[tile] + part - total_shift
        total = total + jnp.where(row == rows - 1, 0.0, pltpu.roll(total_shift, rows - 1, 0))
        out_ref[...] = total.astype(jnp.bfloat16)
        unit = (normed - vec[1:2]) / vec[0:1]
        head = [
            jnp.sum(total * unit, axis=0, keepdims=True),
            jnp.sum(total, axis=0, keepdims=True),
            jnp.sum(part * shifted, axis=0, keepdims=True),
        ]
        sums = jnp.concatenate(head + [g_sums[tile][:5], sums_ref[...]], axis=0)
        shape = (sums.shape[0], LOW)
        behind = jnp.where(iota2(shape, 1) == LANES + iota2(shape, 0), 1.0, 0.0)
        small_ref[:, :LOW] = (
            mxu(normed + shifted * blend, g_hidden[...], TN) + mxu(mix_ref[...], gd_ref[...], TN)
        ).astype(jnp.bfloat16)
        small_ref[:, LOW:] = mxu(sums, behind, TN).astype(jnp.bfloat16)
        small_ref[:, LOW : LOW + SHIFT_LANES] = g_up[tile].T.astype(jnp.bfloat16)


def mixes_back(g_key, g_val, g_recept, g_gate, g_decay, first, low_at, vec, squash, normed, mix, sums):
    rows, width = normed.shape
    own = g_key.shape[1]
    tiles = width // TILE
    block = low_at // LOW
    whole = lambda a: pl.BlockSpec(a.shape, lambda p, n: (0, 0))
    across = lambda r: pl.BlockSpec((r, TILE), lambda p, n: (0, n))
    late = lambda r: pl.BlockSpec((r, TILE), lambda p, n: (0, n * p))
    early = lambda p, n: n * (1 - p) + (tiles - 1) * p
    return pl.pallas_call(
        mixes_back_kernel,
        grid=(2, tiles),
        in_specs=[whole(g_key)] * 4
        + [
            whole(g_decay),
            pl.BlockSpec((TILE, 4 * own), lambda p, n: (early(p, n), 0)),
            pl.BlockSpec((TILE, LOW), lambda p, n: (n, block)),
            pl.BlockSpec((TILE, LOW), lambda p, n: (early(p, n), block + 1)),
            across(vec.shape[0]),
            whole(squash),
            across(rows),
            late(rows),
            late(sums.shape[0]),
        ],
        out_specs=[late(rows), pl.BlockSpec((TILE, 2 * LOW), lambda p, n: (n * p, 0))],
        out_shape=[
            jax.ShapeDtypeStruct((rows, width), jnp.bfloat16),
            jax.ShapeDtypeStruct((width, 2 * LOW), jnp.bfloat16),
        ],
        scratch_shapes=[
            pltpu.VMEM((tiles, rows, TILE), jnp.float32),
            pltpu.VMEM((tiles, rows, TILE), jnp.float32),
            pltpu.VMEM((rows, LOW), jnp.float32),
            pltpu.VMEM((rows, LOW), jnp.bfloat16),
            pltpu.VMEM((tiles, SHIFT_LANES, TILE), jnp.float32),
            pltpu.VMEM((tiles, 8, TILE), jnp.float32),
            pltpu.VMEM((5, rows, LOW), jnp.bfloat16),
            pltpu.VMEM((LOW, rows), jnp.bfloat16),
        ],
        compiler_params=pltpu.CompilerParams(
            dimension_semantics=("arbitrary", "arbitrary"), vmem_limit_bytes=56 * 2**20
        ),
        cost_estimate=pl.CostEstimate(
            flops=2 * rows * width * (4 * own + 17 * LOW),
            bytes_accessed=2 * width * 4 * own + 10 * rows * width,
            transcendentals=0,
        ),
        name="mixes_back",
    )(g_key, g_val, g_recept, g_gate, g_decay, first, first, first, vec, squash, normed, mix, sums)


def shards(
    inputs,
    cotangent,
    states,
    vectors,
    time_mix_weight,
    output_weight,
    channel_receptance_weight,
    rank_down_weight,
    rank_up_weight,
    channel_key_weight,
    channel_value_weight,
):
    token_rows, width = inputs.shape
    own_width = time_mix_weight.shape[2]
    hidden = channel_key_weight.shape[1]
    local_heads = own_width // GROUP_DIMENSION
    col_start = lax.axis_index("span") * own_width
    position = lax.axis_index("span") * token_rows

    x_seg = span_gather(inputs).astype(jnp.float32)
    def blank(count):
        return jnp.zeros((token_rows // 8, count), jnp.bfloat16)

    small_rows = jnp.concatenate(
        [rank_down_weight, blank(LOW - LANES), rank_up_weight.T, vectors.T, blank(LOW - LANES - 16)], axis=1
    )
    early, span_rows = gather_and_split(small_rows, channel_receptance_weight)
    _, time_mix_weight, output_weight = lax.optimization_barrier((early, time_mix_weight, output_weight))
    weights = both_planes(
        lambda proj, out: [proj[g] for g in range(4)] + [out.T], time_mix_weight, output_weight
    )
    first = plane_gather(jnp.concatenate([weights, both_planes(lambda rows: [rows], span_rows)], axis=1))
    second = plane_gather(
        both_planes(lambda key, value: [key, value.T], channel_key_weight, channel_value_weight)
    )
    low_at = 6 * own_width
    out_w, recept_w = first[:, 4 * own_width : 5 * own_width], first[:, 5 * own_width : low_at]
    up_at = low_at + LOW
    vec = first[:, up_at + LANES : up_at + LANES + 16].T.astype(jnp.float32)

    def own_cols(line):
        return lax.dynamic_slice_in_dim(line, col_start, own_width, line.ndim - 1)

    def own_rows(values):
        return lax.dynamic_slice_in_dim(values, position, token_rows, 0)

    x_in = inputs.astype(jnp.float32)
    _, unit_seg, _ = norm_rows(x_seg, 1.0, 0.0)
    *mixes, normed, squash, recept, key_proj, val_proj, gate_pre = mixes_forward(
        unit_seg, first, low_at, vec, own_width
    )
    lane = lax.broadcasted_iota(jnp.int32, squash.shape, 1)
    of_decay = (lane >= SHIFT_LANES) & (lane < LANES)
    decay_low = jnp.where(of_decay, squash, 0.0).astype(jnp.bfloat16)
    up_own = lax.dynamic_slice(first, (col_start, up_at), (own_width, LOW))
    head_vec = jnp.concatenate([own_cols(vec[8:12]), jnp.zeros((4, own_width), jnp.float32)], axis=0)
    first_state = jnp.transpose(states[0], (2, 0, 1)).reshape(GROUP_DIMENSION, own_width)
    heads_in = (recept, key_proj, val_proj, gate_pre, decay_low, up_own, head_vec)
    mixed, wkv, held = wkv_forward(*heads_in, first_state)
    resid = x_in + span_reduce(backward_product(mixed, out_w).astype(jnp.bfloat16))

    normed_two, unit_two, rstd_two = norm_rows(resid, vec[12], vec[13])
    n2 = span_gather(normed_two.astype(jnp.bfloat16)).astype(jnp.float32)
    shifted_two = prior_rows(n2) - n2
    key_in = (n2 + shifted_two * vec[14]).astype(jnp.bfloat16)
    rec_in = (n2 + shifted_two * vec[15]).astype(jnp.bfloat16)
    rec_part = product_lower(rec_in, recept_w).astype(jnp.bfloat16)
    rec_pre, second = lax.optimization_barrier((join_columns(rec_part), second))
    key_w, value_w = second[:, :hidden], second[:, hidden:]
    hidden_two = product_lower(key_in, key_w)
    active = jax.nn.relu(hidden_two)
    squared = (active * active).astype(jnp.bfloat16)
    active = active.astype(jnp.bfloat16)
    half = width // 2
    value_out = jnp.concatenate(
        [
            span_reduce(backward_product(squared, value_w[at : at + half]).astype(jnp.bfloat16))
            for at in (0, half)
        ],
        axis=1,
    )
    rec_gate = jax.nn.sigmoid(rec_pre.astype(jnp.float32))
    output = (resid + rec_gate * value_out).astype(jnp.bfloat16)

    grad_out = cotangent.astype(jnp.float32)
    g_value = (grad_out * rec_gate).astype(jnp.bfloat16)
    g_rec = (grad_out * value_out * rec_gate * (1.0 - rec_gate)).astype(jnp.bfloat16)
    g_value_all = span_gather(g_value)
    g_value_all, g_rec = lax.optimization_barrier((g_value_all, g_rec))
    g_rec_own = split_columns(g_rec)
    cm_total = 2 * hidden + own_width
    cm_part = grad_into(g_value_all, squared, cm_total, hidden)
    g_value_all, cm_part = lax.optimization_barrier((g_value_all, cm_part))
    g_hid = (product_lower(g_value_all, value_w) * 2.0 * active.astype(jnp.float32)).astype(jnp.bfloat16)
    cm_part = grad_into(key_in, g_hid, cm_total, 0, cm_part)
    cm_part = grad_into(rec_in, g_rec_own, cm_total, 2 * hidden, cm_part)
    cm_part, g_hid, g_rec_own = lax.optimization_barrier((cm_part, g_hid, g_rec_own))
    cm_pair = plane_scatter(cm_part)
    g_key_in = backward_product(g_hid, key_w)
    g_rec_in = backward_product(g_rec_own, recept_w)
    vec_fourteen = jnp.sum(g_key_in * shifted_two, axis=0)
    vec_fifteen = jnp.sum(g_rec_in * shifted_two, axis=0)
    g_shift_two = g_key_in * vec[14] + g_rec_in * vec[15]
    g_n2_part = g_key_in + g_rec_in - g_shift_two + next_rows(g_shift_two)
    g_n2 = span_reduce(g_n2_part.astype(jnp.bfloat16))
    vec_twelve = jnp.sum(g_n2 * unit_two, axis=0)
    vec_thirteen = jnp.sum(g_n2, axis=0)
    g_resid = grad_out + norm_back(g_n2, unit_two, rstd_two, vec[12])

    g_att = span_gather(g_resid.astype(jnp.bfloat16))
    g_mixed = product_lower(g_att, out_w)
    g_recept, g_key, g_val, g_gate, g_ww, head_sums, g_first = wkv_backward(
        *heads_in, wkv, held, g_mixed
    )
    state_grad = jnp.transpose(
        g_first.reshape(GROUP_DIMENSION, local_heads, GROUP_DIMENSION), (1, 2, 0)
    )[None]
    tm_total = 5 * own_width
    tm_part = grad_into(g_att, mixed, tm_total, 0)
    for at, mix, grad in ((1, 3, g_recept), (2, 1, g_key), (3, 2, g_val), (4, 4, g_gate)):
        tm_part = grad_into(mixes[mix], grad, tm_total, at * own_width, tm_part)
    tm_part, cm_pair = lax.optimization_barrier((tm_part, cm_pair))
    tm_pair = plane_scatter(tm_part)
    g_key, g_ww, cm_pair = lax.optimization_barrier((g_key, g_ww, cm_pair))

    g_decay_hidden = jnp.where(
        of_decay, product_lower(g_ww, up_own) * (1.0 - squash * squash), 0.0
    ).astype(jnp.bfloat16)
    up_decay_grad = outer_sum(g_ww, decay_low)
    other_sums = jnp.concatenate(
        [
            lax.dynamic_update_slice_in_dim(jnp.zeros((4, width), jnp.float32), head_sums[:4], col_start, 1),
            jnp.stack([vec_twelve, vec_thirteen, vec_fourteen, vec_fifteen]),
        ],
        axis=0,
    )
    g_normed, small_part = mixes_back(
        g_key, g_val, g_recept, g_gate, g_decay_hidden, first, low_at, vec, squash, normed, mixes[0], other_sums
    )
    own_part = lax.dynamic_slice(small_part, (col_start, LOW), (own_width, LOW))
    small_part = lax.dynamic_update_slice(
        small_part, (own_part.astype(jnp.float32) + up_decay_grad).astype(jnp.bfloat16), (col_start, LOW)
    )
    small, cm_grad = reduce_small(small_part, cm_pair)
    tm_grad = finish_scatter(*plane_halves(tm_pair))
    g_n1 = span_reduce(g_normed)
    _, unit_own, rstd_own = norm_rows(x_in, vec[0], vec[1])
    x_grad = g_resid + norm_back(g_n1, unit_own, rstd_own, vec[0])
    down_grad = small[:, :LANES]
    up_grad = small[:, LOW : LOW + LANES].T
    vec_grad = small[:, LOW + LANES : LOW + LANES + 16].T
    rec_grad = join_columns(cm_grad[:, 2 * hidden :])
    value_grad = cm_grad[:, hidden : 2 * hidden].T
    key_grad = cm_grad[:, :hidden]
    out_grad = tm_grad[:, :own_width].T
    proj_grad = jnp.moveaxis(tm_grad[:, own_width:].reshape(-1, 4, own_width), 1, 0)
    return (
        output,
        x_grad,
        state_grad,
        vec_grad,
        proj_grad,
        out_grad,
        rec_grad,
        down_grad,
        up_grad,
        key_grad,
        value_grad,
    )


def solution(mesh):
    rows, columns = P(ALL, None), P(None, ALL)
    state = P("seg", "span", None, None)
    time_mix = P(None, "seg", "span")
    turned, straight = P("span", "seg"), P("seg", "span")
    return jax.shard_map(
        shards,
        mesh=mesh,
        in_specs=(
            rows, rows, state, columns, time_mix, turned, rows, rows, columns, straight, turned
        ),
        out_specs=(
            rows, rows, state, columns, time_mix, turned, rows, rows, columns, straight, turned
        ),
        check_vma=False,
    )
```

```python
import jax
import jax.numpy as jnp
from jax import lax
from jax.experimental import pallas as pl
from jax.experimental.pallas import tpu as pltpu
from jax.experimental.layout import Layout, with_layout_constraint
from jax.sharding import PartitionSpec as P

GROUP_DIMENSION = 64
SHIFT_RANK = 32
ALL = ("seg", "span")

maximal_accuracy = lax.Precision.HIGHEST
ln_eps = 1e-05
gn_eps = 0.00064


def swap(block, bit):
    count = lax.axis_size("seg") * lax.axis_size("span")
    return lax.ppermute(block, ALL, [(i, i ^ bit) for i in range(count)])


def swap_core(block):
    return swap(block, 1)


def swap_low(block):
    return swap(block, 2)


def swap_high(block):
    return swap(block, 4)


def plane_groups():
    half = lax.axis_size("seg") // 2
    return [[2 * j + h for j in range(half)] for h in range(2)]


def in_order(own, other, second):
    return jnp.where(second, other, own), jnp.where(second, own, other)


def span_gather(block, axis=0):
    place = lax.axis_index("span")
    low, core = place // 2, place % 2
    p0, p1 = in_order(block, swap_low(block), low == 1)
    q = swap_core(jnp.stack([p0, p1]))
    a0, a1 = in_order(p0, q[0], core == 1)
    b0, b1 = in_order(p1, q[1], core == 1)
    return jnp.concatenate([a0, a1, b0, b1], axis=axis)


def core_reduce(part):
    core = lax.axis_index("span") % 2
    half = part.shape[1] // 2
    keep, send = in_order(part[:, :half], part[:, half:], core == 1)
    return keep.astype(jnp.float32) + swap_core(send.astype(jnp.bfloat16)).astype(jnp.float32)


def over_cores(part):
    core = lax.axis_index("span") % 2
    b = part.reshape(2, 2, part.shape[0] // 4, part.shape[1])
    keep, send = in_order(b[:, 0], b[:, 1], core == 1)
    return keep.astype(jnp.float32) + swap_core(send.astype(jnp.bfloat16)).astype(jnp.float32)


def over_low(both):
    low = lax.axis_index("span") // 2
    mine, send = in_order(both[0], both[1], low == 1)
    return mine + swap_low(send.astype(jnp.bfloat16)).astype(jnp.float32)


def span_reduce(part):
    return over_low(over_cores(part))


def fill_pair(rows):
    half = rows.shape[2] // 2
    return jnp.concatenate([rows[:, :, :half], rows[:, :, half:]], axis=1)


def from_pair(pairs):
    half = pairs.shape[1] // 2
    return jnp.concatenate([pairs[:, :half], pairs[:, half:]], axis=2)


def other_plane(rows, got):
    high = lax.axis_index("seg") % 2
    return jnp.stack(in_order(rows, got, high == 1), axis=1).reshape(-1, rows.shape[2])


def both_planes(laid, *blocks):
    high = lax.axis_index("seg") % 2
    own, other = (
        jnp.concatenate(laid(*got), axis=1) for got in (blocks, [swap_high(block) for block in blocks])
    )
    return jnp.concatenate(in_order(own, other, high == 1), axis=0)


def plane_gather(pair):
    whole = lax.all_gather(
        pair,
        "seg",
        axis=0,
        tiled=True,
        axis_index_groups=plane_groups(),
    )
    return with_layout_constraint(whole, Layout(major_to_minor=(0, 1)))


def plane_scatter(part):
    return lax.psum_scatter(
        part, "seg", scatter_dimension=0, tiled=True, axis_index_groups=plane_groups()
    )


def plane_halves(pair):
    high = lax.axis_index("seg") % 2
    rows = pair.shape[0] // 2
    return in_order(pair[:rows], pair[rows:], high == 1)


def finish_scatter(mine, send):
    return mine.astype(jnp.float32) + swap_high(send).astype(jnp.float32)


def gather_and_split(small, wide):
    place = lax.axis_index("span")
    n = wide.shape[1] // 4
    messages = [
        jnp.concatenate([lax.dynamic_slice_in_dim(wide, (place ^ bit) * n, n, 1), small], axis=1)
        for bit in range(4)
    ]
    pieces = [m if bit == 0 else swap(m, bit) for bit, m in enumerate(messages)]
    result = jnp.zeros((4, *messages[0].shape), small.dtype)
    for bit, piece in enumerate(pieces):
        result = lax.dynamic_update_index_in_dim(result, piece, place ^ bit, 0)
    return pieces[1], result.reshape(4 * small.shape[0], -1)


def split_columns(block):
    place = lax.axis_index("span")
    n = block.shape[1] // 4

    def columns(at):
        return lax.dynamic_slice_in_dim(block, at * n, n, 1)

    pieces = [columns(place)] + [swap(columns(place ^ bit), bit) for bit in (1, 2, 3)]
    result = jnp.zeros((4, block.shape[0], n), block.dtype)
    for bit, piece in enumerate(pieces):
        result = lax.dynamic_update_index_in_dim(result, piece, place ^ bit, 0)
    return result.reshape(4 * block.shape[0], n)


def join_columns(block):
    place = lax.axis_index("span")
    r, n = block.shape[0] // 4, block.shape[1]

    def rows(at):
        return lax.dynamic_slice_in_dim(block, at * r, r, 0)

    result = jnp.zeros((r, 4 * n), block.dtype)
    for bit in range(4):
        piece = rows(place ^ bit)
        if bit:
            piece = swap(piece, bit)
        result = lax.dynamic_update_slice_in_dim(result, piece, (place ^ bit) * n, 1)
    return result


def product_lower(left_arg, right_arg):
    return jnp.dot(left_arg, right_arg, preferred_element_type=jnp.float32)


def outer_sum(left_arg, right_arg):
    return jnp.einsum("td,te->de", left_arg, right_arg, preferred_element_type=jnp.float32)


def backward_product(gradient, weights):
    return jnp.einsum("te,de->td", gradient, weights, preferred_element_type=jnp.float32)


def norm_rows(values, gain_vec, offset):
    centre = values - jnp.mean(values, -1, keepdims=True)
    row_rstd = lax.rsqrt(jnp.mean(centre * centre, -1, keepdims=True) + ln_eps)
    unit_rows = centre * row_rstd
    return (unit_rows * gain_vec + offset, unit_rows, row_rstd)


def norm_back(gradient, unit_rows, row_rstd, gain_vec):
    scaled = gradient * gain_vec
    return row_rstd * (
        scaled
        - jnp.mean(scaled, -1, keepdims=True)
        - unit_rows * jnp.mean(scaled * unit_rows, -1, keepdims=True)
    )


def prior_rows(values):
    return jnp.concatenate([jnp.zeros_like(values[:1]), values[:-1]], axis=0)


def next_rows(values):
    return jnp.concatenate([values[1:], jnp.zeros_like(values[:1])], axis=0)


def reduce_small(part, both, pair):
    place, high = lax.axis_index("span"), lax.axis_index("seg") % 2
    planes = lax.axis_size("seg") // 2
    width = part.shape[1]
    b = part.reshape(planes, 2, 2, 2, -1, width)

    def summed(b, dim, bit, move):
        at0, at1 = (lax.index_in_dim(b, k, dim, keepdims=False) for k in (0, 1))
        mine, send = in_order(at0, at1, bit == 1)
        return mine.astype(jnp.float32) + move(send.astype(jnp.bfloat16)).astype(jnp.float32)

    b = summed(summed(b, 3, place % 2, swap_core), 2, place // 2, swap_low)
    b, both = lax.optimization_barrier((b, both))
    rows = over_low(both)
    b = summed(b, 1, high, swap_high).astype(jnp.bfloat16)
    b, pair = lax.optimization_barrier((b, pair))
    finished = finish_scatter(*plane_halves(pair))
    arrived = lax.all_to_all(
        b, "seg", split_axis=0, concat_axis=0, tiled=True, axis_index_groups=plane_groups()
    )
    return arrived.astype(jnp.float32).sum(axis=0), rows, finished


SOON = pl.CostEstimate(flops=2**20, bytes_accessed=2**16, transcendentals=0)

CHUNK = 64
PACK = 256


def mxu(a, b, contract):
    return lax.dot_general(
        a.astype(jnp.bfloat16),
        b.astype(jnp.bfloat16),
        (contract, ((), ())),
        preferred_element_type=jnp.float32,
    )


NN, NT, TN = ((1,), (0,)), ((1,), (1,)), ((0,), (0,))


def halves(values):
    high = values.astype(jnp.bfloat16)
    return high, (values - high.astype(jnp.float32)).astype(jnp.bfloat16)


def iota2(shape, dim):
    return lax.broadcasted_iota(jnp.int32, shape, dim)


def head_ones():
    shape = (PACK, PACK)
    same = iota2(shape, 0) // GROUP_DIMENSION == iota2(shape, 1) // GROUP_DIMENSION
    return jnp.where(same, 1.0, 0.0).astype(jnp.float32)


def spread(block, ones):
    return jnp.concatenate([block] * (PACK // CHUNK), axis=0) * ones


def fold(big, ones):
    kept = big * ones
    total = kept[:CHUNK]
    for h in range(1, PACK // CHUNK):
        total = total + kept[h * CHUNK : (h + 1) * CHUNK]
    return total


def head_sum(values, ones):
    high, rest = halves(values)
    return mxu(high, ones, NN) + mxu(rest, ones, NN)


def run_sum(which, values):
    high, rest = halves(values)
    return mxu(which, high, NN) + mxu(which, rest, NN)


def row_of(values, row):
    return values[row : row + 1]


def piece_factors(run, before):
    rows = iota2((CHUNK, PACK), 0)
    t, i = iota2((CHUNK, PACK), 0), iota2((CHUNK, PACK), 1) % CHUNK
    levels = []
    for half in (32, 16):
        upper = rows % (2 * half) >= half
        reference = jnp.broadcast_to(row_of(run, half - 1), run.shape)
        for start in range(2 * half, CHUNK, 2 * half):
            here = jnp.broadcast_to(row_of(run, start + half - 1), run.shape)
            reference = jnp.where(rows >= start, here, reference)
        scale = jnp.exp(jnp.where(upper, before - reference, reference - run))
        pairs = (t // (2 * half) == i // (2 * half)) & (t % (2 * half) >= half) & (i % (2 * half) < half)
        levels.append((jnp.where(upper, scale, 0.0), jnp.where(upper, 0.0, scale), pairs))
    reference = jnp.broadcast_to(row_of(run, 7), run.shape)
    for start in range(16, CHUNK, 16):
        here = jnp.broadcast_to(row_of(run, start + 7), run.shape)
        reference = jnp.where(rows >= start, here, reference)
    pairs = (t // 16 == i // 16) & (t > i)
    to_row = jnp.exp(jnp.minimum(before - reference, 80.0))
    to_prior = jnp.exp(jnp.minimum(reference - run, 80.0))
    levels.append((to_row, to_prior, pairs))
    return levels


def lower_ones():
    return jnp.where(iota2((CHUNK, CHUNK), 0) >= iota2((CHUNK, CHUNK), 1), 1.0, 0.0).astype(jnp.float32)


def decay_of(low_ref, up_ref, par_ref):
    log_decay = -jnp.exp(par_ref[0:1] + mxu(low_ref[...], up_ref[...], NT))
    run = run_sum(lower_ones(), log_decay)
    return log_decay, run, run - log_decay


def unit_heads(wkv, ones):
    centre = wkv - head_sum(wkv, ones) * (1.0 / GROUP_DIMENSION)
    rstd = lax.rsqrt(head_sum(centre * centre, ones) * (1.0 / GROUP_DIMENSION) + gn_eps)
    return centre * rstd, rstd


def lane_groups(refs, kinds):
    width = refs[0].shape[1]
    for g in range(width // PACK):
        lanes = pl.ds(g * PACK, PACK)
        part = {"c": lambda ref: ref.at[:, lanes], "r": lambda ref: ref.at[lanes], "s": lambda ref: ref.at[g]}
        yield [ref if kind == "w" else part[kind](ref) for ref, kind in zip(refs, kinds)]


def wkv_forward_kernel(*refs):
    for group in lane_groups(refs, "ccccwrcccccs"):
        forward_heads(*group)


def wkv_backward_kernel(*refs):
    for group in lane_groups(refs, "ccccwrccccccccccc" + "s"):
        backward_heads(*group)


def forward_heads(
    r_ref, k_ref, v_ref, gate_ref, low_ref, up_ref, par_ref, first_ref, mixed_ref, wkv_ref, held_ref, state
):
    ones = head_ones()

    @pl.when(pl.program_id(0) == 0)
    def _():
        state[...] = spread(first_ref[...], ones)

    r, k, v = r_ref[...], k_ref[...], v_ref[...]
    _, run, before = decay_of(low_ref, up_ref, par_ref)
    held_ref[...] = fold(state[...], ones)
    score = jnp.zeros((CHUNK, PACK), jnp.float32)
    for to_row, to_prior, pairs in piece_factors(run, before):
        score = jnp.where(pairs, mxu(r * to_row, spread(k * to_prior, ones), NT), score)
    out = mxu(score, spread(v, ones), NN) + mxu(r * jnp.exp(before), state[...], NT)
    out = out + head_sum(r * par_ref[1:2] * k, ones) * v
    wkv_ref[...] = out
    last = row_of(run, CHUNK - 1)
    state[...] = jnp.exp(last) * state[...] + mxu(v, k * jnp.exp(last - run), TN) * ones
    unit, _ = unit_heads(out, ones)
    gate = gate_ref[...]
    mixed_ref[...] = ((unit * par_ref[2:3] + par_ref[3:4]) * gate * jax.nn.sigmoid(gate)).astype(jnp.bfloat16)


def wkv_forward(r, k, v, gate, low, up, par, first):
    rows, columns = r.shape
    chunks = rows // CHUNK
    block = pl.BlockSpec((CHUNK, columns), lambda c: (c, 0))
    whole = lambda a: pl.BlockSpec(a.shape, lambda c: (0, 0))
    return pl.pallas_call(
        wkv_forward_kernel,
        grid=(chunks,),
        in_specs=[block] * 4
        + [
            pl.BlockSpec((CHUNK, low.shape[1]), lambda c: (c, 0)),
            whole(up),
            whole(par),
            whole(first),
        ],
        out_specs=[block, block, block],
        out_shape=[
            jax.ShapeDtypeStruct((rows, columns), jnp.bfloat16),
            jax.ShapeDtypeStruct((rows, columns), jnp.float32),
            jax.ShapeDtypeStruct((rows, columns), jnp.float32),
        ],
        scratch_shapes=[pltpu.VMEM((columns // PACK, PACK, PACK), jnp.float32)],
        compiler_params=pltpu.CompilerParams(
            dimension_semantics=("arbitrary",), vmem_limit_bytes=32 * 2**20
        ),
        cost_estimate=SOON,
        name="wkv_forward",
    )(r, k, v, gate, low, up, par, first)


def backward_heads(
    r_ref, k_ref, v_ref, gate_ref, low_ref, up_ref, par_ref, wkv_ref, held_ref, gm_ref,
    gr_ref, gk_ref, gv_ref, gg_ref, gw_ref, sums_ref, first_ref, state,
):
    ones = head_ones()

    @pl.when(pl.program_id(0) == 0)
    def _():
        state[...] = jnp.zeros_like(state)
        sums_ref[...] = jnp.zeros_like(sums_ref)

    r, k, v, gate = r_ref[...], k_ref[...], v_ref[...], gate_ref[...]
    bonus, gain = par_ref[1:2], par_ref[2:3]

    def add_to(row, values):
        sums_ref[row : row + 1] = sums_ref[row : row + 1] + jnp.sum(values, axis=0, keepdims=True)

    unit, rstd = unit_heads(wkv_ref[...], ones)
    sig = jax.nn.sigmoid(gate)
    g_mixed = gm_ref[...].astype(jnp.float32)
    g_grouped = g_mixed * gate * sig
    grouped = unit * gain + par_ref[3:4]
    gg_ref[...] = (g_mixed * grouped * sig * (1.0 + gate * (1.0 - sig))).astype(jnp.bfloat16)
    add_to(2, g_grouped * unit)
    add_to(3, g_grouped)
    g_unit = g_grouped * gain
    scale = 1.0 / GROUP_DIMENSION
    g_out = rstd * (
        g_unit - head_sum(g_unit, ones) * scale - unit * (head_sum(g_unit * unit, ones) * scale)
    )

    log_decay, run, before = decay_of(low_ref, up_ref, par_ref)
    last = row_of(run, CHUNK - 1)
    start = spread(held_ref[...], ones)
    end_grad = state[...]
    v_wide = spread(v, ones)
    g_score = mxu(g_out, v_wide, NT)
    score = jnp.zeros((CHUNK, PACK), jnp.float32)
    from_start = jnp.exp(before)
    g_r = from_start * mxu(g_out, start, NN)
    to_end = jnp.exp(last - run)
    g_end = to_end * mxu(v, end_grad, NN)
    g_k = g_end
    for to_row, to_prior, pairs in piece_factors(run, before):
        r_level = (r * to_row).astype(jnp.bfloat16)
        k_level = spread(k * to_prior, ones).astype(jnp.bfloat16)
        score = jnp.where(pairs, mxu(r_level, k_level, NT), score)
        g_level = jnp.where(pairs, g_score, 0.0).astype(jnp.bfloat16)
        g_r = g_r + to_row * mxu(g_level, k_level, NN)
        g_k = g_k + to_prior * fold(mxu(g_level, r_level, TN), ones)
    g_v = fold(mxu(score, g_out, TN), ones) + mxu(k * to_end, end_grad, NT)
    g_before = r * g_r
    g_run = g_before - k * g_k
    g_last = jnp.sum(k * g_end, axis=0, keepdims=True) + jnp.exp(last) * jnp.sum(
        start * end_grad, axis=0, keepdims=True
    )
    upper = jnp.where(iota2((CHUNK, CHUNK), 0) <= iota2((CHUNK, CHUNK), 1), 1.0, 0.0).astype(jnp.float32)
    g_decay = run_sum(upper, g_run) - g_before + g_last
    g_expo = g_decay * log_decay
    gw_ref[...] = g_expo.astype(jnp.bfloat16)
    add_to(0, g_expo)
    g_diag = head_sum(g_out * v, ones)
    add_to(1, r * k * g_diag)
    gr_ref[...] = (g_r + bonus * k * g_diag).astype(jnp.bfloat16)
    gk_ref[...] = (g_k + bonus * r * g_diag).astype(jnp.bfloat16)
    gv_ref[...] = (g_v + head_sum(r * bonus * k, ones) * g_out).astype(jnp.bfloat16)
    state[...] = jnp.exp(last) * end_grad + mxu(g_out, r * from_start, TN) * ones

    @pl.when(pl.program_id(0) == pl.num_programs(0) - 1)
    def _():
        first_ref[...] = fold(state[...], ones)


def wkv_backward(r, k, v, gate, low, up, par, wkv, held, g_mixed):
    rows, columns = r.shape
    chunks = rows // CHUNK
    block = pl.BlockSpec((CHUNK, columns), lambda c: (chunks - 1 - c, 0))
    whole = lambda a: pl.BlockSpec(a.shape, lambda c: (0, 0))
    of_all = lambda n: pl.BlockSpec((n, columns), lambda c: (0, 0))
    low_type = jax.ShapeDtypeStruct((rows, columns), jnp.bfloat16)
    return pl.pallas_call(
        wkv_backward_kernel,
        grid=(chunks,),
        in_specs=[block] * 4
        + [
            pl.BlockSpec((CHUNK, low.shape[1]), lambda c: (chunks - 1 - c, 0)),
            whole(up),
            whole(par),
            block,
            block,
            block,
        ],
        out_specs=[block] * 5 + [of_all(8), of_all(GROUP_DIMENSION)],
        out_shape=[low_type] * 5
        + [
            jax.ShapeDtypeStruct((8, columns), jnp.float32),
            jax.ShapeDtypeStruct((GROUP_DIMENSION, columns), jnp.float32),
        ],
        scratch_shapes=[pltpu.VMEM((columns // PACK, PACK, PACK), jnp.float32)],
        compiler_params=pltpu.CompilerParams(
            dimension_semantics=("arbitrary",), vmem_limit_bytes=32 * 2**20
        ),
        cost_estimate=SOON,
        name="wkv_backward",
    )(r, k, v, gate, low, up, par, wkv, held, g_mixed)


GRAD_ROWS, GRAD_COLUMNS = 512, 256


def grad_kernel(left_ref, right_ref, *rest):
    out_ref = rest[-1]
    turned = left_ref[...].T
    for at in range(0, out_ref.shape[1], GRAD_COLUMNS):
        columns = slice(at, at + GRAD_COLUMNS)
        out_ref[:, columns] = mxu(turned, right_ref[:, columns], NN).astype(jnp.bfloat16)


def grad_into(left, right, total, at, into=None):
    rows, width = left.shape
    columns = right.shape[1]
    shift = at // columns
    specs = [
        pl.BlockSpec((rows, GRAD_ROWS), lambda i: (0, i)),
        pl.BlockSpec((rows, columns), lambda i: (0, 0)),
    ]
    operands = [left, right]
    alias = {}
    if into is not None:
        specs.append(pl.BlockSpec(memory_space=pltpu.HBM))
        operands.append(into)
        alias = {2: 0}
    return pl.pallas_call(
        grad_kernel,
        grid=(width // GRAD_ROWS,),
        in_specs=specs,
        out_specs=pl.BlockSpec((GRAD_ROWS, columns), lambda i: (i, shift)),
        out_shape=pltpu.HBM((width, total), jnp.bfloat16),
        input_output_aliases=alias,
        compiler_params=pltpu.CompilerParams(
            dimension_semantics=("arbitrary",), vmem_limit_bytes=32 * 2**20
        ),
        cost_estimate=SOON,
        name="weight_grad",
    )(*operands)


def copy_kernel(block_ref, into_ref, out_ref):
    out_ref[...] = block_ref[...]


def copy_into(block, at, into):
    rows, columns = block.shape
    shift = at // columns
    return pl.pallas_call(
        copy_kernel,
        grid=(rows // GRAD_ROWS,),
        in_specs=[
            pl.BlockSpec((GRAD_ROWS, columns), lambda i: (i, 0)),
            pl.BlockSpec(memory_space=pltpu.HBM),
        ],
        out_specs=pl.BlockSpec((GRAD_ROWS, columns), lambda i: (i, shift)),
        out_shape=pltpu.HBM(into.shape, into.dtype),
        input_output_aliases={1: 0},
        compiler_params=pltpu.CompilerParams(dimension_semantics=("arbitrary",)),
        cost_estimate=SOON,
        name="copy_into",
    )(block, into)


LOW = 256
SHIFT_LANES = 5 * SHIFT_RANK
LANES = SHIFT_LANES + 64

TILE = 512


def vectors_kernel(up_ref, out_ref):
    turned = up_ref[...].astype(jnp.float32).T
    out_ref[...] = turned[LANES : LANES + 16]


def turn_vectors(first, up_at):
    width = first.shape[0]
    return pl.pallas_call(
        vectors_kernel,
        grid=(width // TILE,),
        in_specs=[pl.BlockSpec((TILE, LOW), lambda n: (n, up_at // LOW))],
        out_specs=pl.BlockSpec((16, TILE), lambda n: (0, n)),
        out_shape=jax.ShapeDtypeStruct((16, width), jnp.float32),
        compiler_params=pltpu.CompilerParams(dimension_semantics=("arbitrary",)),
        cost_estimate=SOON,
        name="turn_vectors",
    )(first)


def lane_group(shape):
    return iota2(shape, 1) // SHIFT_RANK


def mixes_forward_kernel(
    unit_ref, w_ref, down_ref, up_ref, vec_ref,
    m0_ref, m1_ref, m2_ref, m3_ref, m4_ref, normed_ref, squash_ref, r_ref, k_ref, v_ref, g_ref,
    hidden, grouped,
):
    phase, tile = pl.program_id(0), pl.program_id(1)
    rows = unit_ref.shape[0]
    own = r_ref.shape[1]
    vec = vec_ref[...]
    normed = unit_ref[...] * vec[0:1] + vec[1:2]
    row = iota2(normed.shape, 0)
    shifted = jnp.where(row == 0, 0.0, pltpu.roll(normed, 1, 0)) - normed
    down = down_ref[...]
    of_shift = iota2(down.shape, 1) < SHIFT_LANES

    @pl.when((phase == 0) & (tile == 0))
    def _():
        hidden[...] = jnp.zeros_like(hidden)

    @pl.when(phase == 0)
    def _():
        hidden[...] = hidden[...] + mxu(normed + shifted * vec[2:3], jnp.where(of_shift, down, 0), NN)

    @pl.when((phase == 1) & (tile == 0))
    def _():
        squash = jnp.tanh(hidden[...])
        squash_ref[...] = squash
        group = lane_group(squash.shape)
        for g in range(5):
            grouped[g] = jnp.where(group == g, squash, 0.0).astype(jnp.bfloat16)
        hidden[...] = jnp.zeros_like(hidden)
        for ref in (r_ref, k_ref, v_ref, g_ref):
            ref[...] = jnp.zeros_like(ref)

    @pl.when(phase == 1)
    def _():
        normed_ref[...] = normed
        up = up_ref[...]
        for g, mix_ref in enumerate((m0_ref, m1_ref, m2_ref, m3_ref, m4_ref)):
            mix = (normed + shifted * (vec[3 + g : 4 + g] + mxu(grouped[g], up, NT))).astype(jnp.bfloat16)
            mix_ref[...] = mix
            if g == 0:
                hidden[...] = hidden[...] + mxu(mix, jnp.where(of_shift, 0, down), NN)
            else:
                column = (None, 1, 2, 0, 3)[g] * own
                out = (None, k_ref, v_ref, r_ref, g_ref)[g]
                out[...] = out[...] + mxu(mix, w_ref[:, column : column + own], NN)

    @pl.when((phase == 1) & (tile == pl.num_programs(1) - 1))
    def _():
        squash_ref[...] = squash_ref[...] + jnp.tanh(hidden[...])


def mixes_forward(unit, first, low_at, vec, own):
    rows, width = unit.shape
    tiles = width // TILE
    block = low_at // LOW
    across = lambda r: pl.BlockSpec((r, TILE), lambda p, n: (0, n))
    late = pl.BlockSpec((rows, TILE), lambda p, n: (0, n * p))
    whole = lambda columns: pl.BlockSpec((rows, columns), lambda p, n: (0, 0))
    kept = lambda columns, dtype: jax.ShapeDtypeStruct((rows, columns), dtype)
    return pl.pallas_call(
        mixes_forward_kernel,
        grid=(2, tiles),
        in_specs=[
            across(rows),
            pl.BlockSpec((TILE, 4 * own), lambda p, n: (n * p, 0)),
            pl.BlockSpec((TILE, LOW), lambda p, n: (n, block)),
            pl.BlockSpec((TILE, LOW), lambda p, n: (n, block + 1)),
            across(vec.shape[0]),
        ],
        out_specs=[late] * 6 + [whole(LOW)] + [whole(own)] * 4,
        out_shape=[kept(width, jnp.bfloat16)] * 5
        + [kept(width, jnp.float32), kept(LOW, jnp.float32)]
        + [kept(own, jnp.float32)] * 4,
        scratch_shapes=[pltpu.VMEM((rows, LOW), jnp.float32), pltpu.VMEM((5, rows, LOW), jnp.bfloat16)],
        compiler_params=pltpu.CompilerParams(
            dimension_semantics=("arbitrary", "arbitrary"), vmem_limit_bytes=54 * 2**20
        ),
        cost_estimate=SOON,
        name="mixes_forward",
    )(unit, first, first, first, vec)


def mixes_back_kernel(
    gk_ref, gv_ref, gr_ref, gg_ref, gd_ref, w_ref, down_ref, up_ref, vec_ref, squash_ref, normed_ref,
    mix_ref, sums_ref, out_ref, small_ref,
    g_shift, g_norm, g_squash, g_hidden, g_up, g_sums, grouped, turned,
):
    phase, tile = pl.program_id(0), pl.program_id(1)
    rows = squash_ref.shape[0]
    own = gk_ref.shape[1]
    normed = normed_ref[...]
    row = iota2(normed.shape, 0)
    shifted = jnp.where(row == 0, 0.0, pltpu.roll(normed, 1, 0)) - normed
    squash = squash_ref[...]
    vec = vec_ref[...]

    @pl.when((phase == 0) & (tile == 0))
    def _():
        g_squash[...] = jnp.zeros_like(g_squash)
        group = lane_group(squash.shape)
        for g in range(5):
            grouped[g] = jnp.where(group == g, squash, 0.0).astype(jnp.bfloat16)
        turned[...] = squash.astype(jnp.bfloat16).T

    @pl.when(phase == 0)
    def _():
        up = up_ref[...]
        group_wide = lane_group(up.shape)
        total_shift = jnp.zeros((rows, TILE), jnp.float32)
        total_norm = jnp.zeros((rows, TILE), jnp.float32)
        add_squash = jnp.zeros((rows, LOW), jnp.float32)
        sums = []
        for g in range(5):
            if g == 0:
                part = mxu(gd_ref[...], down_ref[...], NT)
            else:
                column = (None, 1, 2, 0, 3)[g] * own
                grad = (None, gk_ref, gv_ref, gr_ref, gg_ref)[g]
                part = mxu(grad[...], w_ref[:, column : column + own], NT)
            coeff = vec[3 + g : 4 + g] + mxu(grouped[g], up, NT)
            times = part * shifted
            times_low = times.astype(jnp.bfloat16)
            sums.append(jnp.sum(times, axis=0, keepdims=True))
            total_shift = total_shift + part * coeff
            total_norm = total_norm + part
            add_squash = add_squash + mxu(times_low, jnp.where(group_wide == g, up, 0), NN)
            lanes = slice(g * SHIFT_RANK, (g + 1) * SHIFT_RANK)
            g_up[tile, lanes] = mxu(turned[lanes], times_low, NN)
        g_shift[tile] = total_shift
        g_norm[tile] = total_norm
        g_squash[...] = g_squash[...] + add_squash
        g_sums[tile] = jnp.concatenate(sums + [jnp.zeros((3, TILE), jnp.float32)], axis=0)

    @pl.when((phase == 1) & (tile == 0))
    def _():
        g_hidden[...] = (g_squash[...] * (1.0 - squash * squash)).astype(jnp.bfloat16)

    @pl.when(phase == 1)
    def _():
        blend = vec[2:3]
        part = mxu(g_hidden[...], down_ref[...], NT)
        total_shift = g_shift[tile] + part * blend
        total = g_norm[tile] + part - total_shift
        total = total + jnp.where(row == rows - 1, 0.0, pltpu.roll(total_shift, rows - 1, 0))
        out_ref[...] = total.astype(jnp.bfloat16)
        unit = (normed - vec[1:2]) / vec[0:1]
        head = [
            jnp.sum(total * unit, axis=0, keepdims=True),
            jnp.sum(total, axis=0, keepdims=True),
            jnp.sum(part * shifted, axis=0, keepdims=True),
        ]
        sums = jnp.concatenate(head + [g_sums[tile][:5], sums_ref[...]], axis=0)
        shape = (sums.shape[0], LOW)
        behind = jnp.where(iota2(shape, 1) == LANES + iota2(shape, 0), 1.0, 0.0)
        small_ref[:, :LOW] = (
            mxu(normed + shifted * blend, g_hidden[...], TN) + mxu(mix_ref[...], gd_ref[...], TN)
        ).astype(jnp.bfloat16)
        small_ref[:, LOW:] = mxu(sums, behind, TN).astype(jnp.bfloat16)
        small_ref[:, LOW : LOW + SHIFT_LANES] = g_up[tile].T.astype(jnp.bfloat16)


def mixes_back(g_key, g_val, g_recept, g_gate, g_decay, first, low_at, vec, squash, normed, mix, sums):
    rows, width = normed.shape
    own = g_key.shape[1]
    tiles = width // TILE
    block = low_at // LOW
    whole = lambda a: pl.BlockSpec(a.shape, lambda p, n: (0, 0))
    across = lambda r: pl.BlockSpec((r, TILE), lambda p, n: (0, n))
    late = lambda r: pl.BlockSpec((r, TILE), lambda p, n: (0, n * p))
    early = lambda p, n: n * (1 - p) + (tiles - 1) * p
    return pl.pallas_call(
        mixes_back_kernel,
        grid=(2, tiles),
        in_specs=[whole(g_key)] * 4
        + [
            whole(g_decay),
            pl.BlockSpec((TILE, 4 * own), lambda p, n: (early(p, n), 0)),
            pl.BlockSpec((TILE, LOW), lambda p, n: (n, block)),
            pl.BlockSpec((TILE, LOW), lambda p, n: (early(p, n), block + 1)),
            across(vec.shape[0]),
            whole(squash),
            across(rows),
            late(rows),
            late(sums.shape[0]),
        ],
        out_specs=[late(rows), pl.BlockSpec((TILE, 2 * LOW), lambda p, n: (n * p, 0))],
        out_shape=[
            jax.ShapeDtypeStruct((rows, width), jnp.bfloat16),
            jax.ShapeDtypeStruct((width, 2 * LOW), jnp.bfloat16),
        ],
        scratch_shapes=[
            pltpu.VMEM((tiles, rows, TILE), jnp.float32),
            pltpu.VMEM((tiles, rows, TILE), jnp.float32),
            pltpu.VMEM((rows, LOW), jnp.float32),
            pltpu.VMEM((rows, LOW), jnp.bfloat16),
            pltpu.VMEM((tiles, SHIFT_LANES, TILE), jnp.float32),
            pltpu.VMEM((tiles, 8, TILE), jnp.float32),
            pltpu.VMEM((5, rows, LOW), jnp.bfloat16),
            pltpu.VMEM((LOW, rows), jnp.bfloat16),
        ],
        compiler_params=pltpu.CompilerParams(
            dimension_semantics=("arbitrary", "arbitrary"), vmem_limit_bytes=56 * 2**20
        ),
        cost_estimate=SOON,
        name="mixes_back",
    )(g_key, g_val, g_recept, g_gate, g_decay, first, first, first, vec, squash, normed, mix, sums)


def shards(
    inputs,
    cotangent,
    states,
    vectors,
    time_mix_weight,
    output_weight,
    channel_receptance_weight,
    rank_down_weight,
    rank_up_weight,
    channel_key_weight,
    channel_value_weight,
):
    token_rows, width = inputs.shape
    seg_count = lax.axis_size("seg")
    own_width = time_mix_weight.shape[2]
    hidden = channel_key_weight.shape[1]
    local_heads = own_width // GROUP_DIMENSION
    col_start = lax.axis_index("span") * own_width
    position = lax.axis_index("span") * token_rows

    x_seg = span_gather(inputs).astype(jnp.float32)
    grad_columns = split_columns(cotangent).astype(jnp.float32)
    def blank(count):
        return jnp.zeros((token_rows // 8, count), jnp.bfloat16)

    small_rows = jnp.concatenate(
        [rank_down_weight, blank(LOW - LANES), rank_up_weight.T, vectors.T, blank(LOW - LANES - 16)], axis=1
    )
    early, span_rows = gather_and_split(small_rows, channel_receptance_weight)
    _, time_mix_weight = lax.optimization_barrier((early, time_mix_weight))
    weights = both_planes(lambda proj: [proj[g] for g in range(4)], time_mix_weight)
    small_pair = both_planes(lambda rows: [rows], span_rows[:, own_width:])
    late_pairs = [fill_pair(rows[None])[0] for rows in (output_weight.T, span_rows[:, :own_width])]
    first = plane_gather(jnp.concatenate([weights, small_pair] + late_pairs, axis=1))
    _, unit_seg, _ = norm_rows(x_seg, 1.0, 0.0)
    second_pair = both_planes(lambda key, value: [key, value.T], channel_key_weight, channel_value_weight)
    second_pair, unit_seg, grad_columns = lax.optimization_barrier((second_pair, unit_seg, grad_columns))
    second = plane_gather(second_pair)
    low_at = 4 * own_width
    late_at = low_at + 2 * LOW

    def late_rows(at):
        pairs = first[:, at : at + own_width // 2].reshape(-1, 2 * (width // seg_count), own_width // 2)
        return from_pair(pairs)

    out_half, recept_half = late_rows(late_at), late_rows(late_at + own_width // 2)
    late_got = swap_high(jnp.concatenate([out_half, recept_half], axis=2))
    out_got, recept_got = late_got[:, :, :own_width], late_got[:, :, own_width:]
    up_at = low_at + LOW
    vec = first[:, up_at + LANES : up_at + LANES + 16].T.astype(jnp.float32)

    def own_cols(line):
        return lax.dynamic_slice_in_dim(line, col_start, own_width, line.ndim - 1)

    def own_rows(values):
        return lax.dynamic_slice_in_dim(values, position, token_rows, 0)

    x_in = inputs.astype(jnp.float32)
    *mixes, normed, squash, recept, key_proj, val_proj, gate_pre = mixes_forward(
        unit_seg, first, low_at, vec, own_width
    )
    lane = lax.broadcasted_iota(jnp.int32, squash.shape, 1)
    of_decay = (lane >= SHIFT_LANES) & (lane < LANES)
    decay_low = jnp.where(of_decay, squash, 0.0).astype(jnp.bfloat16)
    up_own = lax.dynamic_slice(first, (col_start, up_at), (own_width, LOW))
    head_vec = jnp.concatenate([own_cols(vec[8:12]), jnp.zeros((4, own_width), jnp.float32)], axis=0)
    first_state = jnp.transpose(states[0], (2, 0, 1)).reshape(GROUP_DIMENSION, own_width)
    out_w = other_plane(out_half, out_got)
    heads_in = (recept, key_proj, val_proj, gate_pre, decay_low, up_own, head_vec)
    mixed, wkv, held = wkv_forward(*heads_in, first_state)
    recept_w = other_plane(recept_half, recept_got)
    resid = x_in + span_reduce(backward_product(mixed, out_w).astype(jnp.bfloat16))

    normed_two, unit_two, rstd_two = norm_rows(resid, vec[12], vec[13])
    n2 = span_gather(normed_two.astype(jnp.bfloat16)).astype(jnp.float32)
    shifted_two = prior_rows(n2) - n2
    key_in = (n2 + shifted_two * vec[14]).astype(jnp.bfloat16)
    rec_in = (n2 + shifted_two * vec[15]).astype(jnp.bfloat16)
    rec_gate = jax.nn.sigmoid(product_lower(rec_in, recept_w))
    g_value = (grad_columns * rec_gate).astype(jnp.bfloat16)
    g_value, second = lax.optimization_barrier((g_value, second))
    g_value_all = span_gather(g_value, 1)
    key_w, value_w = second[:, :hidden], second[:, hidden:]
    hidden_two = product_lower(key_in, key_w)
    active = jax.nn.relu(hidden_two)
    squared = (active * active).astype(jnp.bfloat16)
    active = active.astype(jnp.bfloat16)

    low = lax.axis_index("span") // 2

    def value_columns(which):
        weights = lax.dynamic_slice(second, (which * (width // 2), hidden), (width // 2, hidden))
        return core_reduce(backward_product(squared, weights).astype(jnp.bfloat16))

    far, near = value_columns(1 - low), value_columns(low)
    far, g_value_all = lax.optimization_barrier((far.astype(jnp.bfloat16), g_value_all))
    far = swap_low(far)
    cm_total = 2 * hidden
    g_hid = (product_lower(g_value_all, value_w) * 2.0 * active.astype(jnp.float32)).astype(jnp.bfloat16)
    g_value_all, g_hid = lax.optimization_barrier((g_value_all, g_hid))
    cm_part = grad_into(g_value_all, squared, cm_total, hidden)
    far, near, cm_part = lax.optimization_barrier((far, near, cm_part))
    cm_part = grad_into(key_in, g_hid, cm_total, 0, cm_part)
    cm_part, g_hid = lax.optimization_barrier((cm_part, g_hid))
    cm_pair = plane_scatter(cm_part)
    value_out = near + far.astype(jnp.float32)
    gated = (rec_gate * value_out).astype(jnp.bfloat16)
    g_rec = (grad_columns * value_out * rec_gate * (1.0 - rec_gate)).astype(jnp.bfloat16)
    g_key_in = backward_product(g_hid, key_w)
    g_rec_in = backward_product(g_rec, recept_w)
    vec_fourteen = jnp.sum(g_key_in * shifted_two, axis=0)
    vec_fifteen = jnp.sum(g_rec_in * shifted_two, axis=0)
    g_shift_two = g_key_in * vec[14] + g_rec_in * vec[15]
    g_n2_part = g_key_in + g_rec_in - g_shift_two + next_rows(g_shift_two)
    g_n2 = span_reduce(g_n2_part.astype(jnp.bfloat16))
    rec_part = grad_into(rec_in, g_rec, own_width, 0)
    g_n2, rec_part = lax.optimization_barrier((g_n2, rec_part))
    vec_twelve = jnp.sum(g_n2 * unit_two, axis=0)
    vec_thirteen = jnp.sum(g_n2, axis=0)
    g_resid = cotangent.astype(jnp.float32) + norm_back(g_n2, unit_two, rstd_two, vec[12])

    g_att = span_gather(g_resid.astype(jnp.bfloat16))
    rec_part = rec_part.reshape(seg_count // 2, 2, width // seg_count, own_width)
    rec_mine, rec_send = in_order(rec_part[:, 0], rec_part[:, 1], lax.axis_index("seg") % 2 == 1)
    g_att, gated, rec_send = lax.optimization_barrier((g_att, gated, rec_send))
    rec_got = swap_high(rec_send)
    gated_rows = join_columns(gated)
    g_mixed = product_lower(g_att, out_w)
    g_recept, g_key, g_val, g_gate, g_ww, head_sums, g_first = wkv_backward(
        *heads_in, wkv, held, g_mixed
    )
    state_grad = jnp.transpose(
        g_first.reshape(GROUP_DIMENSION, local_heads, GROUP_DIMENSION), (1, 2, 0)
    )[None]
    tm_total = 5 * own_width + own_width // 2
    tm_part = grad_into(g_att, mixed, tm_total, 0)
    rec_got, g_recept = lax.optimization_barrier((rec_got, g_recept))
    rec_sum = (rec_mine.astype(jnp.float32) + rec_got.astype(jnp.float32)).astype(jnp.bfloat16)
    tm_part = lax.dynamic_update_slice(
        tm_part, fill_pair(rec_sum).reshape(width, own_width // 2), (0, 5 * own_width)
    )
    for at, mix, grad in ((1, 3, g_recept), (2, 1, g_key), (3, 2, g_val), (4, 4, g_gate)):
        tm_part = grad_into(mixes[mix], grad, tm_total, at * own_width, tm_part)
    tm_part, cm_pair, gated_rows = lax.optimization_barrier((tm_part, cm_pair, gated_rows))
    output = (resid + gated_rows.astype(jnp.float32)).astype(jnp.bfloat16)
    tm_pair = plane_scatter(tm_part)
    g_key, g_ww, cm_pair = lax.optimization_barrier((g_key, g_ww, cm_pair))

    g_decay_hidden = jnp.where(
        of_decay, product_lower(g_ww, up_own) * (1.0 - squash * squash), 0.0
    ).astype(jnp.bfloat16)
    up_decay_grad = outer_sum(g_ww, decay_low)
    other_sums = jnp.concatenate(
        [
            lax.dynamic_update_slice_in_dim(jnp.zeros((4, width), jnp.float32), head_sums[:4], col_start, 1),
            jnp.stack([vec_twelve, vec_thirteen, vec_fourteen, vec_fifteen]),
        ],
        axis=0,
    )
    g_normed, small_part = mixes_back(
        g_key, g_val, g_recept, g_gate, g_decay_hidden, first, low_at, vec, squash, normed, mixes[0], other_sums
    )
    own_part = lax.dynamic_slice(small_part, (col_start, LOW), (own_width, LOW))
    small_part = lax.dynamic_update_slice(
        small_part, (own_part.astype(jnp.float32) + up_decay_grad).astype(jnp.bfloat16), (col_start, LOW)
    )
    small, g_n1, cm_grad = reduce_small(small_part, over_cores(g_normed), cm_pair)
    rec_own = from_pair(tm_pair[None, :, 5 * own_width :])[0]
    tm_grad = finish_scatter(*plane_halves(tm_pair[:, : 5 * own_width]))
    _, unit_own, rstd_own = norm_rows(x_in, vec[0], vec[1])
    x_grad = g_resid + norm_back(g_n1, unit_own, rstd_own, vec[0])
    down_grad = small[:, :LANES]
    up_grad = small[:, LOW : LOW + LANES].T
    vec_grad = small[:, LOW + LANES : LOW + LANES + 16].T
    rec_grad = join_columns(rec_own).astype(jnp.float32)
    value_grad = cm_grad[:, hidden:].T
    key_grad = cm_grad[:, :hidden]
    out_grad = tm_grad[:, :own_width].T
    proj_grad = jnp.moveaxis(tm_grad[:, own_width : 5 * own_width].reshape(-1, 4, own_width), 1, 0)
    return (
        output,
        x_grad,
        state_grad,
        vec_grad,
        proj_grad,
        out_grad,
        rec_grad,
        down_grad,
        up_grad,
        key_grad,
        value_grad,
    )


def solution(mesh):
    rows, columns = P(ALL, None), P(None, ALL)
    state = P("seg", "span", None, None)
    time_mix = P(None, "seg", "span")
    turned, straight = P("span", "seg"), P("seg", "span")
    return jax.shard_map(
        shards,
        mesh=mesh,
        in_specs=(
            rows, rows, state, columns, time_mix, turned, rows, rows, columns, straight, turned
        ),
        out_specs=(
            rows, rows, state, columns, time_mix, turned, rows, rows, columns, straight, turned
        ),
        check_vma=False,
    )
```

```python
import jax
import jax.numpy as jnp
from jax import lax
from jax.experimental import pallas as pl
from jax.experimental.pallas import tpu as pltpu
from jax.experimental.layout import Layout, with_layout_constraint
from jax.sharding import PartitionSpec as P

GROUP_DIMENSION = 64
SHIFT_RANK = 32
ALL = ("seg", "span")

maximal_accuracy = lax.Precision.HIGHEST
ln_eps = 1e-05
gn_eps = 0.00064


def swap(block, bit):
    count = lax.axis_size("seg") * lax.axis_size("span")
    return lax.ppermute(block, ALL, [(i, i ^ bit) for i in range(count)])


def swap_core(block):
    return swap(block, 1)


def swap_low(block):
    return swap(block, 2)


def swap_high(block):
    return swap(block, 4)


def plane_groups():
    half = lax.axis_size("seg") // 2
    return [[2 * j + h for j in range(half)] for h in range(2)]


def in_order(own, other, second):
    return jnp.where(second, other, own), jnp.where(second, own, other)


def span_gather(block, axis=0):
    place = lax.axis_index("span")
    low, core = place // 2, place % 2
    p0, p1 = in_order(block, swap_low(block), low == 1)
    q = swap_core(jnp.stack([p0, p1]))
    a0, a1 = in_order(p0, q[0], core == 1)
    b0, b1 = in_order(p1, q[1], core == 1)
    return jnp.concatenate([a0, a1, b0, b1], axis=axis)


def core_reduce(part):
    core = lax.axis_index("span") % 2
    half = part.shape[1] // 2
    keep, send = in_order(part[:, :half], part[:, half:], core == 1)
    return keep.astype(jnp.float32) + swap_core(send.astype(jnp.bfloat16)).astype(jnp.float32)


def over_cores(part):
    core = lax.axis_index("span") % 2
    b = part.reshape(2, 2, part.shape[0] // 4, part.shape[1])
    keep, send = in_order(b[:, 0], b[:, 1], core == 1)
    return keep.astype(jnp.float32) + swap_core(send.astype(jnp.bfloat16)).astype(jnp.float32)


def over_low(both):
    low = lax.axis_index("span") // 2
    mine, send = in_order(both[0], both[1], low == 1)
    return mine + swap_low(send.astype(jnp.bfloat16)).astype(jnp.float32)


def span_reduce(part):
    return over_low(over_cores(part))


def fill_pair(rows):
    half = rows.shape[2] // 2
    return jnp.concatenate([rows[:, :, :half], rows[:, :, half:]], axis=1)


def from_pair(pairs):
    half = pairs.shape[1] // 2
    return jnp.concatenate([pairs[:, :half], pairs[:, half:]], axis=2)


def other_plane(rows, got):
    high = lax.axis_index("seg") % 2
    return jnp.stack(in_order(rows, got, high == 1), axis=1).reshape(-1, rows.shape[2])


def both_planes(laid, *blocks):
    high = lax.axis_index("seg") % 2
    own, other = (
        jnp.concatenate(laid(*got), axis=1) for got in (blocks, [swap_high(block) for block in blocks])
    )
    return jnp.concatenate(in_order(own, other, high == 1), axis=0)


def plane_gather(pair):
    whole = lax.all_gather(
        pair,
        "seg",
        axis=0,
        tiled=True,
        axis_index_groups=plane_groups(),
    )
    return with_layout_constraint(whole, Layout(major_to_minor=(0, 1)))


def plane_scatter(part):
    return lax.psum_scatter(
        part, "seg", scatter_dimension=0, tiled=True, axis_index_groups=plane_groups()
    )


def plane_halves(pair):
    high = lax.axis_index("seg") % 2
    rows = pair.shape[0] // 2
    return in_order(pair[:rows], pair[rows:], high == 1)


def finish_scatter(mine, send):
    return mine.astype(jnp.float32) + swap_high(send).astype(jnp.float32)


def gather_and_split(small, wide):
    place = lax.axis_index("span")
    n = wide.shape[1] // 4
    messages = [
        jnp.concatenate([lax.dynamic_slice_in_dim(wide, (place ^ bit) * n, n, 1), small], axis=1)
        for bit in range(4)
    ]
    pieces = [m if bit == 0 else swap(m, bit) for bit, m in enumerate(messages)]
    result = jnp.zeros((4, *messages[0].shape), small.dtype)
    for bit, piece in enumerate(pieces):
        result = lax.dynamic_update_index_in_dim(result, piece, place ^ bit, 0)
    return result.reshape(4 * small.shape[0], -1)


def split_columns(block):
    place = lax.axis_index("span")
    n = block.shape[1] // 4

    def columns(at):
        return lax.dynamic_slice_in_dim(block, at * n, n, 1)

    pieces = [columns(place)] + [swap(columns(place ^ bit), bit) for bit in (1, 2, 3)]
    result = jnp.zeros((4, block.shape[0], n), block.dtype)
    for bit, piece in enumerate(pieces):
        result = lax.dynamic_update_index_in_dim(result, piece, place ^ bit, 0)
    return result.reshape(4 * block.shape[0], n)


def join_columns(block):
    place = lax.axis_index("span")
    r, n = block.shape[0] // 4, block.shape[1]

    def rows(at):
        return lax.dynamic_slice_in_dim(block, at * r, r, 0)

    result = jnp.zeros((r, 4 * n), block.dtype)
    for bit in range(4):
        piece = rows(place ^ bit)
        if bit:
            piece = swap(piece, bit)
        result = lax.dynamic_update_slice_in_dim(result, piece, (place ^ bit) * n, 1)
    return result


def product_lower(left_arg, right_arg):
    return jnp.dot(left_arg, right_arg, preferred_element_type=jnp.float32)


def outer_sum(left_arg, right_arg):
    return jnp.einsum("td,te->de", left_arg, right_arg, preferred_element_type=jnp.float32)


def backward_product(gradient, weights):
    return jnp.einsum("te,de->td", gradient, weights, preferred_element_type=jnp.float32)


def norm_rows(values, gain_vec, offset):
    centre = values - jnp.mean(values, -1, keepdims=True)
    row_rstd = lax.rsqrt(jnp.mean(centre * centre, -1, keepdims=True) + ln_eps)
    unit_rows = centre * row_rstd
    return (unit_rows * gain_vec + offset, unit_rows, row_rstd)


def norm_back(gradient, unit_rows, row_rstd, gain_vec):
    scaled = gradient * gain_vec
    return row_rstd * (
        scaled
        - jnp.mean(scaled, -1, keepdims=True)
        - unit_rows * jnp.mean(scaled * unit_rows, -1, keepdims=True)
    )


def prior_rows(values):
    return jnp.concatenate([jnp.zeros_like(values[:1]), values[:-1]], axis=0)


def next_rows(values):
    return jnp.concatenate([values[1:], jnp.zeros_like(values[:1])], axis=0)


def reduce_small(part, both, pair):
    place, high = lax.axis_index("span"), lax.axis_index("seg") % 2
    planes = lax.axis_size("seg") // 2
    width = part.shape[1]
    b = part.reshape(planes, 2, 2, 2, -1, width)

    def summed(b, dim, bit, move):
        at0, at1 = (lax.index_in_dim(b, k, dim, keepdims=False) for k in (0, 1))
        mine, send = in_order(at0, at1, bit == 1)
        return mine.astype(jnp.float32) + move(send.astype(jnp.bfloat16)).astype(jnp.float32)

    b = summed(summed(b, 3, place % 2, swap_core), 2, place // 2, swap_low)
    b, both = lax.optimization_barrier((b, both))
    rows = over_low(both)
    b = summed(b, 1, high, swap_high).astype(jnp.bfloat16)
    b, pair = lax.optimization_barrier((b, pair))
    finished = finish_scatter(*plane_halves(pair))
    arrived = lax.all_to_all(
        b, "seg", split_axis=0, concat_axis=0, tiled=True, axis_index_groups=plane_groups()
    )
    return arrived.astype(jnp.float32).sum(axis=0), rows, finished


SOON = pl.CostEstimate(flops=2**20, bytes_accessed=2**16, transcendentals=0)

CHUNK = 64
PACK = 256


def mxu(a, b, contract):
    return lax.dot_general(
        a.astype(jnp.bfloat16),
        b.astype(jnp.bfloat16),
        (contract, ((), ())),
        preferred_element_type=jnp.float32,
    )


NN, NT, TN = ((1,), (0,)), ((1,), (1,)), ((0,), (0,))


def halves(values):
    high = values.astype(jnp.bfloat16)
    return high, (values - high.astype(jnp.float32)).astype(jnp.bfloat16)


def iota2(shape, dim):
    return lax.broadcasted_iota(jnp.int32, shape, dim)


def head_ones():
    shape = (PACK, PACK)
    same = (iota2(shape, 0) ^ iota2(shape, 1)) < GROUP_DIMENSION
    return jnp.where(same, 1.0, 0.0).astype(jnp.float32)


def spread(block, ones):
    return jnp.concatenate([block] * (PACK // CHUNK), axis=0) * ones


def fold(big, ones):
    kept = big * ones
    total = kept[:CHUNK]
    for h in range(1, PACK // CHUNK):
        total = total + kept[h * CHUNK : (h + 1) * CHUNK]
    return total


def head_sum(values, ones):
    high, rest = halves(values)
    return mxu(high, ones, NN) + mxu(rest, ones, NN)


def run_sum(which, values):
    high, rest = halves(values)
    return mxu(which, high, NN) + mxu(which, rest, NN)


def row_of(values, row):
    return values[row : row + 1]


def piece_factors(run, before):
    rows = iota2((CHUNK, PACK), 0)
    t, i = rows, iota2((CHUNK, PACK), 1) & (CHUNK - 1)
    apart = t ^ i
    levels = []
    for half in (32, 16):
        upper = (rows & half) != 0
        reference = jnp.broadcast_to(row_of(run, half - 1), run.shape)
        for start in range(2 * half, CHUNK, 2 * half):
            here = jnp.broadcast_to(row_of(run, start + half - 1), run.shape)
            reference = jnp.where(rows >= start, here, reference)
        scale = jnp.exp(jnp.where(upper, before - reference, reference - run))
        pairs = (apart < 2 * half) & upper & ((apart & half) != 0)
        levels.append((jnp.where(upper, scale, 0.0), jnp.where(upper, 0.0, scale), pairs))
    reference = jnp.broadcast_to(row_of(run, 7), run.shape)
    for start in range(16, CHUNK, 16):
        here = jnp.broadcast_to(row_of(run, start + 7), run.shape)
        reference = jnp.where(rows >= start, here, reference)
    pairs = (apart < 16) & (t > i)
    to_row = jnp.exp(jnp.minimum(before - reference, 80.0))
    to_prior = jnp.exp(jnp.minimum(reference - run, 80.0))
    levels.append((to_row, to_prior, pairs))
    return levels


def lower_ones():
    return jnp.where(iota2((CHUNK, CHUNK), 0) >= iota2((CHUNK, CHUNK), 1), 1.0, 0.0).astype(jnp.float32)


def decay_of(low_ref, up_ref, par_ref):
    log_decay = -jnp.exp(par_ref[0:1] + mxu(low_ref[...], up_ref[...], NT))
    run = run_sum(lower_ones(), log_decay)
    return log_decay, run, run - log_decay


def unit_heads(wkv, ones):
    centre = wkv - head_sum(wkv, ones) * (1.0 / GROUP_DIMENSION)
    rstd = lax.rsqrt(head_sum(centre * centre, ones) * (1.0 / GROUP_DIMENSION) + gn_eps)
    return centre * rstd, rstd


def lane_groups(refs, kinds):
    width = refs[0].shape[1]
    for g in range(width // PACK):
        lanes = pl.ds(g * PACK, PACK)
        part = {"c": lambda ref: ref.at[:, lanes], "r": lambda ref: ref.at[lanes], "s": lambda ref: ref.at[g]}
        yield [ref if kind == "w" else part[kind](ref) for ref, kind in zip(refs, kinds)]


def wkv_forward_kernel(*refs):
    for group in lane_groups(refs, "ccccwrcccccs"):
        forward_heads(*group)


def wkv_backward_kernel(*refs):
    for group in lane_groups(refs, "ccccwrccccccccccc" + "s"):
        backward_heads(*group)


def forward_heads(
    r_ref, k_ref, v_ref, gate_ref, low_ref, up_ref, par_ref, first_ref, mixed_ref, wkv_ref, held_ref, state
):
    ones = head_ones()

    @pl.when(pl.program_id(0) == 0)
    def _():
        state[...] = spread(first_ref[...], ones)

    r, k, v = r_ref[...], k_ref[...], v_ref[...]
    _, run, before = decay_of(low_ref, up_ref, par_ref)
    held_ref[...] = fold(state[...], ones)
    score = jnp.zeros((CHUNK, PACK), jnp.float32)
    for to_row, to_prior, pairs in piece_factors(run, before):
        score = jnp.where(pairs, mxu(r * to_row, spread(k * to_prior, ones), NT), score)
    out = mxu(score, spread(v, ones), NN) + mxu(r * jnp.exp(before), state[...], NT)
    out = out + head_sum(r * par_ref[1:2] * k, ones) * v
    wkv_ref[...] = out
    last = row_of(run, CHUNK - 1)
    state[...] = jnp.exp(last) * state[...] + mxu(v, k * jnp.exp(last - run), TN) * ones
    unit, _ = unit_heads(out, ones)
    gate = gate_ref[...]
    mixed_ref[...] = ((unit * par_ref[2:3] + par_ref[3:4]) * gate * jax.nn.sigmoid(gate)).astype(jnp.bfloat16)


def wkv_forward(r, k, v, gate, low, up, par, first):
    rows, columns = r.shape
    chunks = rows // CHUNK
    block = pl.BlockSpec((CHUNK, columns), lambda c: (c, 0))
    whole = lambda a: pl.BlockSpec(a.shape, lambda c: (0, 0))
    return pl.pallas_call(
        wkv_forward_kernel,
        grid=(chunks,),
        in_specs=[block] * 4
        + [
            pl.BlockSpec((CHUNK, low.shape[1]), lambda c: (c, 0)),
            whole(up),
            whole(par),
            whole(first),
        ],
        out_specs=[block, block, block],
        out_shape=[
            jax.ShapeDtypeStruct((rows, columns), jnp.bfloat16),
            jax.ShapeDtypeStruct((rows, columns), jnp.float32),
            jax.ShapeDtypeStruct((rows, columns), jnp.float32),
        ],
        scratch_shapes=[pltpu.VMEM((columns // PACK, PACK, PACK), jnp.float32)],
        compiler_params=pltpu.CompilerParams(
            dimension_semantics=("arbitrary",), vmem_limit_bytes=32 * 2**20
        ),
        cost_estimate=SOON,
        name="wkv_forward",
    )(*[pltpu.with_memory_space_constraint(x, pltpu.HBM) for x in (r, k, v, gate)], low, up, par, first)


def backward_heads(
    r_ref, k_ref, v_ref, gate_ref, low_ref, up_ref, par_ref, wkv_ref, held_ref, gm_ref,
    gr_ref, gk_ref, gv_ref, gg_ref, gw_ref, sums_ref, first_ref, state,
):
    ones = head_ones()

    @pl.when(pl.program_id(0) == 0)
    def _():
        state[...] = jnp.zeros_like(state)
        sums_ref[...] = jnp.zeros_like(sums_ref)

    r, k, v, gate = r_ref[...], k_ref[...], v_ref[...], gate_ref[...]
    bonus, gain = par_ref[1:2], par_ref[2:3]

    def add_to(row, values):
        sums_ref[row : row + 1] = sums_ref[row : row + 1] + jnp.sum(values, axis=0, keepdims=True)

    unit, rstd = unit_heads(wkv_ref[...], ones)
    sig = jax.nn.sigmoid(gate)
    g_mixed = gm_ref[...].astype(jnp.float32)
    g_grouped = g_mixed * gate * sig
    grouped = unit * gain + par_ref[3:4]
    gg_ref[...] = (g_mixed * grouped * sig * (1.0 + gate * (1.0 - sig))).astype(jnp.bfloat16)
    add_to(2, g_grouped * unit)
    add_to(3, g_grouped)
    g_unit = g_grouped * gain
    scale = 1.0 / GROUP_DIMENSION
    g_out = rstd * (
        g_unit - head_sum(g_unit, ones) * scale - unit * (head_sum(g_unit * unit, ones) * scale)
    )

    log_decay, run, before = decay_of(low_ref, up_ref, par_ref)
    last = row_of(run, CHUNK - 1)
    start = spread(held_ref[...], ones)
    end_grad = state[...]
    v_wide = spread(v, ones)
    g_score = mxu(g_out, v_wide, NT)
    score = jnp.zeros((CHUNK, PACK), jnp.float32)
    from_start = jnp.exp(before)
    g_r = from_start * mxu(g_out, start, NN)
    to_end = jnp.exp(last - run)
    g_end = to_end * mxu(v, end_grad, NN)
    g_k = g_end
    for to_row, to_prior, pairs in piece_factors(run, before):
        r_level = (r * to_row).astype(jnp.bfloat16)
        k_level = spread(k * to_prior, ones).astype(jnp.bfloat16)
        score = jnp.where(pairs, mxu(r_level, k_level, NT), score)
        g_level = jnp.where(pairs, g_score, 0.0).astype(jnp.bfloat16)
        g_r = g_r + to_row * mxu(g_level, k_level, NN)
        g_k = g_k + to_prior * fold(mxu(g_level, r_level, TN), ones)
    g_v = fold(mxu(score, g_out, TN), ones) + mxu(k * to_end, end_grad, NT)
    g_before = r * g_r
    g_run = g_before - k * g_k
    g_last = jnp.sum(k * g_end, axis=0, keepdims=True) + jnp.exp(last) * jnp.sum(
        start * end_grad, axis=0, keepdims=True
    )
    upper = jnp.where(iota2((CHUNK, CHUNK), 0) <= iota2((CHUNK, CHUNK), 1), 1.0, 0.0).astype(jnp.float32)
    g_decay = run_sum(upper, g_run) - g_before + g_last
    g_expo = g_decay * log_decay
    gw_ref[...] = g_expo.astype(jnp.bfloat16)
    add_to(0, g_expo)
    g_diag = head_sum(g_out * v, ones)
    add_to(1, r * k * g_diag)
    gr_ref[...] = (g_r + bonus * k * g_diag).astype(jnp.bfloat16)
    gk_ref[...] = (g_k + bonus * r * g_diag).astype(jnp.bfloat16)
    gv_ref[...] = (g_v + head_sum(r * bonus * k, ones) * g_out).astype(jnp.bfloat16)
    state[...] = jnp.exp(last) * end_grad + mxu(g_out, r * from_start, TN) * ones

    @pl.when(pl.program_id(0) == pl.num_programs(0) - 1)
    def _():
        first_ref[...] = fold(state[...], ones)


def wkv_backward(r, k, v, gate, low, up, par, wkv, held, g_mixed):
    rows, columns = r.shape
    chunks = rows // CHUNK
    block = pl.BlockSpec((CHUNK, columns), lambda c: (chunks - 1 - c, 0))
    whole = lambda a: pl.BlockSpec(a.shape, lambda c: (0, 0))
    of_all = lambda n: pl.BlockSpec((n, columns), lambda c: (0, 0))
    low_type = jax.ShapeDtypeStruct((rows, columns), jnp.bfloat16)
    return pl.pallas_call(
        wkv_backward_kernel,
        grid=(chunks,),
        in_specs=[block] * 4
        + [
            pl.BlockSpec((CHUNK, low.shape[1]), lambda c: (chunks - 1 - c, 0)),
            whole(up),
            whole(par),
            block,
            block,
            block,
        ],
        out_specs=[block] * 5 + [of_all(8), of_all(GROUP_DIMENSION)],
        out_shape=[low_type] * 5
        + [
            jax.ShapeDtypeStruct((8, columns), jnp.float32),
            jax.ShapeDtypeStruct((GROUP_DIMENSION, columns), jnp.float32),
        ],
        scratch_shapes=[pltpu.VMEM((columns // PACK, PACK, PACK), jnp.float32)],
        compiler_params=pltpu.CompilerParams(
            dimension_semantics=("arbitrary",), vmem_limit_bytes=32 * 2**20
        ),
        cost_estimate=SOON,
        name="wkv_backward",
    )(r, k, v, gate, low, up, par, wkv, held, g_mixed)


GRAD_ROWS, GRAD_COLUMNS = 512, 256


def grad_kernel(left_ref, right_ref, *rest):
    out_ref = rest[-1]
    turned = left_ref[...].T
    for at in range(0, out_ref.shape[1], GRAD_COLUMNS):
        columns = slice(at, at + GRAD_COLUMNS)
        out_ref[:, columns] = mxu(turned, right_ref[:, columns], NN).astype(jnp.bfloat16)


def grad_into(left, right, total, at, into=None):
    rows, width = left.shape
    columns = right.shape[1]
    shift = at // columns
    specs = [
        pl.BlockSpec((rows, GRAD_ROWS), lambda i: (0, i)),
        pl.BlockSpec((rows, columns), lambda i: (0, 0)),
    ]
    operands = [left, right]
    alias = {}
    if into is not None:
        specs.append(pl.BlockSpec(memory_space=pltpu.HBM))
        operands.append(into)
        alias = {2: 0}
    return pl.pallas_call(
        grad_kernel,
        grid=(width // GRAD_ROWS,),
        in_specs=specs,
        out_specs=pl.BlockSpec((GRAD_ROWS, columns), lambda i: (i, shift)),
        out_shape=pltpu.HBM((width, total), jnp.bfloat16),
        input_output_aliases=alias,
        compiler_params=pltpu.CompilerParams(
            dimension_semantics=("arbitrary",), vmem_limit_bytes=32 * 2**20
        ),
        cost_estimate=SOON,
        name="weight_grad",
    )(*operands)


def grads_kernel(*refs):
    count = len(refs) // 2
    out_ref = refs[-1]
    for n in range(count):

        @pl.when(pl.program_id(0) == n)
        def _(left_ref=refs[n], right_ref=refs[count + n]):
            turned = left_ref[...].T
            for at in range(0, out_ref.shape[1], GRAD_COLUMNS):
                columns = slice(at, at + GRAD_COLUMNS)
                out_ref[:, columns] = mxu(turned, right_ref[:, columns], NN).astype(jnp.bfloat16)


def grads_side_by_side(lefts, rights, total):
    rows, width = lefts[0].shape
    columns = rights[0].shape[1]
    blocks = width // GRAD_ROWS

    def left_spec(n):
        return pl.BlockSpec(
            (rows, GRAD_ROWS),
            lambda p, i: (0, jnp.where(p == n, i, jnp.where(p < n, 0, blocks - 1))),
        )

    return pl.pallas_call(
        grads_kernel,
        grid=(len(lefts), blocks),
        in_specs=[left_spec(n) for n in range(len(lefts))]
        + [pl.BlockSpec((rows, columns), lambda p, i: (0, 0))] * len(rights),
        out_specs=pl.BlockSpec((GRAD_ROWS, columns), lambda p, i: (i, p)),
        out_shape=pltpu.HBM((width, total), jnp.bfloat16),
        compiler_params=pltpu.CompilerParams(
            dimension_semantics=("arbitrary", "arbitrary"), vmem_limit_bytes=32 * 2**20
        ),
        cost_estimate=SOON,
        name="time_mix_grads",
    )(*lefts, *rights)


LOW = 256
SHIFT_LANES = 5 * SHIFT_RANK
LANES = SHIFT_LANES + 64

TILE = 512


def vectors_kernel(up_ref, out_ref):
    turned = up_ref[...].astype(jnp.float32).T
    out_ref[...] = turned[LANES : LANES + 16]


def turn_vectors(first, up_at):
    width = first.shape[0]
    return pl.pallas_call(
        vectors_kernel,
        grid=(width // TILE,),
        in_specs=[pl.BlockSpec((TILE, LOW), lambda n: (n, up_at // LOW))],
        out_specs=pl.BlockSpec((16, TILE), lambda n: (0, n)),
        out_shape=jax.ShapeDtypeStruct((16, width), jnp.float32),
        compiler_params=pltpu.CompilerParams(dimension_semantics=("arbitrary",)),
        cost_estimate=SOON,
        name="turn_vectors",
    )(first)


def lane_group(shape):
    return lax.shift_right_logical(iota2(shape, 1), 5)


def mixes_forward_kernel(
    unit_ref, w_ref, down_ref, up_ref, vec_ref,
    m0_ref, m1_ref, m2_ref, m3_ref, m4_ref, normed_ref, squash_ref, r_ref, k_ref, v_ref, g_ref,
    hidden, grouped,
):
    phase, tile = pl.program_id(0), pl.program_id(1)
    rows = unit_ref.shape[0]
    own = r_ref.shape[1]
    vec = vec_ref[...]
    normed = unit_ref[...] * vec[0:1] + vec[1:2]
    row = iota2(normed.shape, 0)
    shifted = jnp.where(row == 0, 0.0, pltpu.roll(normed, 1, 0)) - normed
    down = down_ref[...]
    of_shift = iota2(down.shape, 1) < SHIFT_LANES

    @pl.when((phase == 0) & (tile == 0))
    def _():
        hidden[...] = jnp.zeros_like(hidden)

    @pl.when(phase == 0)
    def _():
        hidden[...] = hidden[...] + mxu(normed + shifted * vec[2:3], jnp.where(of_shift, down, 0), NN)

    @pl.when((phase == 1) & (tile == 0))
    def _():
        squash = jnp.tanh(hidden[...])
        squash_ref[...] = squash
        group = lane_group(squash.shape)
        for g in range(5):
            grouped[g] = jnp.where(group == g, squash, 0.0).astype(jnp.bfloat16)
        hidden[...] = jnp.zeros_like(hidden)
        for ref in (r_ref, k_ref, v_ref, g_ref):
            ref[...] = jnp.zeros_like(ref)

    @pl.when(phase == 1)
    def _():
        normed_ref[...] = normed
        up = up_ref[...]
        for g, mix_ref in enumerate((m0_ref, m1_ref, m2_ref, m3_ref, m4_ref)):
            mix = (normed + shifted * (vec[3 + g : 4 + g] + mxu(grouped[g], up, NT))).astype(jnp.bfloat16)
            mix_ref[...] = mix
            if g == 0:
                hidden[...] = hidden[...] + mxu(mix, jnp.where(of_shift, 0, down), NN)
            else:
                column = (None, 1, 2, 0, 3)[g] * own
                out = (None, k_ref, v_ref, r_ref, g_ref)[g]
                out[...] = out[...] + mxu(mix, w_ref[:, column : column + own], NN)

    @pl.when((phase == 1) & (tile == pl.num_programs(1) - 1))
    def _():
        squash_ref[...] = squash_ref[...] + jnp.tanh(hidden[...])


def mixes_forward(unit, first, low_at, vec, own):
    rows, width = unit.shape
    tiles = width // TILE
    block = low_at // LOW
    across = lambda r: pl.BlockSpec((r, TILE), lambda p, n: (0, n))
    late = pl.BlockSpec((rows, TILE), lambda p, n: (0, n * p))
    whole = lambda columns: pl.BlockSpec((rows, columns), lambda p, n: (0, 0))
    kept = lambda columns, dtype: jax.ShapeDtypeStruct((rows, columns), dtype)
    return pl.pallas_call(
        mixes_forward_kernel,
        grid=(2, tiles),
        in_specs=[
            across(rows),
            pl.BlockSpec((TILE, 4 * own), lambda p, n: (n * p, 0)),
            pl.BlockSpec((TILE, LOW), lambda p, n: (n, block)),
            pl.BlockSpec((TILE, LOW), lambda p, n: (n, block + 1)),
            across(vec.shape[0]),
        ],
        out_specs=[late] * 6 + [whole(LOW)] + [whole(own)] * 4,
        out_shape=[kept(width, jnp.bfloat16)] * 5
        + [kept(width, jnp.float32), kept(LOW, jnp.float32)]
        + [pltpu.HBM((rows, own), jnp.float32)] * 4,
        scratch_shapes=[pltpu.VMEM((rows, LOW), jnp.float32), pltpu.VMEM((5, rows, LOW), jnp.bfloat16)],
        compiler_params=pltpu.CompilerParams(
            dimension_semantics=("arbitrary", "arbitrary"), vmem_limit_bytes=54 * 2**20
        ),
        cost_estimate=SOON,
        name="mixes_forward",
    )(unit, first, first, first, vec)


def mixes_back_kernel(
    gk_ref, gv_ref, gr_ref, gg_ref, gd_ref, w_ref, down_ref, up_ref, vec_ref, squash_ref, normed_ref,
    mix_ref, sums_ref, out_ref, small_ref,
    g_shift, g_norm, g_squash, g_hidden, g_up, g_sums, grouped, turned,
):
    phase, tile = pl.program_id(0), pl.program_id(1)
    rows = squash_ref.shape[0]
    own = gk_ref.shape[1]
    normed = normed_ref[...]
    row = iota2(normed.shape, 0)
    shifted = jnp.where(row == 0, 0.0, pltpu.roll(normed, 1, 0)) - normed
    squash = squash_ref[...]
    vec = vec_ref[...]

    @pl.when((phase == 0) & (tile == 0))
    def _():
        g_squash[...] = jnp.zeros_like(g_squash)
        group = lane_group(squash.shape)
        for g in range(5):
            grouped[g] = jnp.where(group == g, squash, 0.0).astype(jnp.bfloat16)
        turned[...] = squash.astype(jnp.bfloat16).T

    @pl.when(phase == 0)
    def _():
        up = up_ref[...]
        group_wide = lane_group(up.shape)
        total_shift = jnp.zeros((rows, TILE), jnp.float32)
        total_norm = jnp.zeros((rows, TILE), jnp.float32)
        add_squash = jnp.zeros((rows, LOW), jnp.float32)
        sums = []
        for g in range(5):
            if g == 0:
                part = mxu(gd_ref[...], down_ref[...], NT)
            else:
                column = (None, 1, 2, 0, 3)[g] * own
                grad = (None, gk_ref, gv_ref, gr_ref, gg_ref)[g]
                part = mxu(grad[...], w_ref[:, column : column + own], NT)
            coeff = vec[3 + g : 4 + g] + mxu(grouped[g], up, NT)
            times = part * shifted
            times_low = times.astype(jnp.bfloat16)
            sums.append(jnp.sum(times, axis=0, keepdims=True))
            total_shift = total_shift + part * coeff
            total_norm = total_norm + part
            add_squash = add_squash + mxu(times_low, jnp.where(group_wide == g, up, 0), NN)
            lanes = slice(g * SHIFT_RANK, (g + 1) * SHIFT_RANK)
            g_up[tile, lanes] = mxu(turned[lanes], times_low, NN)
        g_shift[tile] = total_shift
        g_norm[tile] = total_norm
        g_squash[...] = g_squash[...] + add_squash
        g_sums[tile] = jnp.concatenate(sums + [jnp.zeros((3, TILE), jnp.float32)], axis=0)

    @pl.when((phase == 1) & (tile == 0))
    def _():
        g_hidden[...] = (g_squash[...] * (1.0 - squash * squash)).astype(jnp.bfloat16)

    @pl.when(phase == 1)
    def _():
        blend = vec[2:3]
        part = mxu(g_hidden[...], down_ref[...], NT)
        total_shift = g_shift[tile] + part * blend
        total = g_norm[tile] + part - total_shift
        total = total + jnp.where(row == rows - 1, 0.0, pltpu.roll(total_shift, rows - 1, 0))
        out_ref[...] = total.astype(jnp.bfloat16)
        unit = (normed - vec[1:2]) / vec[0:1]
        head = [
            jnp.sum(total * unit, axis=0, keepdims=True),
            jnp.sum(total, axis=0, keepdims=True),
            jnp.sum(part * shifted, axis=0, keepdims=True),
        ]
        sums = jnp.concatenate(head + [g_sums[tile][:5], sums_ref[...]], axis=0)
        shape = (sums.shape[0], LOW)
        behind = jnp.where(iota2(shape, 1) == LANES + iota2(shape, 0), 1.0, 0.0)
        small_ref[:, :LOW] = (
            mxu(normed + shifted * blend, g_hidden[...], TN) + mxu(mix_ref[...], gd_ref[...], TN)
        ).astype(jnp.bfloat16)
        small_ref[:, LOW:] = mxu(sums, behind, TN).astype(jnp.bfloat16)
        small_ref[:, LOW : LOW + SHIFT_LANES] = g_up[tile].T.astype(jnp.bfloat16)


def mixes_back(g_key, g_val, g_recept, g_gate, g_decay, first, low_at, vec, squash, normed, mix, sums):
    rows, width = normed.shape
    own = g_key.shape[1]
    tiles = width // TILE
    block = low_at // LOW
    whole = lambda a: pl.BlockSpec(a.shape, lambda p, n: (0, 0))
    across = lambda r: pl.BlockSpec((r, TILE), lambda p, n: (0, n))
    late = lambda r: pl.BlockSpec((r, TILE), lambda p, n: (0, n * p))
    early = lambda p, n: n * (1 - p) + (tiles - 1) * p
    return pl.pallas_call(
        mixes_back_kernel,
        grid=(2, tiles),
        in_specs=[whole(g_key)] * 4
        + [
            whole(g_decay),
            pl.BlockSpec((TILE, 4 * own), lambda p, n: (early(p, n), 0)),
            pl.BlockSpec((TILE, LOW), lambda p, n: (n, block)),
            pl.BlockSpec((TILE, LOW), lambda p, n: (early(p, n), block + 1)),
            across(vec.shape[0]),
            whole(squash),
            across(rows),
            late(rows),
            late(sums.shape[0]),
        ],
        out_specs=[late(rows), pl.BlockSpec((TILE, 2 * LOW), lambda p, n: (n * p, 0))],
        out_shape=[
            jax.ShapeDtypeStruct((rows, width), jnp.bfloat16),
            jax.ShapeDtypeStruct((width, 2 * LOW), jnp.bfloat16),
        ],
        scratch_shapes=[
            pltpu.VMEM((tiles, rows, TILE), jnp.float32),
            pltpu.VMEM((tiles, rows, TILE), jnp.float32),
            pltpu.VMEM((rows, LOW), jnp.float32),
            pltpu.VMEM((rows, LOW), jnp.bfloat16),
            pltpu.VMEM((tiles, SHIFT_LANES, TILE), jnp.float32),
            pltpu.VMEM((tiles, 8, TILE), jnp.float32),
            pltpu.VMEM((5, rows, LOW), jnp.bfloat16),
            pltpu.VMEM((LOW, rows), jnp.bfloat16),
        ],
        compiler_params=pltpu.CompilerParams(
            dimension_semantics=("arbitrary", "arbitrary"), vmem_limit_bytes=56 * 2**20
        ),
        cost_estimate=SOON,
        name="mixes_back",
    )(g_key, g_val, g_recept, g_gate, g_decay, first, first, first, vec, squash, normed, mix, sums)


def shards(
    inputs,
    cotangent,
    states,
    vectors,
    time_mix_weight,
    output_weight,
    channel_receptance_weight,
    rank_down_weight,
    rank_up_weight,
    channel_key_weight,
    channel_value_weight,
):
    token_rows, width = inputs.shape
    seg_count = lax.axis_size("seg")
    own_width = time_mix_weight.shape[2]
    hidden = channel_key_weight.shape[1]
    local_heads = own_width // GROUP_DIMENSION
    col_start = lax.axis_index("span") * own_width
    position = lax.axis_index("span") * token_rows

    x_seg = span_gather(inputs).astype(jnp.float32)
    grad_columns = split_columns(cotangent).astype(jnp.float32)
    def blank(count):
        return jnp.zeros((token_rows // 8, count), jnp.bfloat16)

    small_rows = jnp.concatenate(
        [rank_down_weight, blank(LOW - LANES), rank_up_weight.T, vectors.T, blank(LOW - LANES - 16)], axis=1
    )
    span_rows = gather_and_split(small_rows, channel_receptance_weight)
    weights = both_planes(lambda proj: [proj[g] for g in range(4)], time_mix_weight)
    small_pair = both_planes(lambda rows: [rows], span_rows[:, own_width:])
    late_pairs = [fill_pair(rows[None])[0] for rows in (output_weight.T, span_rows[:, :own_width])]
    first = plane_gather(jnp.concatenate([weights, small_pair] + late_pairs, axis=1))
    _, unit_seg, _ = norm_rows(x_seg, 1.0, 0.0)
    second_pair = both_planes(lambda key, value: [key, value.T], channel_key_weight, channel_value_weight)
    second_pair, unit_seg, grad_columns = lax.optimization_barrier((second_pair, unit_seg, grad_columns))
    second = plane_gather(second_pair)
    low_at = 4 * own_width
    late_at = low_at + 2 * LOW

    def late_rows(at):
        pairs = first[:, at : at + own_width // 2].reshape(-1, 2 * (width // seg_count), own_width // 2)
        return from_pair(pairs)

    out_half, recept_half = late_rows(late_at), late_rows(late_at + own_width // 2)
    late_got = swap_high(jnp.concatenate([out_half, recept_half], axis=2))
    out_got, recept_got = late_got[:, :, :own_width], late_got[:, :, own_width:]
    up_at = low_at + LOW
    vec = first[:, up_at + LANES : up_at + LANES + 16].T.astype(jnp.float32)

    def own_cols(line):
        return lax.dynamic_slice_in_dim(line, col_start, own_width, line.ndim - 1)

    def own_rows(values):
        return lax.dynamic_slice_in_dim(values, position, token_rows, 0)

    x_in = inputs.astype(jnp.float32)
    *mixes, normed, squash, recept, key_proj, val_proj, gate_pre = mixes_forward(
        unit_seg, first, low_at, vec, own_width
    )
    lane = lax.broadcasted_iota(jnp.int32, squash.shape, 1)
    of_decay = (lane >= SHIFT_LANES) & (lane < LANES)
    decay_low = jnp.where(of_decay, squash, 0.0).astype(jnp.bfloat16)
    up_own = lax.dynamic_slice(first, (col_start, up_at), (own_width, LOW))
    head_vec = jnp.concatenate([own_cols(vec[8:12]), jnp.zeros((4, own_width), jnp.float32)], axis=0)
    first_state = jnp.transpose(states[0], (2, 0, 1)).reshape(GROUP_DIMENSION, own_width)
    out_w = other_plane(out_half, out_got)
    heads_in = (recept, key_proj, val_proj, gate_pre, decay_low, up_own, head_vec)
    mixed, wkv, held = wkv_forward(*heads_in, first_state)
    recept_w = other_plane(recept_half, recept_got)
    resid = x_in + span_reduce(backward_product(mixed, out_w).astype(jnp.bfloat16))

    normed_two, unit_two, rstd_two = norm_rows(resid, vec[12], vec[13])
    n2 = span_gather(normed_two.astype(jnp.bfloat16)).astype(jnp.float32)
    shifted_two = prior_rows(n2) - n2
    key_in = (n2 + shifted_two * vec[14]).astype(jnp.bfloat16)
    rec_in = (n2 + shifted_two * vec[15]).astype(jnp.bfloat16)
    rec_gate = jax.nn.sigmoid(product_lower(rec_in, recept_w))
    g_value = (grad_columns * rec_gate).astype(jnp.bfloat16)
    g_value, second = lax.optimization_barrier((g_value, second))
    g_value_all = span_gather(g_value, 1)
    key_w, value_w = second[:, :hidden], second[:, hidden:]
    hidden_two = product_lower(key_in, key_w)
    active = jax.nn.relu(hidden_two)
    squared = (active * active).astype(jnp.bfloat16)
    active = active.astype(jnp.bfloat16)

    low = lax.axis_index("span") // 2

    def value_columns(which):
        weights = lax.dynamic_slice(second, (which * (width // 2), hidden), (width // 2, hidden))
        return core_reduce(backward_product(squared, weights).astype(jnp.bfloat16))

    far, near = value_columns(1 - low), value_columns(low)
    far, g_value_all = lax.optimization_barrier((far.astype(jnp.bfloat16), g_value_all))
    far = swap_low(far)
    cm_total = 2 * hidden
    g_hid = (product_lower(g_value_all, value_w) * 2.0 * active.astype(jnp.float32)).astype(jnp.bfloat16)
    g_value_all, g_hid = lax.optimization_barrier((g_value_all, g_hid))
    cm_part = grad_into(g_value_all, squared, cm_total, hidden)
    far, near, cm_part = lax.optimization_barrier((far, near, cm_part))
    cm_part = grad_into(key_in, g_hid, cm_total, 0, cm_part)
    cm_part, g_hid = lax.optimization_barrier((cm_part, g_hid))
    cm_pair = plane_scatter(cm_part)
    value_out = near + far.astype(jnp.float32)
    gated = (rec_gate * value_out).astype(jnp.bfloat16)
    g_rec = (grad_columns * value_out * rec_gate * (1.0 - rec_gate)).astype(jnp.bfloat16)
    g_key_in = backward_product(g_hid, key_w)
    g_rec_in = backward_product(g_rec, recept_w)
    vec_fourteen = jnp.sum(g_key_in * shifted_two, axis=0)
    vec_fifteen = jnp.sum(g_rec_in * shifted_two, axis=0)
    g_shift_two = g_key_in * vec[14] + g_rec_in * vec[15]
    g_n2_part = g_key_in + g_rec_in - g_shift_two + next_rows(g_shift_two)
    g_n2 = span_reduce(g_n2_part.astype(jnp.bfloat16))
    rec_part = grad_into(rec_in, g_rec, own_width, 0)
    g_n2, rec_part = lax.optimization_barrier((g_n2, rec_part))
    vec_twelve = jnp.sum(g_n2 * unit_two, axis=0)
    vec_thirteen = jnp.sum(g_n2, axis=0)
    g_resid = cotangent.astype(jnp.float32) + norm_back(g_n2, unit_two, rstd_two, vec[12])

    g_att = span_gather(g_resid.astype(jnp.bfloat16))
    rec_part = rec_part.reshape(seg_count // 2, 2, width // seg_count, own_width)
    rec_mine, rec_send = in_order(rec_part[:, 0], rec_part[:, 1], lax.axis_index("seg") % 2 == 1)
    g_att, gated, rec_send = lax.optimization_barrier((g_att, gated, rec_send))
    rec_got = swap_high(rec_send)
    gated_rows = join_columns(gated)
    g_mixed = product_lower(g_att, out_w)
    g_recept, g_key, g_val, g_gate, g_ww, head_sums, g_first = wkv_backward(
        *heads_in, wkv, held, g_mixed
    )
    state_grad = jnp.transpose(
        g_first.reshape(GROUP_DIMENSION, local_heads, GROUP_DIMENSION), (1, 2, 0)
    )[None]
    tm_total = 5 * own_width + own_width // 2
    tm_part = grads_side_by_side(
        (g_att, mixes[3], mixes[1], mixes[2], mixes[4]), (mixed, g_recept, g_key, g_val, g_gate), tm_total
    )
    rec_got, g_ww = lax.optimization_barrier((rec_got, g_ww))
    rec_sum = (rec_mine.astype(jnp.float32) + rec_got.astype(jnp.float32)).astype(jnp.bfloat16)
    tm_part = lax.dynamic_update_slice(
        tm_part, fill_pair(rec_sum).reshape(width, own_width // 2), (0, 5 * own_width)
    )
    tm_part, cm_pair, gated_rows = lax.optimization_barrier((tm_part, cm_pair, gated_rows))
    output = (resid + gated_rows.astype(jnp.float32)).astype(jnp.bfloat16)
    tm_pair = plane_scatter(tm_part)
    g_key, g_ww, cm_pair = lax.optimization_barrier((g_key, g_ww, cm_pair))

    g_decay_hidden = jnp.where(
        of_decay, product_lower(g_ww, up_own) * (1.0 - squash * squash), 0.0
    ).astype(jnp.bfloat16)
    up_decay_grad = outer_sum(g_ww, decay_low)
    other_sums = jnp.concatenate(
        [
            lax.dynamic_update_slice_in_dim(jnp.zeros((4, width), jnp.float32), head_sums[:4], col_start, 1),
            jnp.stack([vec_twelve, vec_thirteen, vec_fourteen, vec_fifteen]),
        ],
        axis=0,
    )
    g_normed, small_part = mixes_back(
        g_key, g_val, g_recept, g_gate, g_decay_hidden, first, low_at, vec, squash, normed, mixes[0], other_sums
    )
    own_part = lax.dynamic_slice(small_part, (col_start, LOW), (own_width, LOW))
    small_part = lax.dynamic_update_slice(
        small_part, (own_part.astype(jnp.float32) + up_decay_grad).astype(jnp.bfloat16), (col_start, LOW)
    )
    small, g_n1, cm_grad = reduce_small(small_part, over_cores(g_normed), cm_pair)
    rec_own = from_pair(tm_pair[None, :, 5 * own_width :])[0]
    tm_grad = finish_scatter(*plane_halves(tm_pair[:, : 5 * own_width]))
    _, unit_own, rstd_own = norm_rows(x_in, vec[0], vec[1])
    x_grad = g_resid + norm_back(g_n1, unit_own, rstd_own, vec[0])
    down_grad = small[:, :LANES]
    up_grad = small[:, LOW : LOW + LANES].T
    vec_grad = small[:, LOW + LANES : LOW + LANES + 16].T
    rec_grad = join_columns(rec_own).astype(jnp.float32)
    value_grad = cm_grad[:, hidden:].T
    key_grad = cm_grad[:, :hidden]
    out_grad = tm_grad[:, :own_width].T
    proj_grad = jnp.moveaxis(tm_grad[:, own_width : 5 * own_width].reshape(-1, 4, own_width), 1, 0)
    return (
        output,
        x_grad,
        state_grad,
        vec_grad,
        proj_grad,
        out_grad,
        rec_grad,
        down_grad,
        up_grad,
        key_grad,
        value_grad,
    )


def solution(mesh):
    rows, columns = P(ALL, None), P(None, ALL)
    state = P("seg", "span", None, None)
    time_mix = P(None, "seg", "span")
    turned, straight = P("span", "seg"), P("seg", "span")
    return jax.shard_map(
        shards,
        mesh=mesh,
        in_specs=(
            rows, rows, state, columns, time_mix, turned, rows, rows, columns, straight, turned
        ),
        out_specs=(
            rows, rows, state, columns, time_mix, turned, rows, rows, columns, straight, turned
        ),
        check_vma=False,
    )
```

```python
import jax
import jax.numpy as jnp
from jax import lax
from jax.experimental import pallas as pl
from jax.experimental.pallas import tpu as pltpu
from jax.experimental.layout import Layout, with_layout_constraint
from jax.sharding import PartitionSpec as P

GROUP_DIMENSION = 64
SHIFT_RANK = 32
ALL = ("seg", "span")

maximal_accuracy = lax.Precision.HIGHEST
ln_eps = 1e-05
gn_eps = 0.00064


def swap(block, bit):
    count = lax.axis_size("seg") * lax.axis_size("span")
    return lax.ppermute(block, ALL, [(i, i ^ bit) for i in range(count)])


def swap_core(block):
    return swap(block, 1)


def swap_low(block):
    return swap(block, 2)


def swap_high(block):
    return swap(block, 4)


def plane_groups():
    half = lax.axis_size("seg") // 2
    return [[2 * j + h for j in range(half)] for h in range(2)]


def in_order(own, other, second):
    return jnp.where(second, other, own), jnp.where(second, own, other)


def span_gather(block, axis=0):
    place = lax.axis_index("span")
    low, core = place // 2, place % 2
    p0, p1 = in_order(block, swap_low(block), low == 1)
    q = swap_core(jnp.stack([p0, p1]))
    a0, a1 = in_order(p0, q[0], core == 1)
    b0, b1 = in_order(p1, q[1], core == 1)
    return jnp.concatenate([a0, a1, b0, b1], axis=axis)


def core_reduce(part):
    core = lax.axis_index("span") % 2
    half = part.shape[1] // 2
    keep, send = in_order(part[:, :half], part[:, half:], core == 1)
    return keep.astype(jnp.float32) + swap_core(send.astype(jnp.bfloat16)).astype(jnp.float32)


def over_cores(part):
    core = lax.axis_index("span") % 2
    b = part.reshape(2, 2, part.shape[0] // 4, part.shape[1])
    keep, send = in_order(b[:, 0], b[:, 1], core == 1)
    return keep.astype(jnp.float32) + swap_core(send.astype(jnp.bfloat16)).astype(jnp.float32)


def over_low(both):
    low = lax.axis_index("span") // 2
    mine, send = in_order(both[0], both[1], low == 1)
    return mine + swap_low(send.astype(jnp.bfloat16)).astype(jnp.float32)


def span_reduce(part):
    return over_low(over_cores(part))


def fill_pair(rows):
    half = rows.shape[2] // 2
    return jnp.concatenate([rows[:, :, :half], rows[:, :, half:]], axis=1)


def from_pair(pairs):
    half = pairs.shape[1] // 2
    return jnp.concatenate([pairs[:, :half], pairs[:, half:]], axis=2)


def other_plane(rows, got):
    high = lax.axis_index("seg") % 2
    return jnp.stack(in_order(rows, got, high == 1), axis=1).reshape(-1, rows.shape[2])


def both_planes(laid, *blocks):
    high = lax.axis_index("seg") % 2
    own, other = (
        jnp.concatenate(laid(*got), axis=1) for got in (blocks, [swap_high(block) for block in blocks])
    )
    return jnp.concatenate(in_order(own, other, high == 1), axis=0)


def plane_gather(pair):
    whole = lax.all_gather(
        pair,
        "seg",
        axis=0,
        tiled=True,
        axis_index_groups=plane_groups(),
    )
    return with_layout_constraint(whole, Layout(major_to_minor=(0, 1)))


def plane_scatter(part):
    return lax.psum_scatter(
        part, "seg", scatter_dimension=0, tiled=True, axis_index_groups=plane_groups()
    )


def plane_halves(pair):
    high = lax.axis_index("seg") % 2
    rows = pair.shape[0] // 2
    return in_order(pair[:rows], pair[rows:], high == 1)


def finish_scatter(mine, send):
    return mine.astype(jnp.float32) + swap_high(send).astype(jnp.float32)


def gather_and_split(small, wide):
    place = lax.axis_index("span")
    n = wide.shape[1] // 4
    messages = [
        jnp.concatenate([lax.dynamic_slice_in_dim(wide, (place ^ bit) * n, n, 1), small], axis=1)
        for bit in range(4)
    ]
    pieces = [m if bit == 0 else swap(m, bit) for bit, m in enumerate(messages)]
    result = jnp.zeros((4, *messages[0].shape), small.dtype)
    for bit, piece in enumerate(pieces):
        result = lax.dynamic_update_index_in_dim(result, piece, place ^ bit, 0)
    return result.reshape(4 * small.shape[0], -1)


def split_columns(block):
    place = lax.axis_index("span")
    n = block.shape[1] // 4

    def columns(at):
        return lax.dynamic_slice_in_dim(block, at * n, n, 1)

    pieces = [columns(place)] + [swap(columns(place ^ bit), bit) for bit in (1, 2, 3)]
    result = jnp.zeros((4, block.shape[0], n), block.dtype)
    for bit, piece in enumerate(pieces):
        result = lax.dynamic_update_index_in_dim(result, piece, place ^ bit, 0)
    return result.reshape(4 * block.shape[0], n)


def join_columns(block):
    place = lax.axis_index("span")
    r, n = block.shape[0] // 4, block.shape[1]

    def rows(at):
        return lax.dynamic_slice_in_dim(block, at * r, r, 0)

    result = jnp.zeros((r, 4 * n), block.dtype)
    for bit in range(4):
        piece = rows(place ^ bit)
        if bit:
            piece = swap(piece, bit)
        result = lax.dynamic_update_slice_in_dim(result, piece, (place ^ bit) * n, 1)
    return result


def product_lower(left_arg, right_arg):
    return jnp.dot(left_arg, right_arg, preferred_element_type=jnp.float32)


def outer_sum(left_arg, right_arg):
    return jnp.einsum("td,te->de", left_arg, right_arg, preferred_element_type=jnp.float32)


def backward_product(gradient, weights):
    return jnp.einsum("te,de->td", gradient, weights, preferred_element_type=jnp.float32)


def norm_rows(values, gain_vec, offset):
    centre = values - jnp.mean(values, -1, keepdims=True)
    row_rstd = lax.rsqrt(jnp.mean(centre * centre, -1, keepdims=True) + ln_eps)
    unit_rows = centre * row_rstd
    return (unit_rows * gain_vec + offset, unit_rows, row_rstd)


def norm_back(gradient, unit_rows, row_rstd, gain_vec):
    scaled = gradient * gain_vec
    return row_rstd * (
        scaled
        - jnp.mean(scaled, -1, keepdims=True)
        - unit_rows * jnp.mean(scaled * unit_rows, -1, keepdims=True)
    )


def prior_rows(values):
    return jnp.concatenate([jnp.zeros_like(values[:1]), values[:-1]], axis=0)


def next_rows(values):
    return jnp.concatenate([values[1:], jnp.zeros_like(values[:1])], axis=0)


def reduce_small(part, both, pair):
    place, high = lax.axis_index("span"), lax.axis_index("seg") % 2
    planes = lax.axis_size("seg") // 2
    width = part.shape[1]
    b = part.reshape(planes, 2, 2, 2, -1, width)

    def summed(b, dim, bit, move):
        at0, at1 = (lax.index_in_dim(b, k, dim, keepdims=False) for k in (0, 1))
        mine, send = in_order(at0, at1, bit == 1)
        return mine.astype(jnp.float32) + move(send.astype(jnp.bfloat16)).astype(jnp.float32)

    b = summed(summed(b, 3, place % 2, swap_core), 2, place // 2, swap_low)
    b, both = lax.optimization_barrier((b, both))
    rows = over_low(both)
    b = summed(b, 1, high, swap_high).astype(jnp.bfloat16)
    b, pair = lax.optimization_barrier((b, pair))
    finished = finish_scatter(*plane_halves(pair))
    arrived = lax.all_to_all(
        b, "seg", split_axis=0, concat_axis=0, tiled=True, axis_index_groups=plane_groups()
    )
    return arrived.astype(jnp.float32).sum(axis=0), rows, finished


SOON = pl.CostEstimate(flops=2**20, bytes_accessed=2**16, transcendentals=0)

CHUNK = 64
PACK = 256


def mxu(a, b, contract):
    return lax.dot_general(
        a.astype(jnp.bfloat16),
        b.astype(jnp.bfloat16),
        (contract, ((), ())),
        preferred_element_type=jnp.float32,
    )


NN, NT, TN = ((1,), (0,)), ((1,), (1,)), ((0,), (0,))


def halves(values):
    high = values.astype(jnp.bfloat16)
    return high, (values - high.astype(jnp.float32)).astype(jnp.bfloat16)


def iota2(shape, dim):
    return lax.broadcasted_iota(jnp.int32, shape, dim)


def head_ones():
    shape = (PACK, PACK)
    same = (iota2(shape, 0) ^ iota2(shape, 1)) < GROUP_DIMENSION
    return jnp.where(same, 1.0, 0.0).astype(jnp.float32)


def spread(block, ones):
    return jnp.concatenate([block] * (PACK // CHUNK), axis=0) * ones


def fold(big, ones):
    kept = big * ones
    total = kept[:CHUNK]
    for h in range(1, PACK // CHUNK):
        total = total + kept[h * CHUNK : (h + 1) * CHUNK]
    return total


def head_sum(values, ones):
    high, rest = halves(values)
    return mxu(high, ones, NN) + mxu(rest, ones, NN)


def run_sum(which, values):
    high, rest = halves(values)
    return mxu(which, high, NN) + mxu(which, rest, NN)


def row_of(values, row):
    return values[row : row + 1]


def piece_factors(run, before):
    rows = iota2((CHUNK, PACK), 0)
    apart = rows ^ (iota2((CHUNK, PACK), 1) & (CHUNK - 1))
    levels = []
    for half in (32, 16, 8, 4, 2, 1):
        upper = (rows & half) != 0
        if half == 1:
            scale = jnp.ones_like(run)
        else:
            if half == 2:
                reference = run
                for row, shift in ((0, CHUNK - 1), (2, 1), (3, 2)):
                    reference = jnp.where((rows & 3) == row, pltpu.roll(run, shift, 0), reference)
            else:
                reference = jnp.broadcast_to(row_of(run, half - 1), run.shape)
                for start in range(2 * half, CHUNK, 2 * half):
                    here = jnp.broadcast_to(row_of(run, start + half - 1), run.shape)
                    reference = jnp.where(rows >= start, here, reference)
            scale = jnp.exp(jnp.minimum(jnp.where(upper, before - reference, reference - run), 0.0))
        pairs = (apart < 2 * half) & upper & ((apart & half) != 0)
        levels.append((jnp.where(upper, scale, 0.0), jnp.where(upper, 0.0, scale), pairs))
    return levels


NOTHING = -104.0


def lower_ones():
    return jnp.where(iota2((CHUNK, CHUNK), 0) >= iota2((CHUNK, CHUNK), 1), 1.0, 0.0).astype(jnp.float32)


def decay_of(low_ref, up_ref, par_ref):
    log_decay = -jnp.exp(par_ref[0:1] + mxu(low_ref[...], up_ref[...], NT))
    kept = jnp.maximum(log_decay, NOTHING)
    run = run_sum(lower_ones(), kept)
    return jnp.where(log_decay <= NOTHING, 0.0, log_decay), run, run - kept


def unit_heads(wkv, ones):
    centre = wkv - head_sum(wkv, ones) * (1.0 / GROUP_DIMENSION)
    rstd = lax.rsqrt(head_sum(centre * centre, ones) * (1.0 / GROUP_DIMENSION) + gn_eps)
    return centre * rstd, rstd


def lane_groups(refs, kinds):
    width = refs[0].shape[1]
    for g in range(width // PACK):
        lanes = pl.ds(g * PACK, PACK)
        part = {"c": lambda ref: ref.at[:, lanes], "r": lambda ref: ref.at[lanes], "s": lambda ref: ref.at[g]}
        yield [ref if kind == "w" else part[kind](ref) for ref, kind in zip(refs, kinds)]


def wkv_forward_kernel(*refs):
    for group in lane_groups(refs, "ccccwrcccccs"):
        forward_heads(*group)


def wkv_backward_kernel(*refs):
    for group in lane_groups(refs, "ccccwrccccccccccc" + "s"):
        backward_heads(*group)


def forward_heads(
    r_ref, k_ref, v_ref, gate_ref, low_ref, up_ref, par_ref, first_ref, mixed_ref, wkv_ref, held_ref, state
):
    ones = head_ones()

    @pl.when(pl.program_id(0) == 0)
    def _():
        state[...] = spread(first_ref[...], ones)

    r, k, v = r_ref[...], k_ref[...], v_ref[...]
    _, run, before = decay_of(low_ref, up_ref, par_ref)
    held_ref[...] = fold(state[...], ones)
    score = jnp.zeros((CHUNK, PACK), jnp.float32)
    for to_row, to_prior, pairs in piece_factors(run, before):
        score = jnp.where(pairs, mxu(r * to_row, spread(k * to_prior, ones), NT), score)
    out = mxu(score, spread(v, ones), NN) + mxu(r * jnp.exp(before), state[...], NT)
    out = out + head_sum(r * par_ref[1:2] * k, ones) * v
    wkv_ref[...] = out
    last = row_of(run, CHUNK - 1)
    state[...] = jnp.exp(last) * state[...] + mxu(v, k * jnp.exp(last - run), TN) * ones
    unit, _ = unit_heads(out, ones)
    gate = gate_ref[...]
    mixed_ref[...] = ((unit * par_ref[2:3] + par_ref[3:4]) * gate * jax.nn.sigmoid(gate)).astype(jnp.bfloat16)


def wkv_forward(r, k, v, gate, low, up, par, first):
    rows, columns = r.shape
    chunks = rows // CHUNK
    block = pl.BlockSpec((CHUNK, columns), lambda c: (c, 0))
    whole = lambda a: pl.BlockSpec(a.shape, lambda c: (0, 0))
    return pl.pallas_call(
        wkv_forward_kernel,
        grid=(chunks,),
        in_specs=[block] * 4
        + [
            pl.BlockSpec((CHUNK, low.shape[1]), lambda c: (c, 0)),
            whole(up),
            whole(par),
            whole(first),
        ],
        out_specs=[block, block, block],
        out_shape=[
            jax.ShapeDtypeStruct((rows, columns), jnp.bfloat16),
            jax.ShapeDtypeStruct((rows, columns), jnp.float32),
            jax.ShapeDtypeStruct((rows, columns), jnp.float32),
        ],
        scratch_shapes=[pltpu.VMEM((columns // PACK, PACK, PACK), jnp.float32)],
        compiler_params=pltpu.CompilerParams(
            dimension_semantics=("arbitrary",), vmem_limit_bytes=32 * 2**20
        ),
        cost_estimate=SOON,
        name="wkv_forward",
    )(*[pltpu.with_memory_space_constraint(x, pltpu.HBM) for x in (r, k, v, gate)], low, up, par, first)


def backward_heads(
    r_ref, k_ref, v_ref, gate_ref, low_ref, up_ref, par_ref, wkv_ref, held_ref, gm_ref,
    gr_ref, gk_ref, gv_ref, gg_ref, gw_ref, sums_ref, first_ref, state,
):
    ones = head_ones()

    @pl.when(pl.program_id(0) == 0)
    def _():
        state[...] = jnp.zeros_like(state)
        sums_ref[...] = jnp.zeros_like(sums_ref)

    r, k, v, gate = r_ref[...], k_ref[...], v_ref[...], gate_ref[...]
    bonus, gain = par_ref[1:2], par_ref[2:3]

    def add_to(row, values):
        sums_ref[row : row + 1] = sums_ref[row : row + 1] + jnp.sum(values, axis=0, keepdims=True)

    unit, rstd = unit_heads(wkv_ref[...], ones)
    sig = jax.nn.sigmoid(gate)
    g_mixed = gm_ref[...].astype(jnp.float32)
    g_grouped = g_mixed * gate * sig
    grouped = unit * gain + par_ref[3:4]
    gg_ref[...] = (g_mixed * grouped * sig * (1.0 + gate * (1.0 - sig))).astype(jnp.bfloat16)
    add_to(2, g_grouped * unit)
    add_to(3, g_grouped)
    g_unit = g_grouped * gain
    scale = 1.0 / GROUP_DIMENSION
    g_out = rstd * (
        g_unit - head_sum(g_unit, ones) * scale - unit * (head_sum(g_unit * unit, ones) * scale)
    )

    log_decay, run, before = decay_of(low_ref, up_ref, par_ref)
    last = row_of(run, CHUNK - 1)
    start = spread(held_ref[...], ones)
    end_grad = state[...]
    v_wide = spread(v, ones)
    g_score = mxu(g_out, v_wide, NT)
    score = jnp.zeros((CHUNK, PACK), jnp.float32)
    from_start = jnp.exp(before)
    g_r = from_start * mxu(g_out, start, NN)
    g_before = r * g_r
    to_end = jnp.exp(last - run)
    g_end = to_end * mxu(v, end_grad, NN)
    g_k = g_end
    g_after = k * g_end
    for to_row, to_prior, pairs in piece_factors(run, before):
        r_level = (r * to_row).astype(jnp.bfloat16)
        k_rows = (k * to_prior).astype(jnp.bfloat16)
        k_level = spread(k_rows.astype(jnp.float32), ones).astype(jnp.bfloat16)
        score = jnp.where(pairs, mxu(r_level, k_level, NT), score)
        g_level = jnp.where(pairs, g_score, 0.0).astype(jnp.bfloat16)
        g_rows = mxu(g_level, k_level, NN)
        g_prior = fold(mxu(g_level, r_level, TN), ones)
        g_r = g_r + to_row * g_rows
        g_k = g_k + to_prior * g_prior
        g_before = g_before + r_level.astype(jnp.float32) * g_rows
        g_after = g_after + k_rows.astype(jnp.float32) * g_prior
    g_v = fold(mxu(score, g_out, TN), ones) + mxu(k * to_end, end_grad, NT)
    g_run = g_before - g_after
    g_last = jnp.sum(k * g_end, axis=0, keepdims=True) + jnp.exp(last) * jnp.sum(
        start * end_grad, axis=0, keepdims=True
    )
    upper = jnp.where(iota2((CHUNK, CHUNK), 0) <= iota2((CHUNK, CHUNK), 1), 1.0, 0.0).astype(jnp.float32)
    g_decay = run_sum(upper, g_run) - g_before + g_last
    g_expo = g_decay * log_decay
    gw_ref[...] = g_expo.astype(jnp.bfloat16)
    add_to(0, g_expo)
    g_diag = head_sum(g_out * v, ones)
    add_to(1, r * k * g_diag)
    gr_ref[...] = (g_r + bonus * k * g_diag).astype(jnp.bfloat16)
    gk_ref[...] = (g_k + bonus * r * g_diag).astype(jnp.bfloat16)
    gv_ref[...] = (g_v + head_sum(r * bonus * k, ones) * g_out).astype(jnp.bfloat16)
    state[...] = jnp.exp(last) * end_grad + mxu(g_out, r * from_start, TN) * ones

    @pl.when(pl.program_id(0) == pl.num_programs(0) - 1)
    def _():
        first_ref[...] = fold(state[...], ones)


def wkv_backward(r, k, v, gate, low, up, par, wkv, held, g_mixed):
    rows, columns = r.shape
    chunks = rows // CHUNK
    block = pl.BlockSpec((CHUNK, columns), lambda c: (chunks - 1 - c, 0))
    whole = lambda a: pl.BlockSpec(a.shape, lambda c: (0, 0))
    of_all = lambda n: pl.BlockSpec((n, columns), lambda c: (0, 0))
    low_type = jax.ShapeDtypeStruct((rows, columns), jnp.bfloat16)
    return pl.pallas_call(
        wkv_backward_kernel,
        grid=(chunks,),
        in_specs=[block] * 4
        + [
            pl.BlockSpec((CHUNK, low.shape[1]), lambda c: (chunks - 1 - c, 0)),
            whole(up),
            whole(par),
            block,
            block,
            block,
        ],
        out_specs=[block] * 5 + [of_all(8), of_all(GROUP_DIMENSION)],
        out_shape=[low_type] * 5
        + [
            jax.ShapeDtypeStruct((8, columns), jnp.float32),
            jax.ShapeDtypeStruct((GROUP_DIMENSION, columns), jnp.float32),
        ],
        scratch_shapes=[pltpu.VMEM((columns // PACK, PACK, PACK), jnp.float32)],
        compiler_params=pltpu.CompilerParams(
            dimension_semantics=("arbitrary",), vmem_limit_bytes=32 * 2**20
        ),
        cost_estimate=SOON,
        name="wkv_backward",
    )(r, k, v, gate, low, up, par, wkv, held, g_mixed)


GRAD_ROWS, GRAD_COLUMNS = 512, 256


def grad_kernel(left_ref, right_ref, *rest):
    out_ref = rest[-1]
    turned = left_ref[...].T
    for at in range(0, out_ref.shape[1], GRAD_COLUMNS):
        columns = slice(at, at + GRAD_COLUMNS)
        out_ref[:, columns] = mxu(turned, right_ref[:, columns], NN).astype(jnp.bfloat16)


def grad_into(left, right, total, at, into=None):
    rows, width = left.shape
    columns = right.shape[1]
    shift = at // columns
    specs = [
        pl.BlockSpec((rows, GRAD_ROWS), lambda i: (0, i)),
        pl.BlockSpec((rows, columns), lambda i: (0, 0)),
    ]
    operands = [left, right]
    alias = {}
    if into is not None:
        specs.append(pl.BlockSpec(memory_space=pltpu.HBM))
        operands.append(into)
        alias = {2: 0}
    return pl.pallas_call(
        grad_kernel,
        grid=(width // GRAD_ROWS,),
        in_specs=specs,
        out_specs=pl.BlockSpec((GRAD_ROWS, columns), lambda i: (i, shift)),
        out_shape=pltpu.HBM((width, total), jnp.bfloat16),
        input_output_aliases=alias,
        compiler_params=pltpu.CompilerParams(
            dimension_semantics=("arbitrary",), vmem_limit_bytes=32 * 2**20
        ),
        cost_estimate=SOON,
        name="weight_grad",
    )(*operands)


def grads_kernel(*refs):
    count = len(refs) // 2
    out_ref = refs[-1]
    for n in range(count):

        @pl.when(pl.program_id(0) == n)
        def _(left_ref=refs[n], right_ref=refs[count + n]):
            turned = left_ref[...].T
            for at in range(0, out_ref.shape[1], GRAD_COLUMNS):
                columns = slice(at, at + GRAD_COLUMNS)
                out_ref[:, columns] = mxu(turned, right_ref[:, columns], NN).astype(jnp.bfloat16)


def grads_side_by_side(lefts, rights, total):
    rows, width = lefts[0].shape
    columns = rights[0].shape[1]
    blocks = width // GRAD_ROWS

    def left_spec(n):
        return pl.BlockSpec(
            (rows, GRAD_ROWS),
            lambda p, i: (0, jnp.where(p == n, i, jnp.where(p < n, 0, blocks - 1))),
        )

    return pl.pallas_call(
        grads_kernel,
        grid=(len(lefts), blocks),
        in_specs=[left_spec(n) for n in range(len(lefts))]
        + [pl.BlockSpec((rows, columns), lambda p, i: (0, 0))] * len(rights),
        out_specs=pl.BlockSpec((GRAD_ROWS, columns), lambda p, i: (i, p)),
        out_shape=pltpu.HBM((width, total), jnp.bfloat16),
        compiler_params=pltpu.CompilerParams(
            dimension_semantics=("arbitrary", "arbitrary"), vmem_limit_bytes=32 * 2**20
        ),
        cost_estimate=SOON,
        name="time_mix_grads",
    )(*lefts, *rights)


LOW = 256
SHIFT_LANES = 5 * SHIFT_RANK
LANES = SHIFT_LANES + 64

TILE = 512


def vectors_kernel(up_ref, out_ref):
    turned = up_ref[...].astype(jnp.float32).T
    out_ref[...] = turned[LANES : LANES + 16]


def turn_vectors(first, up_at):
    width = first.shape[0]
    return pl.pallas_call(
        vectors_kernel,
        grid=(width // TILE,),
        in_specs=[pl.BlockSpec((TILE, LOW), lambda n: (n, up_at // LOW))],
        out_specs=pl.BlockSpec((16, TILE), lambda n: (0, n)),
        out_shape=jax.ShapeDtypeStruct((16, width), jnp.float32),
        compiler_params=pltpu.CompilerParams(dimension_semantics=("arbitrary",)),
        cost_estimate=SOON,
        name="turn_vectors",
    )(first)


def lane_group(shape):
    return lax.shift_right_logical(iota2(shape, 1), 5)


def mixes_forward_kernel(
    unit_ref, w_ref, down_ref, up_ref, vec_ref,
    m0_ref, m1_ref, m2_ref, m3_ref, m4_ref, normed_ref, squash_ref, r_ref, k_ref, v_ref, g_ref,
    hidden, grouped,
):
    phase, tile = pl.program_id(0), pl.program_id(1)
    rows = unit_ref.shape[0]
    own = r_ref.shape[1]
    vec = vec_ref[...]
    normed = unit_ref[...] * vec[0:1] + vec[1:2]
    row = iota2(normed.shape, 0)
    shifted = jnp.where(row == 0, 0.0, pltpu.roll(normed, 1, 0)) - normed
    down = down_ref[...]
    of_shift = iota2(down.shape, 1) < SHIFT_LANES

    @pl.when((phase == 0) & (tile == 0))
    def _():
        hidden[...] = jnp.zeros_like(hidden)

    @pl.when(phase == 0)
    def _():
        hidden[...] = hidden[...] + mxu(normed + shifted * vec[2:3], jnp.where(of_shift, down, 0), NN)

    @pl.when((phase == 1) & (tile == 0))
    def _():
        squash = jnp.tanh(hidden[...])
        squash_ref[...] = squash
        group = lane_group(squash.shape)
        for g in range(5):
            grouped[g] = jnp.where(group == g, squash, 0.0).astype(jnp.bfloat16)
        hidden[...] = jnp.zeros_like(hidden)
        for ref in (r_ref, k_ref, v_ref, g_ref):
            ref[...] = jnp.zeros_like(ref)

    @pl.when(phase == 1)
    def _():
        normed_ref[...] = normed
        up = up_ref[...]
        for g, mix_ref in enumerate((m0_ref, m1_ref, m2_ref, m3_ref, m4_ref)):
            mix = (normed + shifted * (vec[3 + g : 4 + g] + mxu(grouped[g], up, NT))).astype(jnp.bfloat16)
            mix_ref[...] = mix
            if g == 0:
                hidden[...] = hidden[...] + mxu(mix, jnp.where(of_shift, 0, down), NN)
            else:
                column = (None, 1, 2, 0, 3)[g] * own
                out = (None, k_ref, v_ref, r_ref, g_ref)[g]
                out[...] = out[...] + mxu(mix, w_ref[:, column : column + own], NN)

    @pl.when((phase == 1) & (tile == pl.num_programs(1) - 1))
    def _():
        squash_ref[...] = squash_ref[...] + jnp.tanh(hidden[...])


def mixes_forward(unit, first, low_at, vec, own):
    rows, width = unit.shape
    tiles = width // TILE
    block = low_at // LOW
    across = lambda r: pl.BlockSpec((r, TILE), lambda p, n: (0, n))
    late = pl.BlockSpec((rows, TILE), lambda p, n: (0, n * p))
    whole = lambda columns: pl.BlockSpec((rows, columns), lambda p, n: (0, 0))
    kept = lambda columns, dtype: jax.ShapeDtypeStruct((rows, columns), dtype)
    return pl.pallas_call(
        mixes_forward_kernel,
        grid=(2, tiles),
        in_specs=[
            across(rows),
            pl.BlockSpec((TILE, 4 * own), lambda p, n: (n * p, 0)),
            pl.BlockSpec((TILE, LOW), lambda p, n: (n, block)),
            pl.BlockSpec((TILE, LOW), lambda p, n: (n, block + 1)),
            across(vec.shape[0]),
        ],
        out_specs=[late] * 6 + [whole(LOW)] + [whole(own)] * 4,
        out_shape=[kept(width, jnp.bfloat16)] * 5
        + [kept(width, jnp.float32), kept(LOW, jnp.float32)]
        + [pltpu.HBM((rows, own), jnp.float32)] * 4,
        scratch_shapes=[pltpu.VMEM((rows, LOW), jnp.float32), pltpu.VMEM((5, rows, LOW), jnp.bfloat16)],
        compiler_params=pltpu.CompilerParams(
            dimension_semantics=("arbitrary", "arbitrary"), vmem_limit_bytes=54 * 2**20
        ),
        cost_estimate=SOON,
        name="mixes_forward",
    )(unit, first, first, first, vec)


def mixes_back_kernel(
    gk_ref, gv_ref, gr_ref, gg_ref, gd_ref, w_ref, down_ref, up_ref, vec_ref, squash_ref, normed_ref,
    mix_ref, sums_ref, out_ref, small_ref,
    g_shift, g_norm, g_squash, g_hidden, g_up, g_sums, grouped, turned,
):
    phase, tile = pl.program_id(0), pl.program_id(1)
    rows = squash_ref.shape[0]
    own = gk_ref.shape[1]
    normed = normed_ref[...]
    row = iota2(normed.shape, 0)
    shifted = jnp.where(row == 0, 0.0, pltpu.roll(normed, 1, 0)) - normed
    squash = squash_ref[...]
    vec = vec_ref[...]

    @pl.when((phase == 0) & (tile == 0))
    def _():
        g_squash[...] = jnp.zeros_like(g_squash)
        group = lane_group(squash.shape)
        for g in range(5):
            grouped[g] = jnp.where(group == g, squash, 0.0).astype(jnp.bfloat16)
        turned[...] = squash.astype(jnp.bfloat16).T

    @pl.when(phase == 0)
    def _():
        up = up_ref[...]
        group_wide = lane_group(up.shape)
        total_shift = jnp.zeros((rows, TILE), jnp.float32)
        total_norm = jnp.zeros((rows, TILE), jnp.float32)
        add_squash = jnp.zeros((rows, LOW), jnp.float32)
        sums = []
        for g in range(5):
            if g == 0:
                part = mxu(gd_ref[...], down_ref[...], NT)
            else:
                column = (None, 1, 2, 0, 3)[g] * own
                grad = (None, gk_ref, gv_ref, gr_ref, gg_ref)[g]
                part = mxu(grad[...], w_ref[:, column : column + own], NT)
            coeff = vec[3 + g : 4 + g] + mxu(grouped[g], up, NT)
            times = part * shifted
            times_low = times.astype(jnp.bfloat16)
            sums.append(jnp.sum(times, axis=0, keepdims=True))
            total_shift = total_shift + part * coeff
            total_norm = total_norm + part
            add_squash = add_squash + mxu(times_low, jnp.where(group_wide == g, up, 0), NN)
            lanes = slice(g * SHIFT_RANK, (g + 1) * SHIFT_RANK)
            g_up[tile, lanes] = mxu(turned[lanes], times_low, NN)
        g_shift[tile] = total_shift
        g_norm[tile] = total_norm
        g_squash[...] = g_squash[...] + add_squash
        g_sums[tile] = jnp.concatenate(sums + [jnp.zeros((3, TILE), jnp.float32)], axis=0)

    @pl.when((phase == 1) & (tile == 0))
    def _():
        g_hidden[...] = (g_squash[...] * (1.0 - squash * squash)).astype(jnp.bfloat16)

    @pl.when(phase == 1)
    def _():
        blend = vec[2:3]
        part = mxu(g_hidden[...], down_ref[...], NT)
        total_shift = g_shift[tile] + part * blend
        total = g_norm[tile] + part - total_shift
        total = total + jnp.where(row == rows - 1, 0.0, pltpu.roll(total_shift, rows - 1, 0))
        out_ref[...] = total.astype(jnp.bfloat16)
        unit = (normed - vec[1:2]) / vec[0:1]
        head = [
            jnp.sum(total * unit, axis=0, keepdims=True),
            jnp.sum(total, axis=0, keepdims=True),
            jnp.sum(part * shifted, axis=0, keepdims=True),
        ]
        sums = jnp.concatenate(head + [g_sums[tile][:5], sums_ref[...]], axis=0)
        shape = (sums.shape[0], LOW)
        behind = jnp.where(iota2(shape, 1) == LANES + iota2(shape, 0), 1.0, 0.0)
        small_ref[:, :LOW] = (
            mxu(normed + shifted * blend, g_hidden[...], TN) + mxu(mix_ref[...], gd_ref[...], TN)
        ).astype(jnp.bfloat16)
        small_ref[:, LOW:] = mxu(sums, behind, TN).astype(jnp.bfloat16)
        small_ref[:, LOW : LOW + SHIFT_LANES] = g_up[tile].T.astype(jnp.bfloat16)


def mixes_back(g_key, g_val, g_recept, g_gate, g_decay, first, low_at, vec, squash, normed, mix, sums):
    rows, width = normed.shape
    own = g_key.shape[1]
    tiles = width // TILE
    block = low_at // LOW
    whole = lambda a: pl.BlockSpec(a.shape, lambda p, n: (0, 0))
    across = lambda r: pl.BlockSpec((r, TILE), lambda p, n: (0, n))
    late = lambda r: pl.BlockSpec((r, TILE), lambda p, n: (0, n * p))
    early = lambda p, n: n * (1 - p) + (tiles - 1) * p
    return pl.pallas_call(
        mixes_back_kernel,
        grid=(2, tiles),
        in_specs=[whole(g_key)] * 4
        + [
            whole(g_decay),
            pl.BlockSpec((TILE, 4 * own), lambda p, n: (early(p, n), 0)),
            pl.BlockSpec((TILE, LOW), lambda p, n: (n, block)),
            pl.BlockSpec((TILE, LOW), lambda p, n: (early(p, n), block + 1)),
            across(vec.shape[0]),
            whole(squash),
            across(rows),
            late(rows),
            late(sums.shape[0]),
        ],
        out_specs=[late(rows), pl.BlockSpec((TILE, 2 * LOW), lambda p, n: (n * p, 0))],
        out_shape=[
            jax.ShapeDtypeStruct((rows, width), jnp.bfloat16),
            jax.ShapeDtypeStruct((width, 2 * LOW), jnp.bfloat16),
        ],
        scratch_shapes=[
            pltpu.VMEM((tiles, rows, TILE), jnp.float32),
            pltpu.VMEM((tiles, rows, TILE), jnp.float32),
            pltpu.VMEM((rows, LOW), jnp.float32),
            pltpu.VMEM((rows, LOW), jnp.bfloat16),
            pltpu.VMEM((tiles, SHIFT_LANES, TILE), jnp.float32),
            pltpu.VMEM((tiles, 8, TILE), jnp.float32),
            pltpu.VMEM((5, rows, LOW), jnp.bfloat16),
            pltpu.VMEM((LOW, rows), jnp.bfloat16),
        ],
        compiler_params=pltpu.CompilerParams(
            dimension_semantics=("arbitrary", "arbitrary"), vmem_limit_bytes=56 * 2**20
        ),
        cost_estimate=SOON,
        name="mixes_back",
    )(g_key, g_val, g_recept, g_gate, g_decay, first, first, first, vec, squash, normed, mix, sums)


def shards(
    inputs,
    cotangent,
    states,
    vectors,
    time_mix_weight,
    output_weight,
    channel_receptance_weight,
    rank_down_weight,
    rank_up_weight,
    channel_key_weight,
    channel_value_weight,
):
    token_rows, width = inputs.shape
    seg_count = lax.axis_size("seg")
    own_width = time_mix_weight.shape[2]
    hidden = channel_key_weight.shape[1]
    local_heads = own_width // GROUP_DIMENSION
    col_start = lax.axis_index("span") * own_width
    position = lax.axis_index("span") * token_rows

    x_seg = span_gather(inputs).astype(jnp.float32)
    grad_columns = split_columns(cotangent).astype(jnp.float32)
    def blank(count):
        return jnp.zeros((token_rows // 8, count), jnp.bfloat16)

    small_rows = jnp.concatenate(
        [rank_down_weight, blank(LOW - LANES), rank_up_weight.T, vectors.T, blank(LOW - LANES - 16)], axis=1
    )
    span_rows = gather_and_split(small_rows, channel_receptance_weight)
    weights = both_planes(lambda proj: [proj[g] for g in range(4)], time_mix_weight)
    small_pair = both_planes(lambda rows: [rows], span_rows[:, own_width:])
    late_pairs = [fill_pair(rows[None])[0] for rows in (output_weight.T, span_rows[:, :own_width])]
    first = plane_gather(jnp.concatenate([weights, small_pair] + late_pairs, axis=1))
    _, unit_seg, _ = norm_rows(x_seg, 1.0, 0.0)
    second_pair = both_planes(lambda key, value: [key, value.T], channel_key_weight, channel_value_weight)
    second_pair, unit_seg, grad_columns = lax.optimization_barrier((second_pair, unit_seg, grad_columns))
    second = plane_gather(second_pair)
    low_at = 4 * own_width
    late_at = low_at + 2 * LOW

    def late_rows(at):
        pairs = first[:, at : at + own_width // 2].reshape(-1, 2 * (width // seg_count), own_width // 2)
        return from_pair(pairs)

    out_half, recept_half = late_rows(late_at), late_rows(late_at + own_width // 2)
    late_got = swap_high(jnp.concatenate([out_half, recept_half], axis=2))
    out_got, recept_got = late_got[:, :, :own_width], late_got[:, :, own_width:]
    up_at = low_at + LOW
    vec = first[:, up_at + LANES : up_at + LANES + 16].T.astype(jnp.float32)

    def own_cols(line):
        return lax.dynamic_slice_in_dim(line, col_start, own_width, line.ndim - 1)

    def own_rows(values):
        return lax.dynamic_slice_in_dim(values, position, token_rows, 0)

    x_in = inputs.astype(jnp.float32)
    *mixes, normed, squash, recept, key_proj, val_proj, gate_pre = mixes_forward(
        unit_seg, first, low_at, vec, own_width
    )
    lane = lax.broadcasted_iota(jnp.int32, squash.shape, 1)
    of_decay = (lane >= SHIFT_LANES) & (lane < LANES)
    decay_low = jnp.where(of_decay, squash, 0.0).astype(jnp.bfloat16)
    up_own = lax.dynamic_slice(first, (col_start, up_at), (own_width, LOW))
    head_vec = jnp.concatenate([own_cols(vec[8:12]), jnp.zeros((4, own_width), jnp.float32)], axis=0)
    first_state = jnp.transpose(states[0], (2, 0, 1)).reshape(GROUP_DIMENSION, own_width)
    out_w = other_plane(out_half, out_got)
    heads_in = (recept, key_proj, val_proj, gate_pre, decay_low, up_own, head_vec)
    mixed, wkv, held = wkv_forward(*heads_in, first_state)
    recept_w = other_plane(recept_half, recept_got)
    resid = x_in + span_reduce(backward_product(mixed, out_w).astype(jnp.bfloat16))

    normed_two, unit_two, rstd_two = norm_rows(resid, vec[12], vec[13])
    n2 = span_gather(normed_two.astype(jnp.bfloat16)).astype(jnp.float32)
    shifted_two = prior_rows(n2) - n2
    key_in = (n2 + shifted_two * vec[14]).astype(jnp.bfloat16)
    rec_in = (n2 + shifted_two * vec[15]).astype(jnp.bfloat16)
    rec_gate = jax.nn.sigmoid(product_lower(rec_in, recept_w))
    g_value = (grad_columns * rec_gate).astype(jnp.bfloat16)
    g_value, second = lax.optimization_barrier((g_value, second))
    g_value_all = span_gather(g_value, 1)
    key_w, value_w = second[:, :hidden], second[:, hidden:]
    hidden_two = product_lower(key_in, key_w)
    active = jax.nn.relu(hidden_two)
    squared = (active * active).astype(jnp.bfloat16)
    active = active.astype(jnp.bfloat16)

    low = lax.axis_index("span") // 2

    def value_columns(which):
        weights = lax.dynamic_slice(second, (which * (width // 2), hidden), (width // 2, hidden))
        return core_reduce(backward_product(squared, weights).astype(jnp.bfloat16))

    far, near = value_columns(1 - low), value_columns(low)
    far, g_value_all = lax.optimization_barrier((far.astype(jnp.bfloat16), g_value_all))
    far = swap_low(far)
    cm_total = 2 * hidden
    g_hid = (product_lower(g_value_all, value_w) * 2.0 * active.astype(jnp.float32)).astype(jnp.bfloat16)
    g_value_all, g_hid = lax.optimization_barrier((g_value_all, g_hid))
    cm_part = grad_into(g_value_all, squared, cm_total, hidden)
    far, near, cm_part = lax.optimization_barrier((far, near, cm_part))
    cm_part = grad_into(key_in, g_hid, cm_total, 0, cm_part)
    cm_part, g_hid = lax.optimization_barrier((cm_part, g_hid))
    cm_pair = plane_scatter(cm_part)
    value_out = near + far.astype(jnp.float32)
    gated = (rec_gate * value_out).astype(jnp.bfloat16)
    g_rec = (grad_columns * value_out * rec_gate * (1.0 - rec_gate)).astype(jnp.bfloat16)
    g_key_in = backward_product(g_hid, key_w)
    g_rec_in = backward_product(g_rec, recept_w)
    vec_fourteen = jnp.sum(g_key_in * shifted_two, axis=0)
    vec_fifteen = jnp.sum(g_rec_in * shifted_two, axis=0)
    g_shift_two = g_key_in * vec[14] + g_rec_in * vec[15]
    g_n2_part = g_key_in + g_rec_in - g_shift_two + next_rows(g_shift_two)
    g_n2 = span_reduce(g_n2_part.astype(jnp.bfloat16))
    rec_part = grad_into(rec_in, g_rec, own_width, 0)
    g_n2, rec_part = lax.optimization_barrier((g_n2, rec_part))
    vec_twelve = jnp.sum(g_n2 * unit_two, axis=0)
    vec_thirteen = jnp.sum(g_n2, axis=0)
    g_resid = cotangent.astype(jnp.float32) + norm_back(g_n2, unit_two, rstd_two, vec[12])

    g_att = span_gather(g_resid.astype(jnp.bfloat16))
    rec_part = rec_part.reshape(seg_count // 2, 2, width // seg_count, own_width)
    rec_mine, rec_send = in_order(rec_part[:, 0], rec_part[:, 1], lax.axis_index("seg") % 2 == 1)
    g_att, gated, rec_send = lax.optimization_barrier((g_att, gated, rec_send))
    rec_got = swap_high(rec_send)
    gated_rows = join_columns(gated)
    g_mixed = product_lower(g_att, out_w)
    g_recept, g_key, g_val, g_gate, g_ww, head_sums, g_first = wkv_backward(
        *heads_in, wkv, held, g_mixed
    )
    state_grad = jnp.transpose(
        g_first.reshape(GROUP_DIMENSION, local_heads, GROUP_DIMENSION), (1, 2, 0)
    )[None]
    tm_total = 5 * own_width + own_width // 2
    tm_part = grads_side_by_side(
        (g_att, mixes[3], mixes[1], mixes[2], mixes[4]), (mixed, g_recept, g_key, g_val, g_gate), tm_total
    )
    rec_got, g_ww = lax.optimization_barrier((rec_got, g_ww))
    rec_sum = (rec_mine.astype(jnp.float32) + rec_got.astype(jnp.float32)).astype(jnp.bfloat16)
    tm_part = lax.dynamic_update_slice(
        tm_part, fill_pair(rec_sum).reshape(width, own_width // 2), (0, 5 * own_width)
    )
    tm_part, cm_pair, gated_rows = lax.optimization_barrier((tm_part, cm_pair, gated_rows))
    output = (resid + gated_rows.astype(jnp.float32)).astype(jnp.bfloat16)
    tm_pair = plane_scatter(tm_part)
    g_key, g_ww, cm_pair = lax.optimization_barrier((g_key, g_ww, cm_pair))

    g_decay_hidden = jnp.where(
        of_decay, product_lower(g_ww, up_own) * (1.0 - squash * squash), 0.0
    ).astype(jnp.bfloat16)
    up_decay_grad = outer_sum(g_ww, decay_low)
    other_sums = jnp.concatenate(
        [
            lax.dynamic_update_slice_in_dim(jnp.zeros((4, width), jnp.float32), head_sums[:4], col_start, 1),
            jnp.stack([vec_twelve, vec_thirteen, vec_fourteen, vec_fifteen]),
        ],
        axis=0,
    )
    g_normed, small_part = mixes_back(
        g_key, g_val, g_recept, g_gate, g_decay_hidden, first, low_at, vec, squash, normed, mixes[0], other_sums
    )
    own_part = lax.dynamic_slice(small_part, (col_start, LOW), (own_width, LOW))
    small_part = lax.dynamic_update_slice(
        small_part, (own_part.astype(jnp.float32) + up_decay_grad).astype(jnp.bfloat16), (col_start, LOW)
    )
    small, g_n1, cm_grad = reduce_small(small_part, over_cores(g_normed), cm_pair)
    rec_own = from_pair(tm_pair[None, :, 5 * own_width :])[0]
    tm_grad = finish_scatter(*plane_halves(tm_pair[:, : 5 * own_width]))
    _, unit_own, rstd_own = norm_rows(x_in, vec[0], vec[1])
    x_grad = g_resid + norm_back(g_n1, unit_own, rstd_own, vec[0])
    down_grad = small[:, :LANES]
    up_grad = small[:, LOW : LOW + LANES].T
    vec_grad = small[:, LOW + LANES : LOW + LANES + 16].T
    rec_grad = join_columns(rec_own).astype(jnp.float32)
    value_grad = cm_grad[:, hidden:].T
    key_grad = cm_grad[:, :hidden]
    out_grad = tm_grad[:, :own_width].T
    proj_grad = jnp.moveaxis(tm_grad[:, own_width : 5 * own_width].reshape(-1, 4, own_width), 1, 0)
    return (
        output,
        x_grad,
        state_grad,
        vec_grad,
        proj_grad,
        out_grad,
        rec_grad,
        down_grad,
        up_grad,
        key_grad,
        value_grad,
    )


def solution(mesh):
    rows, columns = P(ALL, None), P(None, ALL)
    state = P("seg", "span", None, None)
    time_mix = P(None, "seg", "span")
    turned, straight = P("span", "seg"), P("seg", "span")
    return jax.shard_map(
        shards,
        mesh=mesh,
        in_specs=(
            rows, rows, state, columns, time_mix, turned, rows, rows, columns, straight, turned
        ),
        out_specs=(
            rows, rows, state, columns, time_mix, turned, rows, rows, columns, straight, turned
        ),
        check_vma=False,
    )
```

```python
import jax
import jax.numpy as jnp
from jax import lax
from jax.experimental import pallas as pl
from jax.experimental.pallas import tpu as pltpu
from jax.experimental.layout import Layout, with_layout_constraint
from jax.sharding import PartitionSpec as P

GROUP_DIMENSION = 64
SHIFT_RANK = 32
ALL = ("seg", "span")

maximal_accuracy = lax.Precision.HIGHEST
ln_eps = 1e-05
gn_eps = 0.00064


def swap(block, bit):
    count = lax.axis_size("seg") * lax.axis_size("span")
    return lax.ppermute(block, ALL, [(i, i ^ bit) for i in range(count)])


def swap_core(block):
    return swap(block, 1)


def swap_low(block):
    return swap(block, 2)


def swap_high(block):
    return swap(block, 4)


def plane_groups():
    half = lax.axis_size("seg") // 2
    return [[2 * j + h for j in range(half)] for h in range(2)]


def in_order(own, other, second):
    return jnp.where(second, other, own), jnp.where(second, own, other)


def span_gather(block, axis=0):
    place = lax.axis_index("span")
    low, core = place // 2, place % 2
    p0, p1 = in_order(block, swap_low(block), low == 1)
    q = swap_core(jnp.stack([p0, p1]))
    a0, a1 = in_order(p0, q[0], core == 1)
    b0, b1 = in_order(p1, q[1], core == 1)
    return jnp.concatenate([a0, a1, b0, b1], axis=axis)


def core_reduce(part):
    core = lax.axis_index("span") % 2
    half = part.shape[1] // 2
    keep, send = in_order(part[:, :half], part[:, half:], core == 1)
    return keep.astype(jnp.float32) + swap_core(send.astype(jnp.bfloat16)).astype(jnp.float32)


def over_cores(part):
    core = lax.axis_index("span") % 2
    b = part.reshape(2, 2, part.shape[0] // 4, part.shape[1])
    keep, send = in_order(b[:, 0], b[:, 1], core == 1)
    return keep.astype(jnp.float32) + swap_core(send.astype(jnp.bfloat16)).astype(jnp.float32)


def over_low(both):
    low = lax.axis_index("span") // 2
    mine, send = in_order(both[0], both[1], low == 1)
    return mine + swap_low(send.astype(jnp.bfloat16)).astype(jnp.float32)


def span_reduce(part):
    return over_low(over_cores(part))


def fill_pair(rows):
    half = rows.shape[2] // 2
    return jnp.concatenate([rows[:, :, :half], rows[:, :, half:]], axis=1)


def from_pair(pairs):
    half = pairs.shape[1] // 2
    return jnp.concatenate([pairs[:, :half], pairs[:, half:]], axis=2)


def other_plane(rows, got):
    high = lax.axis_index("seg") % 2
    return jnp.stack(in_order(rows, got, high == 1), axis=1).reshape(-1, rows.shape[2])


def both_planes(laid, *blocks):
    high = lax.axis_index("seg") % 2
    own, other = (
        jnp.concatenate(laid(*got), axis=1) for got in (blocks, [swap_high(block) for block in blocks])
    )
    return jnp.concatenate(in_order(own, other, high == 1), axis=0)


def plane_gather(pair):
    whole = lax.all_gather(
        pair,
        "seg",
        axis=0,
        tiled=True,
        axis_index_groups=plane_groups(),
    )
    return with_layout_constraint(whole, Layout(major_to_minor=(0, 1)))


def plane_scatter(part):
    return lax.psum_scatter(
        part, "seg", scatter_dimension=0, tiled=True, axis_index_groups=plane_groups()
    )


def plane_halves(pair):
    high = lax.axis_index("seg") % 2
    rows = pair.shape[0] // 2
    return in_order(pair[:rows], pair[rows:], high == 1)


def finish_scatter(mine, send):
    return mine.astype(jnp.float32) + swap_high(send).astype(jnp.float32)


def gather_and_split(small, wide):
    place = lax.axis_index("span")
    n = wide.shape[1] // 4
    messages = [
        jnp.concatenate([lax.dynamic_slice_in_dim(wide, (place ^ bit) * n, n, 1), small], axis=1)
        for bit in range(4)
    ]
    pieces = [m if bit == 0 else swap(m, bit) for bit, m in enumerate(messages)]
    result = jnp.zeros((4, *messages[0].shape), small.dtype)
    for bit, piece in enumerate(pieces):
        result = lax.dynamic_update_index_in_dim(result, piece, place ^ bit, 0)
    return result.reshape(4 * small.shape[0], -1)


def split_columns(block):
    place = lax.axis_index("span")
    n = block.shape[1] // 4

    def columns(at):
        return lax.dynamic_slice_in_dim(block, at * n, n, 1)

    pieces = [columns(place)] + [swap(columns(place ^ bit), bit) for bit in (1, 2, 3)]
    result = jnp.zeros((4, block.shape[0], n), block.dtype)
    for bit, piece in enumerate(pieces):
        result = lax.dynamic_update_index_in_dim(result, piece, place ^ bit, 0)
    return result.reshape(4 * block.shape[0], n)


def join_columns(block):
    place = lax.axis_index("span")
    r, n = block.shape[0] // 4, block.shape[1]

    def rows(at):
        return lax.dynamic_slice_in_dim(block, at * r, r, 0)

    result = jnp.zeros((r, 4 * n), block.dtype)
    for bit in range(4):
        piece = rows(place ^ bit)
        if bit:
            piece = swap(piece, bit)
        result = lax.dynamic_update_slice_in_dim(result, piece, (place ^ bit) * n, 1)
    return result


def product_lower(left_arg, right_arg):
    return jnp.dot(left_arg, right_arg, preferred_element_type=jnp.float32)


def outer_sum(left_arg, right_arg):
    return jnp.einsum("td,te->de", left_arg, right_arg, preferred_element_type=jnp.float32)


def backward_product(gradient, weights):
    return jnp.einsum("te,de->td", gradient, weights, preferred_element_type=jnp.float32)


def norm_rows(values, gain_vec, offset):
    centre = values - jnp.mean(values, -1, keepdims=True)
    row_rstd = lax.rsqrt(jnp.mean(centre * centre, -1, keepdims=True) + ln_eps)
    unit_rows = centre * row_rstd
    return (unit_rows * gain_vec + offset, unit_rows, row_rstd)


def norm_back(gradient, unit_rows, row_rstd, gain_vec):
    scaled = gradient * gain_vec
    return row_rstd * (
        scaled
        - jnp.mean(scaled, -1, keepdims=True)
        - unit_rows * jnp.mean(scaled * unit_rows, -1, keepdims=True)
    )


def prior_rows(values):
    return jnp.concatenate([jnp.zeros_like(values[:1]), values[:-1]], axis=0)


def next_rows(values):
    return jnp.concatenate([values[1:], jnp.zeros_like(values[:1])], axis=0)


def reduce_small(part, both, pair):
    place, high = lax.axis_index("span"), lax.axis_index("seg") % 2
    planes = lax.axis_size("seg") // 2
    width = part.shape[1]
    b = part.reshape(planes, 2, 2, 2, -1, width)

    def summed(b, dim, bit, move):
        at0, at1 = (lax.index_in_dim(b, k, dim, keepdims=False) for k in (0, 1))
        mine, send = in_order(at0, at1, bit == 1)
        return mine.astype(jnp.float32) + move(send.astype(jnp.bfloat16)).astype(jnp.float32)

    b = summed(summed(b, 3, place % 2, swap_core), 2, place // 2, swap_low)
    b, both = lax.optimization_barrier((b, both))
    rows = over_low(both)
    b = summed(b, 1, high, swap_high).astype(jnp.bfloat16)
    b, pair = lax.optimization_barrier((b, pair))
    finished = finish_scatter(*plane_halves(pair))
    arrived = lax.all_to_all(
        b, "seg", split_axis=0, concat_axis=0, tiled=True, axis_index_groups=plane_groups()
    )
    return arrived.astype(jnp.float32).sum(axis=0), rows, finished


SOON = pl.CostEstimate(flops=2**20, bytes_accessed=2**16, transcendentals=0)

CHUNK = 64
PACK = 256


def mxu(a, b, contract):
    return lax.dot_general(
        a.astype(jnp.bfloat16),
        b.astype(jnp.bfloat16),
        (contract, ((), ())),
        preferred_element_type=jnp.float32,
    )


NN, NT, TN = ((1,), (0,)), ((1,), (1,)), ((0,), (0,))


def halves(values):
    high = values.astype(jnp.bfloat16)
    return high, (values - high.astype(jnp.float32)).astype(jnp.bfloat16)


def iota2(shape, dim):
    return lax.broadcasted_iota(jnp.int32, shape, dim)


def head_ones():
    shape = (PACK, PACK)
    same = (iota2(shape, 0) ^ iota2(shape, 1)) < GROUP_DIMENSION
    return jnp.where(same, 1.0, 0.0).astype(jnp.float32)


def spread(block, ones):
    return jnp.concatenate([block] * (PACK // CHUNK), axis=0) * ones


def fold(big, ones):
    kept = big * ones
    total = kept[:CHUNK]
    for h in range(1, PACK // CHUNK):
        total = total + kept[h * CHUNK : (h + 1) * CHUNK]
    return total


def head_sum(values, ones):
    high, rest = halves(values)
    return mxu(high, ones, NN) + mxu(rest, ones, NN)


def run_sum(which, values):
    high, rest = halves(values)
    return mxu(which, high, NN) + mxu(which, rest, NN)


def row_of(values, row):
    return values[row : row + 1]


def piece_factors(run, before):
    rows = iota2((CHUNK, PACK), 0)
    apart = rows ^ (iota2((CHUNK, PACK), 1) & (CHUNK - 1))
    levels = []
    for half in (32, 16, 8, 4, 2, 1):
        upper = (rows & half) != 0
        if half == 1:
            scale = jnp.ones_like(run)
        else:
            if half == 2:
                reference = run
                for row, shift in ((0, CHUNK - 1), (2, 1), (3, 2)):
                    reference = jnp.where((rows & 3) == row, pltpu.roll(run, shift, 0), reference)
            else:
                reference = jnp.broadcast_to(row_of(run, half - 1), run.shape)
                for start in range(2 * half, CHUNK, 2 * half):
                    here = jnp.broadcast_to(row_of(run, start + half - 1), run.shape)
                    reference = jnp.where(rows >= start, here, reference)
            scale = jnp.exp(jnp.minimum(jnp.where(upper, before - reference, reference - run), 0.0))
        pairs = (apart < 2 * half) & upper & ((apart & half) != 0)
        levels.append((jnp.where(upper, scale, 0.0), jnp.where(upper, 0.0, scale), pairs))
    return levels


NOTHING = -104.0


def lower_ones():
    return jnp.where(iota2((CHUNK, CHUNK), 0) >= iota2((CHUNK, CHUNK), 1), 1.0, 0.0).astype(jnp.float32)


def decay_of(low_ref, up_ref, par_ref):
    log_decay = -jnp.exp(par_ref[0:1] + mxu(low_ref[...], up_ref[...], NT))
    kept = jnp.maximum(log_decay, NOTHING)
    run = run_sum(lower_ones(), kept)
    return jnp.where(log_decay <= NOTHING, 0.0, log_decay), run, run - kept


def unit_heads(wkv, ones):
    centre = wkv - head_sum(wkv, ones) * (1.0 / GROUP_DIMENSION)
    rstd = lax.rsqrt(head_sum(centre * centre, ones) * (1.0 / GROUP_DIMENSION) + gn_eps)
    return centre * rstd, rstd


def lane_groups(refs, kinds):
    width = refs[0].shape[1]
    for g in range(width // PACK):
        lanes = pl.ds(g * PACK, PACK)
        part = {"c": lambda ref: ref.at[:, lanes], "r": lambda ref: ref.at[lanes], "s": lambda ref: ref.at[g]}
        yield [ref if kind == "w" else part[kind](ref) for ref, kind in zip(refs, kinds)]


def wkv_forward_kernel(*refs):
    groups = list(lane_groups(refs, "ccccwrcccccs"))
    ones = head_ones()

    @pl.when(pl.program_id(0) == 0)
    def _():
        for *_, first_ref, _, _, _, state in groups:
            state[...] = spread(first_ref[...], ones)

    for group in groups:
        forward_heads(ones, *group)


def wkv_backward_kernel(*refs):
    groups = list(lane_groups(refs, "ccccwrccccccccccc" + "s"))
    ones = head_ones()

    @pl.when(pl.program_id(0) == 0)
    def _():
        for *_, sums_ref, _, state in groups:
            state[...] = jnp.zeros_like(state)
            sums_ref[...] = jnp.zeros_like(sums_ref)

    for group in groups:
        backward_heads(ones, *group)

    @pl.when(pl.program_id(0) == pl.num_programs(0) - 1)
    def _():
        for *_, first_ref, state in groups:
            first_ref[...] = fold(state[...], ones)


def forward_heads(
    ones, r_ref, k_ref, v_ref, gate_ref, low_ref, up_ref, par_ref, first_ref, mixed_ref, wkv_ref, held_ref, state
):
    r, k, v = r_ref[...], k_ref[...], v_ref[...]
    _, run, before = decay_of(low_ref, up_ref, par_ref)
    held_ref[...] = fold(state[...], ones)
    score = jnp.zeros((CHUNK, PACK), jnp.float32)
    for to_row, to_prior, pairs in piece_factors(run, before):
        score = jnp.where(pairs, mxu(r * to_row, spread(k * to_prior, ones), NT), score)
    out = mxu(score, spread(v, ones), NN) + mxu(r * jnp.exp(before), state[...], NT)
    out = out + head_sum(r * par_ref[1:2] * k, ones) * v
    wkv_ref[...] = out
    last = row_of(run, CHUNK - 1)
    state[...] = jnp.exp(last) * state[...] + mxu(v, k * jnp.exp(last - run), TN) * ones
    unit, _ = unit_heads(out, ones)
    gate = gate_ref[...]
    mixed_ref[...] = ((unit * par_ref[2:3] + par_ref[3:4]) * gate * jax.nn.sigmoid(gate)).astype(jnp.bfloat16)


def wkv_forward(r, k, v, gate, low, up, par, first):
    rows, columns = r.shape
    chunks = rows // CHUNK
    block = pl.BlockSpec((CHUNK, columns), lambda c: (c, 0))
    whole = lambda a: pl.BlockSpec(a.shape, lambda c: (0, 0))
    return pl.pallas_call(
        wkv_forward_kernel,
        grid=(chunks,),
        in_specs=[block] * 4
        + [
            pl.BlockSpec((CHUNK, low.shape[1]), lambda c: (c, 0)),
            whole(up),
            whole(par),
            whole(first),
        ],
        out_specs=[block, block, block],
        out_shape=[
            jax.ShapeDtypeStruct((rows, columns), jnp.bfloat16),
            jax.ShapeDtypeStruct((rows, columns), jnp.float32),
            jax.ShapeDtypeStruct((rows, columns), jnp.float32),
        ],
        scratch_shapes=[pltpu.VMEM((columns // PACK, PACK, PACK), jnp.float32)],
        compiler_params=pltpu.CompilerParams(
            dimension_semantics=("arbitrary",), vmem_limit_bytes=32 * 2**20
        ),
        cost_estimate=SOON,
        name="wkv_forward",
    )(*[pltpu.with_memory_space_constraint(x, pltpu.HBM) for x in (r, k, v, gate)], low, up, par, first)


def backward_heads(
    ones, r_ref, k_ref, v_ref, gate_ref, low_ref, up_ref, par_ref, wkv_ref, held_ref, gm_ref,
    gr_ref, gk_ref, gv_ref, gg_ref, gw_ref, sums_ref, first_ref, state,
):
    r, k, v, gate = r_ref[...], k_ref[...], v_ref[...], gate_ref[...]
    bonus, gain = par_ref[1:2], par_ref[2:3]

    def add_to(row, values):
        sums_ref[row : row + 1] = sums_ref[row : row + 1] + jnp.sum(values, axis=0, keepdims=True)

    unit, rstd = unit_heads(wkv_ref[...], ones)
    sig = jax.nn.sigmoid(gate)
    g_mixed = gm_ref[...].astype(jnp.float32)
    g_grouped = g_mixed * gate * sig
    grouped = unit * gain + par_ref[3:4]
    gg_ref[...] = (g_mixed * grouped * sig * (1.0 + gate * (1.0 - sig))).astype(jnp.bfloat16)
    add_to(2, g_grouped * unit)
    add_to(3, g_grouped)
    g_unit = g_grouped * gain
    scale = 1.0 / GROUP_DIMENSION
    g_out = rstd * (
        g_unit - head_sum(g_unit, ones) * scale - unit * (head_sum(g_unit * unit, ones) * scale)
    )

    log_decay, run, before = decay_of(low_ref, up_ref, par_ref)
    last = row_of(run, CHUNK - 1)
    start = spread(held_ref[...], ones)
    end_grad = state[...]
    v_wide = spread(v, ones)
    g_score = mxu(g_out, v_wide, NT)
    score = jnp.zeros((CHUNK, PACK), jnp.float32)
    from_start = jnp.exp(before)
    g_r = from_start * mxu(g_out, start, NN)
    g_before = r * g_r
    to_end = jnp.exp(last - run)
    g_end = to_end * mxu(v, end_grad, NN)
    g_k = g_end
    g_after = k * g_end
    for to_row, to_prior, pairs in piece_factors(run, before):
        r_level = (r * to_row).astype(jnp.bfloat16)
        k_rows = (k * to_prior).astype(jnp.bfloat16)
        k_level = spread(k_rows.astype(jnp.float32), ones).astype(jnp.bfloat16)
        score = jnp.where(pairs, mxu(r_level, k_level, NT), score)
        g_level = jnp.where(pairs, g_score, 0.0).astype(jnp.bfloat16)
        g_rows = mxu(g_level, k_level, NN)
        g_prior = fold(mxu(g_level, r_level, TN), ones)
        g_r = g_r + to_row * g_rows
        g_k = g_k + to_prior * g_prior
        g_before = g_before + r_level.astype(jnp.float32) * g_rows
        g_after = g_after + k_rows.astype(jnp.float32) * g_prior
    g_v = fold(mxu(score, g_out, TN), ones) + mxu(k * to_end, end_grad, NT)
    g_run = g_before - g_after
    g_last = jnp.sum(k * g_end, axis=0, keepdims=True) + jnp.exp(last) * jnp.sum(
        start * end_grad, axis=0, keepdims=True
    )
    upper = jnp.where(iota2((CHUNK, CHUNK), 0) <= iota2((CHUNK, CHUNK), 1), 1.0, 0.0).astype(jnp.float32)
    g_decay = run_sum(upper, g_run) - g_before + g_last
    g_expo = g_decay * log_decay
    gw_ref[...] = g_expo.astype(jnp.bfloat16)
    add_to(0, g_expo)
    g_diag = head_sum(g_out * v, ones)
    add_to(1, r * k * g_diag)
    gr_ref[...] = (g_r + bonus * k * g_diag).astype(jnp.bfloat16)
    gk_ref[...] = (g_k + bonus * r * g_diag).astype(jnp.bfloat16)
    gv_ref[...] = (g_v + head_sum(r * bonus * k, ones) * g_out).astype(jnp.bfloat16)
    state[...] = jnp.exp(last) * end_grad + mxu(g_out, r * from_start, TN) * ones


def wkv_backward(r, k, v, gate, low, up, par, wkv, held, g_mixed):
    rows, columns = r.shape
    chunks = rows // CHUNK
    block = pl.BlockSpec((CHUNK, columns), lambda c: (chunks - 1 - c, 0))
    whole = lambda a: pl.BlockSpec(a.shape, lambda c: (0, 0))
    of_all = lambda n: pl.BlockSpec((n, columns), lambda c: (0, 0))
    low_type = jax.ShapeDtypeStruct((rows, columns), jnp.bfloat16)
    return pl.pallas_call(
        wkv_backward_kernel,
        grid=(chunks,),
        in_specs=[block] * 4
        + [
            pl.BlockSpec((CHUNK, low.shape[1]), lambda c: (chunks - 1 - c, 0)),
            whole(up),
            whole(par),
            block,
            block,
            block,
        ],
        out_specs=[block] * 5 + [of_all(8), of_all(GROUP_DIMENSION)],
        out_shape=[low_type] * 5
        + [
            jax.ShapeDtypeStruct((8, columns), jnp.float32),
            jax.ShapeDtypeStruct((GROUP_DIMENSION, columns), jnp.float32),
        ],
        scratch_shapes=[pltpu.VMEM((columns // PACK, PACK, PACK), jnp.float32)],
        compiler_params=pltpu.CompilerParams(
            dimension_semantics=("arbitrary",), vmem_limit_bytes=32 * 2**20
        ),
        cost_estimate=SOON,
        name="wkv_backward",
    )(r, k, v, gate, low, up, par, wkv, held, g_mixed)


GRAD_ROWS, GRAD_COLUMNS = 512, 256


def grad_kernel(left_ref, right_ref, *rest):
    out_ref = rest[-1]
    turned = left_ref[...].T
    for at in range(0, out_ref.shape[1], GRAD_COLUMNS):
        columns = slice(at, at + GRAD_COLUMNS)
        out_ref[:, columns] = mxu(turned, right_ref[:, columns], NN).astype(jnp.bfloat16)


def grad_into(left, right, total, at, into=None):
    rows, width = left.shape
    columns = right.shape[1]
    shift = at // columns
    specs = [
        pl.BlockSpec((rows, GRAD_ROWS), lambda i: (0, i)),
        pl.BlockSpec((rows, columns), lambda i: (0, 0)),
    ]
    operands = [left, right]
    alias = {}
    if into is not None:
        specs.append(pl.BlockSpec(memory_space=pltpu.HBM))
        operands.append(into)
        alias = {2: 0}
    return pl.pallas_call(
        grad_kernel,
        grid=(width // GRAD_ROWS,),
        in_specs=specs,
        out_specs=pl.BlockSpec((GRAD_ROWS, columns), lambda i: (i, shift)),
        out_shape=pltpu.HBM((width, total), jnp.bfloat16),
        input_output_aliases=alias,
        compiler_params=pltpu.CompilerParams(
            dimension_semantics=("arbitrary",), vmem_limit_bytes=32 * 2**20
        ),
        cost_estimate=SOON,
        name="weight_grad",
    )(*operands)


def grads_kernel(*refs):
    count = len(refs) // 2
    out_ref = refs[-1]
    for n in range(count):

        @pl.when(pl.program_id(0) == n)
        def _(left_ref=refs[n], right_ref=refs[count + n]):
            turned = left_ref[...].T
            for at in range(0, out_ref.shape[1], GRAD_COLUMNS):
                columns = slice(at, at + GRAD_COLUMNS)
                out_ref[:, columns] = mxu(turned, right_ref[:, columns], NN).astype(jnp.bfloat16)


def grads_side_by_side(lefts, rights, total):
    rows, width = lefts[0].shape
    columns = rights[0].shape[1]
    blocks = width // GRAD_ROWS

    def left_spec(n):
        return pl.BlockSpec(
            (rows, GRAD_ROWS),
            lambda p, i: (0, jnp.where(p == n, i, jnp.where(p < n, 0, blocks - 1))),
        )

    return pl.pallas_call(
        grads_kernel,
        grid=(len(lefts), blocks),
        in_specs=[left_spec(n) for n in range(len(lefts))]
        + [pl.BlockSpec((rows, columns), lambda p, i: (0, 0))] * len(rights),
        out_specs=pl.BlockSpec((GRAD_ROWS, columns), lambda p, i: (i, p)),
        out_shape=pltpu.HBM((width, total), jnp.bfloat16),
        compiler_params=pltpu.CompilerParams(
            dimension_semantics=("arbitrary", "arbitrary"), vmem_limit_bytes=32 * 2**20
        ),
        cost_estimate=SOON,
        name="time_mix_grads",
    )(*lefts, *rights)


LOW = 256
SHIFT_LANES = 5 * SHIFT_RANK
LANES = SHIFT_LANES + 64

TILE = 512


def vectors_kernel(up_ref, out_ref):
    turned = up_ref[...].astype(jnp.float32).T
    out_ref[...] = turned[LANES : LANES + 16]


def turn_vectors(first, up_at):
    width = first.shape[0]
    return pl.pallas_call(
        vectors_kernel,
        grid=(width // TILE,),
        in_specs=[pl.BlockSpec((TILE, LOW), lambda n: (n, up_at // LOW))],
        out_specs=pl.BlockSpec((16, TILE), lambda n: (0, n)),
        out_shape=jax.ShapeDtypeStruct((16, width), jnp.float32),
        compiler_params=pltpu.CompilerParams(dimension_semantics=("arbitrary",)),
        cost_estimate=SOON,
        name="turn_vectors",
    )(first)


def lane_group(shape):
    return lax.shift_right_logical(iota2(shape, 1), 5)


def mixes_forward_kernel(
    unit_ref, w_ref, down_ref, up_ref, vec_ref,
    m0_ref, m1_ref, m2_ref, m3_ref, m4_ref, normed_ref, squash_ref, r_ref, k_ref, v_ref, g_ref,
    hidden, grouped,
):
    phase, tile = pl.program_id(0), pl.program_id(1)
    rows = unit_ref.shape[0]
    own = r_ref.shape[1]
    vec = vec_ref[...]
    normed = unit_ref[...] * vec[0:1] + vec[1:2]
    row = iota2(normed.shape, 0)
    shifted = jnp.where(row == 0, 0.0, pltpu.roll(normed, 1, 0)) - normed
    down = down_ref[...]
    of_shift = iota2(down.shape, 1) < SHIFT_LANES

    @pl.when((phase == 0) & (tile == 0))
    def _():
        hidden[...] = jnp.zeros_like(hidden)

    @pl.when(phase == 0)
    def _():
        hidden[...] = hidden[...] + mxu(normed + shifted * vec[2:3], jnp.where(of_shift, down, 0), NN)

    @pl.when((phase == 1) & (tile == 0))
    def _():
        squash = jnp.tanh(hidden[...])
        squash_ref[...] = squash
        group = lane_group(squash.shape)
        for g in range(5):
            grouped[g] = jnp.where(group == g, squash, 0.0).astype(jnp.bfloat16)
        hidden[...] = jnp.zeros_like(hidden)
        for ref in (r_ref, k_ref, v_ref, g_ref):
            ref[...] = jnp.zeros_like(ref)

    @pl.when(phase == 1)
    def _():
        normed_ref[...] = normed
        up = up_ref[...]
        for g, mix_ref in enumerate((m0_ref, m1_ref, m2_ref, m3_ref, m4_ref)):
            mix = (normed + shifted * (vec[3 + g : 4 + g] + mxu(grouped[g], up, NT))).astype(jnp.bfloat16)
            mix_ref[...] = mix
            if g == 0:
                hidden[...] = hidden[...] + mxu(mix, jnp.where(of_shift, 0, down), NN)
            else:
                column = (None, 1, 2, 0, 3)[g] * own
                out = (None, k_ref, v_ref, r_ref, g_ref)[g]
                out[...] = out[...] + mxu(mix, w_ref[:, column : column + own], NN)

    @pl.when((phase == 1) & (tile == pl.num_programs(1) - 1))
    def _():
        squash_ref[...] = squash_ref[...] + jnp.tanh(hidden[...])


def mixes_forward(unit, first, low_at, vec, own):
    rows, width = unit.shape
    tiles = width // TILE
    block = low_at // LOW
    across = lambda r: pl.BlockSpec((r, TILE), lambda p, n: (0, n))
    late = pl.BlockSpec((rows, TILE), lambda p, n: (0, n * p))
    whole = lambda columns: pl.BlockSpec((rows, columns), lambda p, n: (0, 0))
    kept = lambda columns, dtype: jax.ShapeDtypeStruct((rows, columns), dtype)
    return pl.pallas_call(
        mixes_forward_kernel,
        grid=(2, tiles),
        in_specs=[
            across(rows),
            pl.BlockSpec((TILE, 4 * own), lambda p, n: (n * p, 0)),
            pl.BlockSpec((TILE, LOW), lambda p, n: (n, block)),
            pl.BlockSpec((TILE, LOW), lambda p, n: (n, block + 1)),
            across(vec.shape[0]),
        ],
        out_specs=[late] * 6 + [whole(LOW)] + [whole(own)] * 4,
        out_shape=[kept(width, jnp.bfloat16)] * 5
        + [kept(width, jnp.float32), kept(LOW, jnp.float32)]
        + [pltpu.HBM((rows, own), jnp.float32)] * 4,
        scratch_shapes=[pltpu.VMEM((rows, LOW), jnp.float32), pltpu.VMEM((5, rows, LOW), jnp.bfloat16)],
        compiler_params=pltpu.CompilerParams(
            dimension_semantics=("arbitrary", "arbitrary"), vmem_limit_bytes=54 * 2**20
        ),
        cost_estimate=SOON,
        name="mixes_forward",
    )(unit, first, first, first, vec)


def mixes_back_kernel(
    gk_ref, gv_ref, gr_ref, gg_ref, gd_ref, w_ref, down_ref, up_ref, vec_ref, squash_ref, normed_ref,
    mix_ref, sums_ref, out_ref, small_ref,
    g_shift, g_norm, g_squash, g_hidden, g_up, g_sums, grouped, turned,
):
    phase, tile = pl.program_id(0), pl.program_id(1)
    rows = squash_ref.shape[0]
    own = gk_ref.shape[1]
    normed = normed_ref[...]
    row = iota2(normed.shape, 0)
    shifted = jnp.where(row == 0, 0.0, pltpu.roll(normed, 1, 0)) - normed
    squash = squash_ref[...]
    vec = vec_ref[...]

    @pl.when((phase == 0) & (tile == 0))
    def _():
        g_squash[...] = jnp.zeros_like(g_squash)
        group = lane_group(squash.shape)
        for g in range(5):
            grouped[g] = jnp.where(group == g, squash, 0.0).astype(jnp.bfloat16)
        turned[...] = squash.astype(jnp.bfloat16).T

    @pl.when(phase == 0)
    def _():
        up = up_ref[...]
        group_wide = lane_group(up.shape)
        total_shift = jnp.zeros((rows, TILE), jnp.float32)
        total_norm = jnp.zeros((rows, TILE), jnp.float32)
        add_squash = jnp.zeros((rows, LOW), jnp.float32)
        sums = []
        for g in range(5):
            if g == 0:
                part = mxu(gd_ref[...], down_ref[...], NT)
            else:
                column = (None, 1, 2, 0, 3)[g] * own
                grad = (None, gk_ref, gv_ref, gr_ref, gg_ref)[g]
                part = mxu(grad[...], w_ref[:, column : column + own], NT)
            coeff = vec[3 + g : 4 + g] + mxu(grouped[g], up, NT)
            times = part * shifted
            times_low = times.astype(jnp.bfloat16)
            sums.append(jnp.sum(times, axis=0, keepdims=True))
            total_shift = total_shift + part * coeff
            total_norm = total_norm + part
            add_squash = add_squash + mxu(times_low, jnp.where(group_wide == g, up, 0), NN)
            lanes = slice(g * SHIFT_RANK, (g + 1) * SHIFT_RANK)
            g_up[tile, lanes] = mxu(turned[lanes], times_low, NN)
        g_shift[tile] = total_shift
        g_norm[tile] = total_norm
        g_squash[...] = g_squash[...] + add_squash
        g_sums[tile] = jnp.concatenate(sums + [jnp.zeros((3, TILE), jnp.float32)], axis=0)

    @pl.when((phase == 1) & (tile == 0))
    def _():
        g_hidden[...] = (g_squash[...] * (1.0 - squash * squash)).astype(jnp.bfloat16)

    @pl.when(phase == 1)
    def _():
        blend = vec[2:3]
        part = mxu(g_hidden[...], down_ref[...], NT)
        total_shift = g_shift[tile] + part * blend
        total = g_norm[tile] + part - total_shift
        total = total + jnp.where(row == rows - 1, 0.0, pltpu.roll(total_shift, rows - 1, 0))
        out_ref[...] = total.astype(jnp.bfloat16)
        unit = (normed - vec[1:2]) / vec[0:1]
        head = [
            jnp.sum(total * unit, axis=0, keepdims=True),
            jnp.sum(total, axis=0, keepdims=True),
            jnp.sum(part * shifted, axis=0, keepdims=True),
        ]
        sums = jnp.concatenate(head + [g_sums[tile][:5], sums_ref[...]], axis=0)
        shape = (sums.shape[0], LOW)
        behind = jnp.where(iota2(shape, 1) == LANES + iota2(shape, 0), 1.0, 0.0)
        small_ref[:, :LOW] = (
            mxu(normed + shifted * blend, g_hidden[...], TN) + mxu(mix_ref[...], gd_ref[...], TN)
        ).astype(jnp.bfloat16)
        small_ref[:, LOW:] = mxu(sums, behind, TN).astype(jnp.bfloat16)
        small_ref[:, LOW : LOW + SHIFT_LANES] = g_up[tile].T.astype(jnp.bfloat16)


def mixes_back(g_key, g_val, g_recept, g_gate, g_decay, first, low_at, vec, squash, normed, mix, sums):
    rows, width = normed.shape
    own = g_key.shape[1]
    tiles = width // TILE
    block = low_at // LOW
    whole = lambda a: pl.BlockSpec(a.shape, lambda p, n: (0, 0))
    across = lambda r: pl.BlockSpec((r, TILE), lambda p, n: (0, n))
    late = lambda r: pl.BlockSpec((r, TILE), lambda p, n: (0, n * p))
    early = lambda p, n: n * (1 - p) + (tiles - 1) * p
    return pl.pallas_call(
        mixes_back_kernel,
        grid=(2, tiles),
        in_specs=[whole(g_key)] * 4
        + [
            whole(g_decay),
            pl.BlockSpec((TILE, 4 * own), lambda p, n: (early(p, n), 0)),
            pl.BlockSpec((TILE, LOW), lambda p, n: (n, block)),
            pl.BlockSpec((TILE, LOW), lambda p, n: (early(p, n), block + 1)),
            across(vec.shape[0]),
            whole(squash),
            across(rows),
            late(rows),
            late(sums.shape[0]),
        ],
        out_specs=[late(rows), pl.BlockSpec((TILE, 2 * LOW), lambda p, n: (n * p, 0))],
        out_shape=[
            jax.ShapeDtypeStruct((rows, width), jnp.bfloat16),
            jax.ShapeDtypeStruct((width, 2 * LOW), jnp.bfloat16),
        ],
        scratch_shapes=[
            pltpu.VMEM((tiles, rows, TILE), jnp.float32),
            pltpu.VMEM((tiles, rows, TILE), jnp.float32),
            pltpu.VMEM((rows, LOW), jnp.float32),
            pltpu.VMEM((rows, LOW), jnp.bfloat16),
            pltpu.VMEM((tiles, SHIFT_LANES, TILE), jnp.float32),
            pltpu.VMEM((tiles, 8, TILE), jnp.float32),
            pltpu.VMEM((5, rows, LOW), jnp.bfloat16),
            pltpu.VMEM((LOW, rows), jnp.bfloat16),
        ],
        compiler_params=pltpu.CompilerParams(
            dimension_semantics=("arbitrary", "arbitrary"), vmem_limit_bytes=56 * 2**20
        ),
        cost_estimate=SOON,
        name="mixes_back",
    )(g_key, g_val, g_recept, g_gate, g_decay, first, first, first, vec, squash, normed, mix, sums)


def shards(
    inputs,
    cotangent,
    states,
    vectors,
    time_mix_weight,
    output_weight,
    channel_receptance_weight,
    rank_down_weight,
    rank_up_weight,
    channel_key_weight,
    channel_value_weight,
):
    token_rows, width = inputs.shape
    seg_count = lax.axis_size("seg")
    own_width = time_mix_weight.shape[2]
    hidden = channel_key_weight.shape[1]
    local_heads = own_width // GROUP_DIMENSION
    col_start = lax.axis_index("span") * own_width
    position = lax.axis_index("span") * token_rows

    x_seg = span_gather(inputs).astype(jnp.float32)
    grad_columns = split_columns(cotangent).astype(jnp.float32)
    def blank(count):
        return jnp.zeros((token_rows // 8, count), jnp.bfloat16)

    small_rows = jnp.concatenate(
        [rank_down_weight, blank(LOW - LANES), rank_up_weight.T, vectors.T, blank(LOW - LANES - 16)], axis=1
    )
    span_rows = gather_and_split(small_rows, channel_receptance_weight)
    weights = both_planes(lambda proj: [proj[g] for g in range(4)], time_mix_weight)
    small_pair = both_planes(lambda rows: [rows], span_rows[:, own_width:])
    late_pairs = [fill_pair(rows[None])[0] for rows in (output_weight.T, span_rows[:, :own_width])]
    first = plane_gather(jnp.concatenate([weights, small_pair] + late_pairs, axis=1))
    _, unit_seg, _ = norm_rows(x_seg, 1.0, 0.0)
    second_pair = both_planes(lambda key, value: [key, value.T], channel_key_weight, channel_value_weight)
    second_pair, unit_seg, grad_columns = lax.optimization_barrier((second_pair, unit_seg, grad_columns))
    second = plane_gather(second_pair)
    low_at = 4 * own_width
    late_at = low_at + 2 * LOW

    def late_rows(at):
        pairs = first[:, at : at + own_width // 2].reshape(-1, 2 * (width // seg_count), own_width // 2)
        return from_pair(pairs)

    out_half, recept_half = late_rows(late_at), late_rows(late_at + own_width // 2)
    late_got = swap_high(jnp.concatenate([out_half, recept_half], axis=2))
    out_got, recept_got = late_got[:, :, :own_width], late_got[:, :, own_width:]
    up_at = low_at + LOW
    vec = first[:, up_at + LANES : up_at + LANES + 16].T.astype(jnp.float32)

    def own_cols(line):
        return lax.dynamic_slice_in_dim(line, col_start, own_width, line.ndim - 1)

    def own_rows(values):
        return lax.dynamic_slice_in_dim(values, position, token_rows, 0)

    x_in = inputs.astype(jnp.float32)
    *mixes, normed, squash, recept, key_proj, val_proj, gate_pre = mixes_forward(
        unit_seg, first, low_at, vec, own_width
    )
    lane = lax.broadcasted_iota(jnp.int32, squash.shape, 1)
    of_decay = (lane >= SHIFT_LANES) & (lane < LANES)
    decay_low = jnp.where(of_decay, squash, 0.0).astype(jnp.bfloat16)
    up_own = lax.dynamic_slice(first, (col_start, up_at), (own_width, LOW))
    head_vec = jnp.concatenate([own_cols(vec[8:12]), jnp.zeros((4, own_width), jnp.float32)], axis=0)
    first_state = jnp.transpose(states[0], (2, 0, 1)).reshape(GROUP_DIMENSION, own_width)
    out_w = other_plane(out_half, out_got)
    heads_in = (recept, key_proj, val_proj, gate_pre, decay_low, up_own, head_vec)
    mixed, wkv, held = wkv_forward(*heads_in, first_state)
    recept_w = other_plane(recept_half, recept_got)
    resid = x_in + span_reduce(backward_product(mixed, out_w).astype(jnp.bfloat16))

    normed_two, unit_two, rstd_two = norm_rows(resid, vec[12], vec[13])
    n2 = span_gather(normed_two.astype(jnp.bfloat16)).astype(jnp.float32)
    shifted_two = prior_rows(n2) - n2
    key_in = (n2 + shifted_two * vec[14]).astype(jnp.bfloat16)
    rec_in = (n2 + shifted_two * vec[15]).astype(jnp.bfloat16)
    rec_gate = jax.nn.sigmoid(product_lower(rec_in, recept_w))
    g_value = (grad_columns * rec_gate).astype(jnp.bfloat16)
    g_value, second = lax.optimization_barrier((g_value, second))
    g_value_all = span_gather(g_value, 1)
    key_w, value_w = second[:, :hidden], second[:, hidden:]
    hidden_two = product_lower(key_in, key_w)
    active = jax.nn.relu(hidden_two)
    squared = (active * active).astype(jnp.bfloat16)
    active = active.astype(jnp.bfloat16)

    low = lax.axis_index("span") // 2

    def value_columns(which):
        weights = lax.dynamic_slice(second, (which * (width // 2), hidden), (width // 2, hidden))
        return core_reduce(backward_product(squared, weights).astype(jnp.bfloat16))

    far, near = value_columns(1 - low), value_columns(low)
    far, g_value_all = lax.optimization_barrier((far.astype(jnp.bfloat16), g_value_all))
    far = swap_low(far)
    cm_total = 2 * hidden
    g_hid = (product_lower(g_value_all, value_w) * 2.0 * active.astype(jnp.float32)).astype(jnp.bfloat16)
    g_value_all, g_hid = lax.optimization_barrier((g_value_all, g_hid))
    cm_part = grad_into(g_value_all, squared, cm_total, hidden)
    far, near, cm_part = lax.optimization_barrier((far, near, cm_part))
    cm_part = grad_into(key_in, g_hid, cm_total, 0, cm_part)
    cm_part, g_hid = lax.optimization_barrier((cm_part, g_hid))
    cm_pair = plane_scatter(cm_part)
    value_out = near + far.astype(jnp.float32)
    gated = (rec_gate * value_out).astype(jnp.bfloat16)
    g_rec = (grad_columns * value_out * rec_gate * (1.0 - rec_gate)).astype(jnp.bfloat16)
    g_key_in = backward_product(g_hid, key_w)
    g_rec_in = backward_product(g_rec, recept_w)
    vec_fourteen = jnp.sum(g_key_in * shifted_two, axis=0)
    vec_fifteen = jnp.sum(g_rec_in * shifted_two, axis=0)
    g_shift_two = g_key_in * vec[14] + g_rec_in * vec[15]
    g_n2_part = g_key_in + g_rec_in - g_shift_two + next_rows(g_shift_two)
    g_n2 = span_reduce(g_n2_part.astype(jnp.bfloat16))
    rec_part = grad_into(rec_in, g_rec, own_width, 0)
    g_n2, rec_part = lax.optimization_barrier((g_n2, rec_part))
    vec_twelve = jnp.sum(g_n2 * unit_two, axis=0)
    vec_thirteen = jnp.sum(g_n2, axis=0)
    g_resid = cotangent.astype(jnp.float32) + norm_back(g_n2, unit_two, rstd_two, vec[12])

    g_att = span_gather(g_resid.astype(jnp.bfloat16))
    rec_part = rec_part.reshape(seg_count // 2, 2, width // seg_count, own_width)
    rec_mine, rec_send = in_order(rec_part[:, 0], rec_part[:, 1], lax.axis_index("seg") % 2 == 1)
    g_att, gated, rec_send = lax.optimization_barrier((g_att, gated, rec_send))
    rec_got = swap_high(rec_send)
    gated_rows = join_columns(gated)
    g_mixed = product_lower(g_att, out_w)
    g_recept, g_key, g_val, g_gate, g_ww, head_sums, g_first = wkv_backward(
        *heads_in, wkv, held, g_mixed
    )
    state_grad = jnp.transpose(
        g_first.reshape(GROUP_DIMENSION, local_heads, GROUP_DIMENSION), (1, 2, 0)
    )[None]
    tm_total = 5 * own_width + own_width // 2
    tm_part = grads_side_by_side(
        (g_att, mixes[3], mixes[1], mixes[2], mixes[4]), (mixed, g_recept, g_key, g_val, g_gate), tm_total
    )
    rec_got, g_ww = lax.optimization_barrier((rec_got, g_ww))
    rec_sum = (rec_mine.astype(jnp.float32) + rec_got.astype(jnp.float32)).astype(jnp.bfloat16)
    tm_part = lax.dynamic_update_slice(
        tm_part, fill_pair(rec_sum).reshape(width, own_width // 2), (0, 5 * own_width)
    )
    tm_part, cm_pair, gated_rows = lax.optimization_barrier((tm_part, cm_pair, gated_rows))
    output = (resid + gated_rows.astype(jnp.float32)).astype(jnp.bfloat16)
    tm_pair = plane_scatter(tm_part)
    g_key, g_ww, cm_pair = lax.optimization_barrier((g_key, g_ww, cm_pair))

    g_decay_hidden = jnp.where(
        of_decay, product_lower(g_ww, up_own) * (1.0 - squash * squash), 0.0
    ).astype(jnp.bfloat16)
    up_decay_grad = outer_sum(g_ww, decay_low)
    other_sums = jnp.concatenate(
        [
            lax.dynamic_update_slice_in_dim(jnp.zeros((4, width), jnp.float32), head_sums[:4], col_start, 1),
            jnp.stack([vec_twelve, vec_thirteen, vec_fourteen, vec_fifteen]),
        ],
        axis=0,
    )
    g_normed, small_part = mixes_back(
        g_key, g_val, g_recept, g_gate, g_decay_hidden, first, low_at, vec, squash, normed, mixes[0], other_sums
    )
    own_part = lax.dynamic_slice(small_part, (col_start, LOW), (own_width, LOW))
    small_part = lax.dynamic_update_slice(
        small_part, (own_part.astype(jnp.float32) + up_decay_grad).astype(jnp.bfloat16), (col_start, LOW)
    )
    small, g_n1, cm_grad = reduce_small(small_part, over_cores(g_normed), cm_pair)
    rec_own = from_pair(tm_pair[None, :, 5 * own_width :])[0]
    tm_grad = finish_scatter(*plane_halves(tm_pair[:, : 5 * own_width]))
    _, unit_own, rstd_own = norm_rows(x_in, vec[0], vec[1])
    x_grad = g_resid + norm_back(g_n1, unit_own, rstd_own, vec[0])
    down_grad = small[:, :LANES]
    up_grad = small[:, LOW : LOW + LANES].T
    vec_grad = small[:, LOW + LANES : LOW + LANES + 16].T
    rec_grad = join_columns(rec_own).astype(jnp.float32)
    value_grad = cm_grad[:, hidden:].T
    key_grad = cm_grad[:, :hidden]
    out_grad = tm_grad[:, :own_width].T
    proj_grad = jnp.moveaxis(tm_grad[:, own_width : 5 * own_width].reshape(-1, 4, own_width), 1, 0)
    return (
        output,
        x_grad,
        state_grad,
        vec_grad,
        proj_grad,
        out_grad,
        rec_grad,
        down_grad,
        up_grad,
        key_grad,
        value_grad,
    )


def solution(mesh):
    rows, columns = P(ALL, None), P(None, ALL)
    state = P("seg", "span", None, None)
    time_mix = P(None, "seg", "span")
    turned, straight = P("span", "seg"), P("seg", "span")
    return jax.shard_map(
        shards,
        mesh=mesh,
        in_specs=(
            rows, rows, state, columns, time_mix, turned, rows, rows, columns, straight, turned
        ),
        out_specs=(
            rows, rows, state, columns, time_mix, turned, rows, rows, columns, straight, turned
        ),
        check_vma=False,
    )
```

```python
import jax
import jax.numpy as jnp
from jax import lax
from jax.experimental import pallas as pl
from jax.experimental.pallas import tpu as pltpu
from jax.experimental.layout import Layout, with_layout_constraint
from jax.sharding import PartitionSpec as P

GROUP_DIMENSION = 64
SHIFT_RANK = 32
ALL = ("seg", "span")

maximal_accuracy = lax.Precision.HIGHEST
ln_eps = 1e-05
gn_eps = 0.00064


def swap(block, bit):
    count = lax.axis_size("seg") * lax.axis_size("span")
    return lax.ppermute(block, ALL, [(i, i ^ bit) for i in range(count)])


def swap_core(block):
    return swap(block, 1)


def swap_low(block):
    return swap(block, 2)


def swap_high(block):
    return swap(block, 4)


def plane_groups():
    half = lax.axis_size("seg") // 2
    return [[2 * j + h for j in range(half)] for h in range(2)]


def in_order(own, other, second):
    return jnp.where(second, other, own), jnp.where(second, own, other)


def span_gather(block, axis=0):
    place = lax.axis_index("span")
    low, core = place // 2, place % 2
    p0, p1 = in_order(block, swap_low(block), low == 1)
    q = swap_core(jnp.stack([p0, p1]))
    a0, a1 = in_order(p0, q[0], core == 1)
    b0, b1 = in_order(p1, q[1], core == 1)
    return jnp.concatenate([a0, a1, b0, b1], axis=axis)


def core_reduce(part):
    core = lax.axis_index("span") % 2
    half = part.shape[1] // 2
    keep, send = in_order(part[:, :half], part[:, half:], core == 1)
    return keep.astype(jnp.float32) + swap_core(send.astype(jnp.bfloat16)).astype(jnp.float32)


def over_cores(part):
    core = lax.axis_index("span") % 2
    b = part.reshape(2, 2, part.shape[0] // 4, part.shape[1])
    keep, send = in_order(b[:, 0], b[:, 1], core == 1)
    return keep.astype(jnp.float32) + swap_core(send.astype(jnp.bfloat16)).astype(jnp.float32)


def over_low(both):
    low = lax.axis_index("span") // 2
    mine, send = in_order(both[0], both[1], low == 1)
    return mine + swap_low(send.astype(jnp.bfloat16)).astype(jnp.float32)


def span_reduce(part):
    return over_low(over_cores(part))


def fill_pair(rows):
    half = rows.shape[2] // 2
    return jnp.concatenate([rows[:, :, :half], rows[:, :, half:]], axis=1)


def from_pair(pairs):
    half = pairs.shape[1] // 2
    return jnp.concatenate([pairs[:, :half], pairs[:, half:]], axis=2)


def other_plane(rows, got):
    high = lax.axis_index("seg") % 2
    return jnp.stack(in_order(rows, got, high == 1), axis=1).reshape(-1, rows.shape[2])


def both_planes(laid, *blocks):
    high = lax.axis_index("seg") % 2
    own, other = (
        jnp.concatenate(laid(*got), axis=1) for got in (blocks, [swap_high(block) for block in blocks])
    )
    return jnp.concatenate(in_order(own, other, high == 1), axis=0)


def plane_gather(pair):
    whole = lax.all_gather(
        pair,
        "seg",
        axis=0,
        tiled=True,
        axis_index_groups=plane_groups(),
    )
    return with_layout_constraint(whole, Layout(major_to_minor=(0, 1)))


def plane_scatter(part):
    return lax.psum_scatter(
        part, "seg", scatter_dimension=0, tiled=True, axis_index_groups=plane_groups()
    )


def plane_halves(pair):
    high = lax.axis_index("seg") % 2
    rows = pair.shape[0] // 2
    return in_order(pair[:rows], pair[rows:], high == 1)


def finish_scatter(mine, send):
    return mine.astype(jnp.float32) + swap_high(send).astype(jnp.float32)


def gather_and_split(small, wide):
    place = lax.axis_index("span")
    n = wide.shape[1] // 4
    messages = [
        jnp.concatenate([lax.dynamic_slice_in_dim(wide, (place ^ bit) * n, n, 1), small], axis=1)
        for bit in range(4)
    ]
    pieces = [m if bit == 0 else swap(m, bit) for bit, m in enumerate(messages)]
    result = jnp.zeros((4, *messages[0].shape), small.dtype)
    for bit, piece in enumerate(pieces):
        result = lax.dynamic_update_index_in_dim(result, piece, place ^ bit, 0)
    return result.reshape(4 * small.shape[0], -1)


def split_columns(block):
    place = lax.axis_index("span")
    n = block.shape[1] // 4

    def columns(at):
        return lax.dynamic_slice_in_dim(block, at * n, n, 1)

    pieces = [columns(place)] + [swap(columns(place ^ bit), bit) for bit in (1, 2, 3)]
    result = jnp.zeros((4, block.shape[0], n), block.dtype)
    for bit, piece in enumerate(pieces):
        result = lax.dynamic_update_index_in_dim(result, piece, place ^ bit, 0)
    return result.reshape(4 * block.shape[0], n)


def join_columns(block):
    place = lax.axis_index("span")
    r, n = block.shape[0] // 4, block.shape[1]

    def rows(at):
        return lax.dynamic_slice_in_dim(block, at * r, r, 0)

    result = jnp.zeros((r, 4 * n), block.dtype)
    for bit in range(4):
        piece = rows(place ^ bit)
        if bit:
            piece = swap(piece, bit)
        result = lax.dynamic_update_slice_in_dim(result, piece, (place ^ bit) * n, 1)
    return result


def product_lower(left_arg, right_arg):
    return jnp.dot(left_arg, right_arg, preferred_element_type=jnp.float32)


def outer_sum(left_arg, right_arg):
    return jnp.einsum("td,te->de", left_arg, right_arg, preferred_element_type=jnp.float32)


def backward_product(gradient, weights):
    return jnp.einsum("te,de->td", gradient, weights, preferred_element_type=jnp.float32)


def norm_rows(values, gain_vec, offset):
    centre = values - jnp.mean(values, -1, keepdims=True)
    row_rstd = lax.rsqrt(jnp.mean(centre * centre, -1, keepdims=True) + ln_eps)
    unit_rows = centre * row_rstd
    return (unit_rows * gain_vec + offset, unit_rows, row_rstd)


def norm_back(gradient, unit_rows, row_rstd, gain_vec):
    scaled = gradient * gain_vec
    return row_rstd * (
        scaled
        - jnp.mean(scaled, -1, keepdims=True)
        - unit_rows * jnp.mean(scaled * unit_rows, -1, keepdims=True)
    )


def prior_rows(values):
    return jnp.concatenate([jnp.zeros_like(values[:1]), values[:-1]], axis=0)


def next_rows(values):
    return jnp.concatenate([values[1:], jnp.zeros_like(values[:1])], axis=0)


def reduce_small(part, both, pair):
    place, high = lax.axis_index("span"), lax.axis_index("seg") % 2
    planes = lax.axis_size("seg") // 2
    width = part.shape[1]
    b = part.reshape(planes, 2, 2, 2, -1, width)

    def summed(b, dim, bit, move):
        at0, at1 = (lax.index_in_dim(b, k, dim, keepdims=False) for k in (0, 1))
        mine, send = in_order(at0, at1, bit == 1)
        return mine.astype(jnp.float32) + move(send.astype(jnp.bfloat16)).astype(jnp.float32)

    b = summed(summed(b, 3, place % 2, swap_core), 2, place // 2, swap_low)
    b, both = lax.optimization_barrier((b, both))
    rows = over_low(both)
    b = summed(b, 1, high, swap_high).astype(jnp.bfloat16)
    b, pair = lax.optimization_barrier((b, pair))
    finished = finish_scatter(*plane_halves(pair))
    arrived = lax.all_to_all(
        b, "seg", split_axis=0, concat_axis=0, tiled=True, axis_index_groups=plane_groups()
    )
    return arrived.astype(jnp.float32).sum(axis=0), rows, finished


SOON = pl.CostEstimate(flops=2**20, bytes_accessed=2**16, transcendentals=0)

CHUNK = 64
PACK = 256


def mxu(a, b, contract):
    return lax.dot_general(
        a.astype(jnp.bfloat16),
        b.astype(jnp.bfloat16),
        (contract, ((), ())),
        preferred_element_type=jnp.float32,
    )


NN, NT, TN = ((1,), (0,)), ((1,), (1,)), ((0,), (0,))


def halves(values):
    high = values.astype(jnp.bfloat16)
    return high, (values - high.astype(jnp.float32)).astype(jnp.bfloat16)


def iota2(shape, dim):
    return lax.broadcasted_iota(jnp.int32, shape, dim)


def head_ones():
    shape = (PACK, PACK)
    same = (iota2(shape, 0) ^ iota2(shape, 1)) < GROUP_DIMENSION
    return jnp.where(same, 1.0, 0.0).astype(jnp.float32)


def spread(block, ones):
    return jnp.concatenate([block] * (PACK // CHUNK), axis=0) * ones


def fold(big, ones):
    kept = big * ones
    total = kept[:CHUNK]
    for h in range(1, PACK // CHUNK):
        total = total + kept[h * CHUNK : (h + 1) * CHUNK]
    return total


def head_sum(values, ones):
    high, rest = halves(values)
    return mxu(high, ones, NN) + mxu(rest, ones, NN)


def run_sum(which, values):
    high, rest = halves(values)
    return mxu(which, high, NN) + mxu(which, rest, NN)


def row_of(values, row):
    return values[row : row + 1]


def piece_factors(run, before):
    rows = iota2((CHUNK, PACK), 0)
    apart = rows ^ (iota2((CHUNK, PACK), 1) & (CHUNK - 1))
    levels = []
    for half in (32, 16, 8, 4, 2, 1):
        upper = (rows & half) != 0
        if half == 1:
            scale = jnp.ones_like(run)
        else:
            if half == 2:
                reference = run
                for row, shift in ((0, CHUNK - 1), (2, 1), (3, 2)):
                    reference = jnp.where((rows & 3) == row, pltpu.roll(run, shift, 0), reference)
            else:
                reference = jnp.broadcast_to(row_of(run, half - 1), run.shape)
                for start in range(2 * half, CHUNK, 2 * half):
                    here = jnp.broadcast_to(row_of(run, start + half - 1), run.shape)
                    reference = jnp.where(rows >= start, here, reference)
            scale = jnp.exp(jnp.minimum(jnp.where(upper, before - reference, reference - run), 0.0))
        pairs = (apart < 2 * half) & upper & ((apart & half) != 0)
        levels.append((jnp.where(upper, scale, 0.0), jnp.where(upper, 0.0, scale), pairs))
    return levels


NOTHING = -104.0


def lower_ones():
    return jnp.where(iota2((CHUNK, CHUNK), 0) >= iota2((CHUNK, CHUNK), 1), 1.0, 0.0).astype(jnp.float32)


def decay_of(low_ref, up_ref, par_ref):
    log_decay = -jnp.exp(par_ref[0:1] + mxu(low_ref[...], up_ref[...], NT))
    kept = jnp.maximum(log_decay, NOTHING)
    run = run_sum(lower_ones(), kept)
    return jnp.where(log_decay <= NOTHING, 0.0, log_decay), run, run - kept


def unit_heads(wkv, ones):
    centre = wkv - head_sum(wkv, ones) * (1.0 / GROUP_DIMENSION)
    rstd = lax.rsqrt(head_sum(centre * centre, ones) * (1.0 / GROUP_DIMENSION) + gn_eps)
    return centre * rstd, rstd


def lane_groups(refs, kinds):
    width = refs[0].shape[1]
    for g in range(width // PACK):
        lanes = pl.ds(g * PACK, PACK)
        part = {"c": lambda ref: ref.at[:, lanes], "r": lambda ref: ref.at[lanes], "s": lambda ref: ref.at[g]}
        yield [ref if kind == "w" else part[kind](ref) for ref, kind in zip(refs, kinds)]


def in_turns(*bodies):
    bodies = list(bodies)
    while bodies:
        bodies = [body for body in bodies if next(body, body) is not body]


def wkv_forward_kernel(*refs):
    groups = list(lane_groups(refs, "ccccwrcccccs"))
    ones = head_ones()

    @pl.when(pl.program_id(0) == 0)
    def _():
        for *_, first_ref, _, _, _, state in groups:
            state[...] = spread(first_ref[...], ones)

    in_turns(*(forward_heads(ones, *group) for group in groups))


def wkv_backward_kernel(*refs):
    groups = list(lane_groups(refs, "ccccwrccccccccccc" + "s"))
    ones = head_ones()

    @pl.when(pl.program_id(0) == 0)
    def _():
        for *_, sums_ref, _, state in groups:
            state[...] = jnp.zeros_like(state)
            sums_ref[...] = jnp.zeros_like(sums_ref)

    in_turns(*(backward_heads(ones, *group) for group in groups))

    @pl.when(pl.program_id(0) == pl.num_programs(0) - 1)
    def _():
        for *_, first_ref, state in groups:
            first_ref[...] = fold(state[...], ones)


def forward_heads(
    ones, r_ref, k_ref, v_ref, gate_ref, low_ref, up_ref, par_ref, first_ref, mixed_ref, wkv_ref, held_ref, state
):
    r, k, v = r_ref[...], k_ref[...], v_ref[...]
    _, run, before = decay_of(low_ref, up_ref, par_ref)
    yield
    held_ref[...] = fold(state[...], ones)
    score = jnp.zeros((CHUNK, PACK), jnp.float32)
    for to_row, to_prior, pairs in piece_factors(run, before):
        score = jnp.where(pairs, mxu(r * to_row, spread(k * to_prior, ones), NT), score)
        yield
    out = mxu(score, spread(v, ones), NN) + mxu(r * jnp.exp(before), state[...], NT)
    out = out + head_sum(r * par_ref[1:2] * k, ones) * v
    yield
    wkv_ref[...] = out
    last = row_of(run, CHUNK - 1)
    state[...] = jnp.exp(last) * state[...] + mxu(v, k * jnp.exp(last - run), TN) * ones
    yield
    unit, _ = unit_heads(out, ones)
    yield
    gate = gate_ref[...]
    mixed_ref[...] = ((unit * par_ref[2:3] + par_ref[3:4]) * gate * jax.nn.sigmoid(gate)).astype(jnp.bfloat16)


def wkv_forward(r, k, v, gate, low, up, par, first):
    rows, columns = r.shape
    chunks = rows // CHUNK
    block = pl.BlockSpec((CHUNK, columns), lambda c: (c, 0))
    whole = lambda a: pl.BlockSpec(a.shape, lambda c: (0, 0))
    return pl.pallas_call(
        wkv_forward_kernel,
        grid=(chunks,),
        in_specs=[block] * 4
        + [
            pl.BlockSpec((CHUNK, low.shape[1]), lambda c: (c, 0)),
            whole(up),
            whole(par),
            whole(first),
        ],
        out_specs=[block, block, block],
        out_shape=[
            jax.ShapeDtypeStruct((rows, columns), jnp.bfloat16),
            jax.ShapeDtypeStruct((rows, columns), jnp.float32),
            jax.ShapeDtypeStruct((rows, columns), jnp.float32),
        ],
        scratch_shapes=[pltpu.VMEM((columns // PACK, PACK, PACK), jnp.float32)],
        compiler_params=pltpu.CompilerParams(
            dimension_semantics=("arbitrary",), vmem_limit_bytes=32 * 2**20
        ),
        cost_estimate=SOON,
        name="wkv_forward",
    )(*[pltpu.with_memory_space_constraint(x, pltpu.HBM) for x in (r, k, v, gate)], low, up, par, first)


def backward_heads(
    ones, r_ref, k_ref, v_ref, gate_ref, low_ref, up_ref, par_ref, wkv_ref, held_ref, gm_ref,
    gr_ref, gk_ref, gv_ref, gg_ref, gw_ref, sums_ref, first_ref, state,
):
    r, k, v, gate = r_ref[...], k_ref[...], v_ref[...], gate_ref[...]
    bonus, gain = par_ref[1:2], par_ref[2:3]

    def add_to(row, values):
        sums_ref[row : row + 1] = sums_ref[row : row + 1] + jnp.sum(values, axis=0, keepdims=True)

    unit, rstd = unit_heads(wkv_ref[...], ones)
    yield
    sig = jax.nn.sigmoid(gate)
    g_mixed = gm_ref[...].astype(jnp.float32)
    g_grouped = g_mixed * gate * sig
    grouped = unit * gain + par_ref[3:4]
    gg_ref[...] = (g_mixed * grouped * sig * (1.0 + gate * (1.0 - sig))).astype(jnp.bfloat16)
    add_to(2, g_grouped * unit)
    add_to(3, g_grouped)
    g_unit = g_grouped * gain
    scale = 1.0 / GROUP_DIMENSION
    g_out = rstd * (
        g_unit - head_sum(g_unit, ones) * scale - unit * (head_sum(g_unit * unit, ones) * scale)
    )

    yield
    log_decay, run, before = decay_of(low_ref, up_ref, par_ref)
    yield
    last = row_of(run, CHUNK - 1)
    start = spread(held_ref[...], ones)
    end_grad = state[...]
    v_wide = spread(v, ones)
    g_score = mxu(g_out, v_wide, NT)
    score = jnp.zeros((CHUNK, PACK), jnp.float32)
    from_start = jnp.exp(before)
    g_r = from_start * mxu(g_out, start, NN)
    g_before = r * g_r
    to_end = jnp.exp(last - run)
    g_end = to_end * mxu(v, end_grad, NN)
    g_k = g_end
    g_after = k * g_end
    for to_row, to_prior, pairs in piece_factors(run, before):
        r_level = (r * to_row).astype(jnp.bfloat16)
        k_rows = (k * to_prior).astype(jnp.bfloat16)
        k_level = spread(k_rows.astype(jnp.float32), ones).astype(jnp.bfloat16)
        score = jnp.where(pairs, mxu(r_level, k_level, NT), score)
        g_level = jnp.where(pairs, g_score, 0.0).astype(jnp.bfloat16)
        g_rows = mxu(g_level, k_level, NN)
        g_prior = fold(mxu(g_level, r_level, TN), ones)
        g_r = g_r + to_row * g_rows
        g_k = g_k + to_prior * g_prior
        g_before = g_before + r_level.astype(jnp.float32) * g_rows
        g_after = g_after + k_rows.astype(jnp.float32) * g_prior
        yield
    g_v = fold(mxu(score, g_out, TN), ones) + mxu(k * to_end, end_grad, NT)
    g_run = g_before - g_after
    g_last = jnp.sum(k * g_end, axis=0, keepdims=True) + jnp.exp(last) * jnp.sum(
        start * end_grad, axis=0, keepdims=True
    )
    upper = jnp.where(iota2((CHUNK, CHUNK), 0) <= iota2((CHUNK, CHUNK), 1), 1.0, 0.0).astype(jnp.float32)
    g_decay = run_sum(upper, g_run) - g_before + g_last
    yield
    g_expo = g_decay * log_decay
    gw_ref[...] = g_expo.astype(jnp.bfloat16)
    add_to(0, g_expo)
    g_diag = head_sum(g_out * v, ones)
    add_to(1, r * k * g_diag)
    gr_ref[...] = (g_r + bonus * k * g_diag).astype(jnp.bfloat16)
    gk_ref[...] = (g_k + bonus * r * g_diag).astype(jnp.bfloat16)
    gv_ref[...] = (g_v + head_sum(r * bonus * k, ones) * g_out).astype(jnp.bfloat16)
    state[...] = jnp.exp(last) * end_grad + mxu(g_out, r * from_start, TN) * ones


def wkv_backward(r, k, v, gate, low, up, par, wkv, held, g_mixed):
    rows, columns = r.shape
    chunks = rows // CHUNK
    block = pl.BlockSpec((CHUNK, columns), lambda c: (chunks - 1 - c, 0))
    whole = lambda a: pl.BlockSpec(a.shape, lambda c: (0, 0))
    of_all = lambda n: pl.BlockSpec((n, columns), lambda c: (0, 0))
    low_type = jax.ShapeDtypeStruct((rows, columns), jnp.bfloat16)
    return pl.pallas_call(
        wkv_backward_kernel,
        grid=(chunks,),
        in_specs=[block] * 4
        + [
            pl.BlockSpec((CHUNK, low.shape[1]), lambda c: (chunks - 1 - c, 0)),
            whole(up),
            whole(par),
            block,
            block,
            block,
        ],
        out_specs=[block] * 5 + [of_all(8), of_all(GROUP_DIMENSION)],
        out_shape=[low_type] * 5
        + [
            jax.ShapeDtypeStruct((8, columns), jnp.float32),
            jax.ShapeDtypeStruct((GROUP_DIMENSION, columns), jnp.float32),
        ],
        scratch_shapes=[pltpu.VMEM((columns // PACK, PACK, PACK), jnp.float32)],
        compiler_params=pltpu.CompilerParams(
            dimension_semantics=("arbitrary",), vmem_limit_bytes=32 * 2**20
        ),
        cost_estimate=SOON,
        name="wkv_backward",
    )(r, k, v, gate, low, up, par, wkv, held, g_mixed)


GRAD_ROWS, GRAD_COLUMNS = 512, 256


def grad_kernel(left_ref, right_ref, *rest):
    out_ref = rest[-1]
    turned = left_ref[...].T
    for at in range(0, out_ref.shape[1], GRAD_COLUMNS):
        columns = slice(at, at + GRAD_COLUMNS)
        out_ref[:, columns] = mxu(turned, right_ref[:, columns], NN).astype(jnp.bfloat16)


def grad_into(left, right, total, at, into=None):
    rows, width = left.shape
    columns = right.shape[1]
    shift = at // columns
    specs = [
        pl.BlockSpec((rows, GRAD_ROWS), lambda i: (0, i)),
        pl.BlockSpec((rows, columns), lambda i: (0, 0)),
    ]
    operands = [left, right]
    alias = {}
    if into is not None:
        specs.append(pl.BlockSpec(memory_space=pltpu.HBM))
        operands.append(into)
        alias = {2: 0}
    return pl.pallas_call(
        grad_kernel,
        grid=(width // GRAD_ROWS,),
        in_specs=specs,
        out_specs=pl.BlockSpec((GRAD_ROWS, columns), lambda i: (i, shift)),
        out_shape=pltpu.HBM((width, total), jnp.bfloat16),
        input_output_aliases=alias,
        compiler_params=pltpu.CompilerParams(
            dimension_semantics=("arbitrary",), vmem_limit_bytes=32 * 2**20
        ),
        cost_estimate=SOON,
        name="weight_grad",
    )(*operands)


def grads_kernel(*refs):
    count = len(refs) // 2
    out_ref = refs[-1]
    for n in range(count):

        @pl.when(pl.program_id(0) == n)
        def _(left_ref=refs[n], right_ref=refs[count + n]):
            turned = left_ref[...].T
            for at in range(0, out_ref.shape[1], GRAD_COLUMNS):
                columns = slice(at, at + GRAD_COLUMNS)
                out_ref[:, columns] = mxu(turned, right_ref[:, columns], NN).astype(jnp.bfloat16)


def grads_side_by_side(lefts, rights, total):
    rows, width = lefts[0].shape
    columns = rights[0].shape[1]
    blocks = width // GRAD_ROWS

    def left_spec(n):
        return pl.BlockSpec(
            (rows, GRAD_ROWS),
            lambda p, i: (0, jnp.where(p == n, i, jnp.where(p < n, 0, blocks - 1))),
        )

    return pl.pallas_call(
        grads_kernel,
        grid=(len(lefts), blocks),
        in_specs=[left_spec(n) for n in range(len(lefts))]
        + [pl.BlockSpec((rows, columns), lambda p, i: (0, 0))] * len(rights),
        out_specs=pl.BlockSpec((GRAD_ROWS, columns), lambda p, i: (i, p)),
        out_shape=pltpu.HBM((width, total), jnp.bfloat16),
        compiler_params=pltpu.CompilerParams(
            dimension_semantics=("arbitrary", "arbitrary"), vmem_limit_bytes=32 * 2**20
        ),
        cost_estimate=SOON,
        name="time_mix_grads",
    )(*lefts, *rights)


LOW = 256
SHIFT_LANES = 5 * SHIFT_RANK
LANES = SHIFT_LANES + 64

TILE = 512


def vectors_kernel(up_ref, out_ref):
    turned = up_ref[...].astype(jnp.float32).T
    out_ref[...] = turned[LANES : LANES + 16]


def turn_vectors(first, up_at):
    width = first.shape[0]
    return pl.pallas_call(
        vectors_kernel,
        grid=(width // TILE,),
        in_specs=[pl.BlockSpec((TILE, LOW), lambda n: (n, up_at // LOW))],
        out_specs=pl.BlockSpec((16, TILE), lambda n: (0, n)),
        out_shape=jax.ShapeDtypeStruct((16, width), jnp.float32),
        compiler_params=pltpu.CompilerParams(dimension_semantics=("arbitrary",)),
        cost_estimate=SOON,
        name="turn_vectors",
    )(first)


def lane_group(shape):
    return lax.shift_right_logical(iota2(shape, 1), 5)


def mixes_forward_kernel(
    unit_ref, w_ref, down_ref, up_ref, vec_ref,
    m0_ref, m1_ref, m2_ref, m3_ref, m4_ref, normed_ref, squash_ref, r_ref, k_ref, v_ref, g_ref,
    hidden, grouped,
):
    phase, tile = pl.program_id(0), pl.program_id(1)
    rows = unit_ref.shape[0]
    own = r_ref.shape[1]
    vec = vec_ref[...]
    normed = unit_ref[...] * vec[0:1] + vec[1:2]
    row = iota2(normed.shape, 0)
    shifted = jnp.where(row == 0, 0.0, pltpu.roll(normed, 1, 0)) - normed
    down = down_ref[...]
    of_shift = iota2(down.shape, 1) < SHIFT_LANES

    @pl.when((phase == 0) & (tile == 0))
    def _():
        hidden[...] = jnp.zeros_like(hidden)

    @pl.when(phase == 0)
    def _():
        hidden[...] = hidden[...] + mxu(normed + shifted * vec[2:3], jnp.where(of_shift, down, 0), NN)

    @pl.when((phase == 1) & (tile == 0))
    def _():
        squash = jnp.tanh(hidden[...])
        squash_ref[...] = squash
        group = lane_group(squash.shape)
        for g in range(5):
            grouped[g] = jnp.where(group == g, squash, 0.0).astype(jnp.bfloat16)
        hidden[...] = jnp.zeros_like(hidden)
        for ref in (r_ref, k_ref, v_ref, g_ref):
            ref[...] = jnp.zeros_like(ref)

    @pl.when(phase == 1)
    def _():
        normed_ref[...] = normed
        up = up_ref[...]
        for g, mix_ref in enumerate((m0_ref, m1_ref, m2_ref, m3_ref, m4_ref)):
            mix = (normed + shifted * (vec[3 + g : 4 + g] + mxu(grouped[g], up, NT))).astype(jnp.bfloat16)
            mix_ref[...] = mix
            if g == 0:
                hidden[...] = hidden[...] + mxu(mix, jnp.where(of_shift, 0, down), NN)
            else:
                column = (None, 1, 2, 0, 3)[g] * own
                out = (None, k_ref, v_ref, r_ref, g_ref)[g]
                out[...] = out[...] + mxu(mix, w_ref[:, column : column + own], NN)

    @pl.when((phase == 1) & (tile == pl.num_programs(1) - 1))
    def _():
        squash_ref[...] = squash_ref[...] + jnp.tanh(hidden[...])


def mixes_forward(unit, first, low_at, vec, own):
    rows, width = unit.shape
    tiles = width // TILE
    block = low_at // LOW
    across = lambda r: pl.BlockSpec((r, TILE), lambda p, n: (0, n))
    late = pl.BlockSpec((rows, TILE), lambda p, n: (0, n * p))
    whole = lambda columns: pl.BlockSpec((rows, columns), lambda p, n: (0, 0))
    kept = lambda columns, dtype: jax.ShapeDtypeStruct((rows, columns), dtype)
    return pl.pallas_call(
        mixes_forward_kernel,
        grid=(2, tiles),
        in_specs=[
            across(rows),
            pl.BlockSpec((TILE, 4 * own), lambda p, n: (n * p, 0)),
            pl.BlockSpec((TILE, LOW), lambda p, n: (n, block)),
            pl.BlockSpec((TILE, LOW), lambda p, n: (n, block + 1)),
            across(vec.shape[0]),
        ],
        out_specs=[late] * 6 + [whole(LOW)] + [whole(own)] * 4,
        out_shape=[kept(width, jnp.bfloat16)] * 5
        + [kept(width, jnp.float32), kept(LOW, jnp.float32)]
        + [pltpu.HBM((rows, own), jnp.float32)] * 4,
        scratch_shapes=[pltpu.VMEM((rows, LOW), jnp.float32), pltpu.VMEM((5, rows, LOW), jnp.bfloat16)],
        compiler_params=pltpu.CompilerParams(
            dimension_semantics=("arbitrary", "arbitrary"), vmem_limit_bytes=54 * 2**20
        ),
        cost_estimate=SOON,
        name="mixes_forward",
    )(unit, first, first, first, vec)


def mixes_back_kernel(
    gk_ref, gv_ref, gr_ref, gg_ref, gd_ref, w_ref, down_ref, up_ref, vec_ref, squash_ref, normed_ref,
    mix_ref, sums_ref, out_ref, small_ref,
    g_shift, g_norm, g_squash, g_hidden, g_up, g_sums, grouped, turned,
):
    phase, tile = pl.program_id(0), pl.program_id(1)
    rows = squash_ref.shape[0]
    own = gk_ref.shape[1]
    normed = normed_ref[...]
    row = iota2(normed.shape, 0)
    shifted = jnp.where(row == 0, 0.0, pltpu.roll(normed, 1, 0)) - normed
    squash = squash_ref[...]
    vec = vec_ref[...]

    @pl.when((phase == 0) & (tile == 0))
    def _():
        g_squash[...] = jnp.zeros_like(g_squash)
        group = lane_group(squash.shape)
        for g in range(5):
            grouped[g] = jnp.where(group == g, squash, 0.0).astype(jnp.bfloat16)
        turned[...] = squash.astype(jnp.bfloat16).T

    @pl.when(phase == 0)
    def _():
        up = up_ref[...]
        group_wide = lane_group(up.shape)
        total_shift = jnp.zeros((rows, TILE), jnp.float32)
        total_norm = jnp.zeros((rows, TILE), jnp.float32)
        add_squash = jnp.zeros((rows, LOW), jnp.float32)
        sums = []
        for g in range(5):
            if g == 0:
                part = mxu(gd_ref[...], down_ref[...], NT)
            else:
                column = (None, 1, 2, 0, 3)[g] * own
                grad = (None, gk_ref, gv_ref, gr_ref, gg_ref)[g]
                part = mxu(grad[...], w_ref[:, column : column + own], NT)
            coeff = vec[3 + g : 4 + g] + mxu(grouped[g], up, NT)
            times = part * shifted
            times_low = times.astype(jnp.bfloat16)
            sums.append(jnp.sum(times, axis=0, keepdims=True))
            total_shift = total_shift + part * coeff
            total_norm = total_norm + part
            add_squash = add_squash + mxu(times_low, jnp.where(group_wide == g, up, 0), NN)
            lanes = slice(g * SHIFT_RANK, (g + 1) * SHIFT_RANK)
            g_up[tile, lanes] = mxu(turned[lanes], times_low, NN)
        g_shift[tile] = total_shift
        g_norm[tile] = total_norm
        g_squash[...] = g_squash[...] + add_squash
        g_sums[tile] = jnp.concatenate(sums + [jnp.zeros((3, TILE), jnp.float32)], axis=0)

    @pl.when((phase == 1) & (tile == 0))
    def _():
        g_hidden[...] = (g_squash[...] * (1.0 - squash * squash)).astype(jnp.bfloat16)

    @pl.when(phase == 1)
    def _():
        blend = vec[2:3]
        part = mxu(g_hidden[...], down_ref[...], NT)
        total_shift = g_shift[tile] + part * blend
        total = g_norm[tile] + part - total_shift
        total = total + jnp.where(row == rows - 1, 0.0, pltpu.roll(total_shift, rows - 1, 0))
        out_ref[...] = total.astype(jnp.bfloat16)
        unit = (normed - vec[1:2]) / vec[0:1]
        head = [
            jnp.sum(total * unit, axis=0, keepdims=True),
            jnp.sum(total, axis=0, keepdims=True),
            jnp.sum(part * shifted, axis=0, keepdims=True),
        ]
        sums = jnp.concatenate(head + [g_sums[tile][:5], sums_ref[...]], axis=0)
        shape = (sums.shape[0], LOW)
        behind = jnp.where(iota2(shape, 1) == LANES + iota2(shape, 0), 1.0, 0.0)
        small_ref[:, :LOW] = (
            mxu(normed + shifted * blend, g_hidden[...], TN) + mxu(mix_ref[...], gd_ref[...], TN)
        ).astype(jnp.bfloat16)
        small_ref[:, LOW:] = mxu(sums, behind, TN).astype(jnp.bfloat16)
        small_ref[:, LOW : LOW + SHIFT_LANES] = g_up[tile].T.astype(jnp.bfloat16)


def mixes_back(g_key, g_val, g_recept, g_gate, g_decay, first, low_at, vec, squash, normed, mix, sums):
    rows, width = normed.shape
    own = g_key.shape[1]
    tiles = width // TILE
    block = low_at // LOW
    whole = lambda a: pl.BlockSpec(a.shape, lambda p, n: (0, 0))
    across = lambda r: pl.BlockSpec((r, TILE), lambda p, n: (0, n))
    late = lambda r: pl.BlockSpec((r, TILE), lambda p, n: (0, n * p))
    early = lambda p, n: n * (1 - p) + (tiles - 1) * p
    return pl.pallas_call(
        mixes_back_kernel,
        grid=(2, tiles),
        in_specs=[whole(g_key)] * 4
        + [
            whole(g_decay),
            pl.BlockSpec((TILE, 4 * own), lambda p, n: (early(p, n), 0)),
            pl.BlockSpec((TILE, LOW), lambda p, n: (n, block)),
            pl.BlockSpec((TILE, LOW), lambda p, n: (early(p, n), block + 1)),
            across(vec.shape[0]),
            whole(squash),
            across(rows),
            late(rows),
            late(sums.shape[0]),
        ],
        out_specs=[late(rows), pl.BlockSpec((TILE, 2 * LOW), lambda p, n: (n * p, 0))],
        out_shape=[
            jax.ShapeDtypeStruct((rows, width), jnp.bfloat16),
            jax.ShapeDtypeStruct((width, 2 * LOW), jnp.bfloat16),
        ],
        scratch_shapes=[
            pltpu.VMEM((tiles, rows, TILE), jnp.float32),
            pltpu.VMEM((tiles, rows, TILE), jnp.float32),
            pltpu.VMEM((rows, LOW), jnp.float32),
            pltpu.VMEM((rows, LOW), jnp.bfloat16),
            pltpu.VMEM((tiles, SHIFT_LANES, TILE), jnp.float32),
            pltpu.VMEM((tiles, 8, TILE), jnp.float32),
            pltpu.VMEM((5, rows, LOW), jnp.bfloat16),
            pltpu.VMEM((LOW, rows), jnp.bfloat16),
        ],
        compiler_params=pltpu.CompilerParams(
            dimension_semantics=("arbitrary", "arbitrary"), vmem_limit_bytes=56 * 2**20
        ),
        cost_estimate=SOON,
        name="mixes_back",
    )(g_key, g_val, g_recept, g_gate, g_decay, first, first, first, vec, squash, normed, mix, sums)


def shards(
    inputs,
    cotangent,
    states,
    vectors,
    time_mix_weight,
    output_weight,
    channel_receptance_weight,
    rank_down_weight,
    rank_up_weight,
    channel_key_weight,
    channel_value_weight,
):
    token_rows, width = inputs.shape
    seg_count = lax.axis_size("seg")
    own_width = time_mix_weight.shape[2]
    hidden = channel_key_weight.shape[1]
    local_heads = own_width // GROUP_DIMENSION
    col_start = lax.axis_index("span") * own_width
    position = lax.axis_index("span") * token_rows

    x_seg = span_gather(inputs).astype(jnp.float32)
    grad_columns = split_columns(cotangent).astype(jnp.float32)
    def blank(count):
        return jnp.zeros((token_rows // 8, count), jnp.bfloat16)

    small_rows = jnp.concatenate(
        [rank_down_weight, blank(LOW - LANES), rank_up_weight.T, vectors.T, blank(LOW - LANES - 16)], axis=1
    )
    span_rows = gather_and_split(small_rows, channel_receptance_weight)
    weights = both_planes(lambda proj: [proj[g] for g in range(4)], time_mix_weight)
    small_pair = both_planes(lambda rows: [rows], span_rows[:, own_width:])
    late_pairs = [fill_pair(rows[None])[0] for rows in (output_weight.T, span_rows[:, :own_width])]
    first = plane_gather(jnp.concatenate([weights, small_pair] + late_pairs, axis=1))
    _, unit_seg, _ = norm_rows(x_seg, 1.0, 0.0)
    second_pair = both_planes(lambda key, value: [key, value.T], channel_key_weight, channel_value_weight)
    second_pair, unit_seg, grad_columns = lax.optimization_barrier((second_pair, unit_seg, grad_columns))
    second = plane_gather(second_pair)
    low_at = 4 * own_width
    late_at = low_at + 2 * LOW

    def late_rows(at):
        pairs = first[:, at : at + own_width // 2].reshape(-1, 2 * (width // seg_count), own_width // 2)
        return from_pair(pairs)

    out_half, recept_half = late_rows(late_at), late_rows(late_at + own_width // 2)
    late_got = swap_high(jnp.concatenate([out_half, recept_half], axis=2))
    out_got, recept_got = late_got[:, :, :own_width], late_got[:, :, own_width:]
    up_at = low_at + LOW
    vec = first[:, up_at + LANES : up_at + LANES + 16].T.astype(jnp.float32)

    def own_cols(line):
        return lax.dynamic_slice_in_dim(line, col_start, own_width, line.ndim - 1)

    def own_rows(values):
        return lax.dynamic_slice_in_dim(values, position, token_rows, 0)

    x_in = inputs.astype(jnp.float32)
    *mixes, normed, squash, recept, key_proj, val_proj, gate_pre = mixes_forward(
        unit_seg, first, low_at, vec, own_width
    )
    lane = lax.broadcasted_iota(jnp.int32, squash.shape, 1)
    of_decay = (lane >= SHIFT_LANES) & (lane < LANES)
    decay_low = jnp.where(of_decay, squash, 0.0).astype(jnp.bfloat16)
    up_own = lax.dynamic_slice(first, (col_start, up_at), (own_width, LOW))
    head_vec = jnp.concatenate([own_cols(vec[8:12]), jnp.zeros((4, own_width), jnp.float32)], axis=0)
    first_state = jnp.transpose(states[0], (2, 0, 1)).reshape(GROUP_DIMENSION, own_width)
    out_w = other_plane(out_half, out_got)
    heads_in = (recept, key_proj, val_proj, gate_pre, decay_low, up_own, head_vec)
    mixed, wkv, held = wkv_forward(*heads_in, first_state)
    recept_w = other_plane(recept_half, recept_got)
    resid = x_in + span_reduce(backward_product(mixed, out_w).astype(jnp.bfloat16))

    normed_two, unit_two, rstd_two = norm_rows(resid, vec[12], vec[13])
    n2 = span_gather(normed_two.astype(jnp.bfloat16)).astype(jnp.float32)
    shifted_two = prior_rows(n2) - n2
    key_in = (n2 + shifted_two * vec[14]).astype(jnp.bfloat16)
    rec_in = (n2 + shifted_two * vec[15]).astype(jnp.bfloat16)
    rec_gate = jax.nn.sigmoid(product_lower(rec_in, recept_w))
    g_value = (grad_columns * rec_gate).astype(jnp.bfloat16)
    g_value, second = lax.optimization_barrier((g_value, second))
    g_value_all = span_gather(g_value, 1)
    key_w, value_w = second[:, :hidden], second[:, hidden:]
    hidden_two = product_lower(key_in, key_w)
    active = jax.nn.relu(hidden_two)
    squared = (active * active).astype(jnp.bfloat16)
    active = active.astype(jnp.bfloat16)

    low = lax.axis_index("span") // 2

    def value_columns(which):
        weights = lax.dynamic_slice(second, (which * (width // 2), hidden), (width // 2, hidden))
        return core_reduce(backward_product(squared, weights).astype(jnp.bfloat16))

    far, near = value_columns(1 - low), value_columns(low)
    far, g_value_all = lax.optimization_barrier((far.astype(jnp.bfloat16), g_value_all))
    far = swap_low(far)
    cm_total = 2 * hidden
    g_hid = (product_lower(g_value_all, value_w) * 2.0 * active.astype(jnp.float32)).astype(jnp.bfloat16)
    g_value_all, g_hid = lax.optimization_barrier((g_value_all, g_hid))
    cm_part = grad_into(g_value_all, squared, cm_total, hidden)
    far, near, cm_part = lax.optimization_barrier((far, near, cm_part))
    cm_part = grad_into(key_in, g_hid, cm_total, 0, cm_part)
    cm_part, g_hid = lax.optimization_barrier((cm_part, g_hid))
    cm_pair = plane_scatter(cm_part)
    value_out = near + far.astype(jnp.float32)
    gated = (rec_gate * value_out).astype(jnp.bfloat16)
    g_rec = (grad_columns * value_out * rec_gate * (1.0 - rec_gate)).astype(jnp.bfloat16)
    g_key_in = backward_product(g_hid, key_w)
    g_rec_in = backward_product(g_rec, recept_w)
    vec_fourteen = jnp.sum(g_key_in * shifted_two, axis=0)
    vec_fifteen = jnp.sum(g_rec_in * shifted_two, axis=0)
    g_shift_two = g_key_in * vec[14] + g_rec_in * vec[15]
    g_n2_part = g_key_in + g_rec_in - g_shift_two + next_rows(g_shift_two)
    g_n2 = span_reduce(g_n2_part.astype(jnp.bfloat16))
    rec_part = grad_into(rec_in, g_rec, own_width, 0)
    g_n2, rec_part = lax.optimization_barrier((g_n2, rec_part))
    vec_twelve = jnp.sum(g_n2 * unit_two, axis=0)
    vec_thirteen = jnp.sum(g_n2, axis=0)
    g_resid = cotangent.astype(jnp.float32) + norm_back(g_n2, unit_two, rstd_two, vec[12])

    g_att = span_gather(g_resid.astype(jnp.bfloat16))
    rec_part = rec_part.reshape(seg_count // 2, 2, width // seg_count, own_width)
    rec_mine, rec_send = in_order(rec_part[:, 0], rec_part[:, 1], lax.axis_index("seg") % 2 == 1)
    g_att, gated, rec_send = lax.optimization_barrier((g_att, gated, rec_send))
    rec_got = swap_high(rec_send)
    gated_rows = join_columns(gated)
    g_mixed = product_lower(g_att, out_w)
    g_recept, g_key, g_val, g_gate, g_ww, head_sums, g_first = wkv_backward(
        *heads_in, wkv, held, g_mixed
    )
    state_grad = jnp.transpose(
        g_first.reshape(GROUP_DIMENSION, local_heads, GROUP_DIMENSION), (1, 2, 0)
    )[None]
    tm_total = 5 * own_width + own_width // 2
    tm_part = grads_side_by_side(
        (g_att, mixes[3], mixes[1], mixes[2], mixes[4]), (mixed, g_recept, g_key, g_val, g_gate), tm_total
    )
    rec_got, g_ww = lax.optimization_barrier((rec_got, g_ww))
    rec_sum = (rec_mine.astype(jnp.float32) + rec_got.astype(jnp.float32)).astype(jnp.bfloat16)
    tm_part = lax.dynamic_update_slice(
        tm_part, fill_pair(rec_sum).reshape(width, own_width // 2), (0, 5 * own_width)
    )
    tm_part, cm_pair, gated_rows = lax.optimization_barrier((tm_part, cm_pair, gated_rows))
    output = (resid + gated_rows.astype(jnp.float32)).astype(jnp.bfloat16)
    tm_pair = plane_scatter(tm_part)
    g_key, g_ww, cm_pair = lax.optimization_barrier((g_key, g_ww, cm_pair))

    g_decay_hidden = jnp.where(
        of_decay, product_lower(g_ww, up_own) * (1.0 - squash * squash), 0.0
    ).astype(jnp.bfloat16)
    up_decay_grad = outer_sum(g_ww, decay_low)
    other_sums = jnp.concatenate(
        [
            lax.dynamic_update_slice_in_dim(jnp.zeros((4, width), jnp.float32), head_sums[:4], col_start, 1),
            jnp.stack([vec_twelve, vec_thirteen, vec_fourteen, vec_fifteen]),
        ],
        axis=0,
    )
    g_normed, small_part = mixes_back(
        g_key, g_val, g_recept, g_gate, g_decay_hidden, first, low_at, vec, squash, normed, mixes[0], other_sums
    )
    own_part = lax.dynamic_slice(small_part, (col_start, LOW), (own_width, LOW))
    small_part = lax.dynamic_update_slice(
        small_part, (own_part.astype(jnp.float32) + up_decay_grad).astype(jnp.bfloat16), (col_start, LOW)
    )
    small, g_n1, cm_grad = reduce_small(small_part, over_cores(g_normed), cm_pair)
    rec_own = from_pair(tm_pair[None, :, 5 * own_width :])[0]
    tm_grad = finish_scatter(*plane_halves(tm_pair[:, : 5 * own_width]))
    _, unit_own, rstd_own = norm_rows(x_in, vec[0], vec[1])
    x_grad = g_resid + norm_back(g_n1, unit_own, rstd_own, vec[0])
    down_grad = small[:, :LANES]
    up_grad = small[:, LOW : LOW + LANES].T
    vec_grad = small[:, LOW + LANES : LOW + LANES + 16].T
    rec_grad = join_columns(rec_own).astype(jnp.float32)
    value_grad = cm_grad[:, hidden:].T
    key_grad = cm_grad[:, :hidden]
    out_grad = tm_grad[:, :own_width].T
    proj_grad = jnp.moveaxis(tm_grad[:, own_width : 5 * own_width].reshape(-1, 4, own_width), 1, 0)
    return (
        output,
        x_grad,
        state_grad,
        vec_grad,
        proj_grad,
        out_grad,
        rec_grad,
        down_grad,
        up_grad,
        key_grad,
        value_grad,
    )


def solution(mesh):
    rows, columns = P(ALL, None), P(None, ALL)
    state = P("seg", "span", None, None)
    time_mix = P(None, "seg", "span")
    turned, straight = P("span", "seg"), P("seg", "span")
    return jax.shard_map(
        shards,
        mesh=mesh,
        in_specs=(
            rows, rows, state, columns, time_mix, turned, rows, rows, columns, straight, turned
        ),
        out_specs=(
            rows, rows, state, columns, time_mix, turned, rows, rows, columns, straight, turned
        ),
        check_vma=False,
    )
```

```python
import jax
import jax.numpy as jnp
from jax import lax
from jax.experimental import pallas as pl
from jax.experimental.pallas import tpu as pltpu
from jax.experimental.layout import Layout, with_layout_constraint
from jax.sharding import PartitionSpec as P

GROUP_DIMENSION = 64
SHIFT_RANK = 32
ALL = ("seg", "span")

maximal_accuracy = lax.Precision.HIGHEST
ln_eps = 1e-05
gn_eps = 0.00064


def swap(block, bit):
    count = lax.axis_size("seg") * lax.axis_size("span")
    return lax.ppermute(block, ALL, [(i, i ^ bit) for i in range(count)])


def swap_core(block):
    return swap(block, 1)


def swap_low(block):
    return swap(block, 2)


def swap_high(block):
    return swap(block, 4)


def plane_groups():
    half = lax.axis_size("seg") // 2
    return [[2 * j + h for j in range(half)] for h in range(2)]


def in_order(own, other, second):
    return jnp.where(second, other, own), jnp.where(second, own, other)


def span_gather(block, axis=0):
    place = lax.axis_index("span")
    low, core = place // 2, place % 2
    p0, p1 = in_order(block, swap_low(block), low == 1)
    q = swap_core(jnp.stack([p0, p1]))
    a0, a1 = in_order(p0, q[0], core == 1)
    b0, b1 = in_order(p1, q[1], core == 1)
    return jnp.concatenate([a0, a1, b0, b1], axis=axis)


def core_reduce(part):
    core = lax.axis_index("span") % 2
    half = part.shape[1] // 2
    keep, send = in_order(part[:, :half], part[:, half:], core == 1)
    return keep.astype(jnp.float32) + swap_core(send.astype(jnp.bfloat16)).astype(jnp.float32)


def over_cores(part):
    core = lax.axis_index("span") % 2
    b = part.reshape(2, 2, part.shape[0] // 4, part.shape[1])
    keep, send = in_order(b[:, 0], b[:, 1], core == 1)
    return keep.astype(jnp.float32) + swap_core(send.astype(jnp.bfloat16)).astype(jnp.float32)


def over_low(both):
    low = lax.axis_index("span") // 2
    mine, send = in_order(both[0], both[1], low == 1)
    return mine + swap_low(send.astype(jnp.bfloat16)).astype(jnp.float32)


def span_reduce(part):
    return over_low(over_cores(part))


def fill_pair(rows):
    half = rows.shape[2] // 2
    return jnp.concatenate([rows[:, :, :half], rows[:, :, half:]], axis=1)


def from_pair(pairs):
    half = pairs.shape[1] // 2
    return jnp.concatenate([pairs[:, :half], pairs[:, half:]], axis=2)


def other_plane(rows, got):
    high = lax.axis_index("seg") % 2
    return jnp.stack(in_order(rows, got, high == 1), axis=1).reshape(-1, rows.shape[2])


def both_planes(laid, *blocks):
    high = lax.axis_index("seg") % 2
    own, other = (
        jnp.concatenate(laid(*got), axis=1) for got in (blocks, [swap_high(block) for block in blocks])
    )
    return jnp.concatenate(in_order(own, other, high == 1), axis=0)


def plane_gather(pair):
    whole = lax.all_gather(
        pair,
        "seg",
        axis=0,
        tiled=True,
        axis_index_groups=plane_groups(),
    )
    return with_layout_constraint(whole, Layout(major_to_minor=(0, 1)))


def plane_scatter(part):
    return lax.psum_scatter(
        part, "seg", scatter_dimension=0, tiled=True, axis_index_groups=plane_groups()
    )


def plane_halves(pair):
    high = lax.axis_index("seg") % 2
    rows = pair.shape[0] // 2
    return in_order(pair[:rows], pair[rows:], high == 1)


def finish_scatter(mine, send):
    return mine.astype(jnp.float32) + swap_high(send).astype(jnp.float32)


def gather_and_split(small, wide):
    place = lax.axis_index("span")
    n = wide.shape[1] // 4
    messages = [
        jnp.concatenate([lax.dynamic_slice_in_dim(wide, (place ^ bit) * n, n, 1), small], axis=1)
        for bit in range(4)
    ]
    pieces = [m if bit == 0 else swap(m, bit) for bit, m in enumerate(messages)]
    result = jnp.zeros((4, *messages[0].shape), small.dtype)
    for bit, piece in enumerate(pieces):
        result = lax.dynamic_update_index_in_dim(result, piece, place ^ bit, 0)
    return result.reshape(4 * small.shape[0], -1)


def split_columns(block):
    place = lax.axis_index("span")
    n = block.shape[1] // 4

    def columns(at):
        return lax.dynamic_slice_in_dim(block, at * n, n, 1)

    pieces = [columns(place)] + [swap(columns(place ^ bit), bit) for bit in (1, 2, 3)]
    result = jnp.zeros((4, block.shape[0], n), block.dtype)
    for bit, piece in enumerate(pieces):
        result = lax.dynamic_update_index_in_dim(result, piece, place ^ bit, 0)
    return result.reshape(4 * block.shape[0], n)


def join_columns(block):
    place = lax.axis_index("span")
    r, n = block.shape[0] // 4, block.shape[1]

    def rows(at):
        return lax.dynamic_slice_in_dim(block, at * r, r, 0)

    result = jnp.zeros((r, 4 * n), block.dtype)
    for bit in range(4):
        piece = rows(place ^ bit)
        if bit:
            piece = swap(piece, bit)
        result = lax.dynamic_update_slice_in_dim(result, piece, (place ^ bit) * n, 1)
    return result


def product_lower(left_arg, right_arg):
    return jnp.dot(left_arg, right_arg, preferred_element_type=jnp.float32)


def outer_sum(left_arg, right_arg):
    return jnp.einsum("td,te->de", left_arg, right_arg, preferred_element_type=jnp.float32)


def backward_product(gradient, weights):
    return jnp.einsum("te,de->td", gradient, weights, preferred_element_type=jnp.float32)


def norm_rows(values, gain_vec, offset):
    centre = values - jnp.mean(values, -1, keepdims=True)
    row_rstd = lax.rsqrt(jnp.mean(centre * centre, -1, keepdims=True) + ln_eps)
    unit_rows = centre * row_rstd
    return (unit_rows * gain_vec + offset, unit_rows, row_rstd)


def norm_back(gradient, unit_rows, row_rstd, gain_vec):
    scaled = gradient * gain_vec
    return row_rstd * (
        scaled
        - jnp.mean(scaled, -1, keepdims=True)
        - unit_rows * jnp.mean(scaled * unit_rows, -1, keepdims=True)
    )


def prior_rows(values):
    return jnp.concatenate([jnp.zeros_like(values[:1]), values[:-1]], axis=0)


def next_rows(values):
    return jnp.concatenate([values[1:], jnp.zeros_like(values[:1])], axis=0)


def reduce_small(part, both, pair):
    place, high = lax.axis_index("span"), lax.axis_index("seg") % 2
    planes = lax.axis_size("seg") // 2
    width = part.shape[1]
    b = part.reshape(planes, 2, 2, 2, -1, width)

    def summed(b, dim, bit, move):
        at0, at1 = (lax.index_in_dim(b, k, dim, keepdims=False) for k in (0, 1))
        mine, send = in_order(at0, at1, bit == 1)
        return mine.astype(jnp.float32) + move(send.astype(jnp.bfloat16)).astype(jnp.float32)

    b = summed(summed(b, 3, place % 2, swap_core), 2, place // 2, swap_low)
    b, both = lax.optimization_barrier((b, both))
    rows = over_low(both)
    b = summed(b, 1, high, swap_high).astype(jnp.bfloat16)
    b, pair = lax.optimization_barrier((b, pair))
    finished = finish_scatter(*plane_halves(pair))
    arrived = lax.all_to_all(
        b, "seg", split_axis=0, concat_axis=0, tiled=True, axis_index_groups=plane_groups()
    )
    return arrived.astype(jnp.float32).sum(axis=0), rows, finished


SOON = pl.CostEstimate(flops=2**20, bytes_accessed=2**16, transcendentals=0)

CHUNK = 64
PACK = 256


def mxu(a, b, contract):
    return lax.dot_general(
        a.astype(jnp.bfloat16),
        b.astype(jnp.bfloat16),
        (contract, ((), ())),
        preferred_element_type=jnp.float32,
    )


NN, NT, TN = ((1,), (0,)), ((1,), (1,)), ((0,), (0,))


def halves(values):
    high = values.astype(jnp.bfloat16)
    return high, (values - high.astype(jnp.float32)).astype(jnp.bfloat16)


def iota2(shape, dim):
    return lax.broadcasted_iota(jnp.int32, shape, dim)


def head_ones():
    shape = (PACK, PACK)
    same = (iota2(shape, 0) ^ iota2(shape, 1)) < GROUP_DIMENSION
    return jnp.where(same, 1.0, 0.0).astype(jnp.float32)


def spread(block, ones):
    return jnp.concatenate([block] * (PACK // CHUNK), axis=0) * ones


def fold(big, ones):
    kept = big * ones
    total = kept[:CHUNK]
    for h in range(1, PACK // CHUNK):
        total = total + kept[h * CHUNK : (h + 1) * CHUNK]
    return total


def head_sum(values, ones):
    high, rest = halves(values)
    return mxu(high, ones, NN) + mxu(rest, ones, NN)


def run_sum(which, values):
    high, rest = halves(values)
    return mxu(which, high, NN) + mxu(which, rest, NN)


def row_of(values, row):
    return values[row : row + 1]


def piece_factors(run, before):
    rows = iota2((CHUNK, PACK), 0)
    apart = rows ^ (iota2((CHUNK, PACK), 1) & (CHUNK - 1))
    levels = []
    for half in (32, 16, 8, 4, 2, 1):
        upper = (rows & half) != 0
        if half == 1:
            scale = jnp.ones_like(run)
        else:
            if half == 2:
                reference = run
                for row, shift in ((0, CHUNK - 1), (2, 1), (3, 2)):
                    reference = jnp.where((rows & 3) == row, pltpu.roll(run, shift, 0), reference)
            else:
                reference = jnp.broadcast_to(row_of(run, half - 1), run.shape)
                for start in range(2 * half, CHUNK, 2 * half):
                    here = jnp.broadcast_to(row_of(run, start + half - 1), run.shape)
                    reference = jnp.where(rows >= start, here, reference)
            scale = jnp.exp(jnp.minimum(jnp.where(upper, before - reference, reference - run), 0.0))
        pairs = (apart < 2 * half) & upper & ((apart & half) != 0)
        levels.append((jnp.where(upper, scale, 0.0), jnp.where(upper, 0.0, scale), pairs))
    return levels


NOTHING = -104.0


def lower_ones():
    return jnp.where(iota2((CHUNK, CHUNK), 0) >= iota2((CHUNK, CHUNK), 1), 1.0, 0.0).astype(jnp.float32)


def decay_of(low_ref, up_ref, par_ref):
    log_decay = -jnp.exp(par_ref[0:1] + mxu(low_ref[...], up_ref[...], NT))
    kept = jnp.maximum(log_decay, NOTHING)
    run = run_sum(lower_ones(), kept)
    return jnp.where(log_decay <= NOTHING, 0.0, log_decay), run, run - kept


def unit_heads(wkv, ones):
    centre = wkv - head_sum(wkv, ones) * (1.0 / GROUP_DIMENSION)
    rstd = lax.rsqrt(head_sum(centre * centre, ones) * (1.0 / GROUP_DIMENSION) + gn_eps)
    return centre * rstd, rstd


def lane_groups(refs, kinds):
    width = refs[0].shape[1]
    for g in range(width // PACK):
        lanes = pl.ds(g * PACK, PACK)
        part = {"c": lambda ref: ref.at[:, lanes], "r": lambda ref: ref.at[lanes], "s": lambda ref: ref.at[g]}
        yield [ref if kind == "w" else part[kind](ref) for ref, kind in zip(refs, kinds)]


def in_turns(*bodies):
    bodies = list(bodies)
    while bodies:
        bodies = [body for body in bodies if next(body, body) is not body]


def wkv_forward_kernel(*refs):
    groups = list(lane_groups(refs, "ccccwrcccccs"))
    ones = head_ones()

    @pl.when(pl.program_id(0) == 0)
    def _():
        for *_, first_ref, _, _, _, state in groups:
            state[...] = spread(first_ref[...], ones)

    in_turns(*(forward_heads(ones, *group) for group in groups))


def wkv_backward_kernel(*refs):
    groups = list(lane_groups(refs, "ccccwrccccccccccc" + "s"))
    ones = head_ones()

    @pl.when(pl.program_id(0) == 0)
    def _():
        for *_, sums_ref, _, state in groups:
            state[...] = jnp.zeros_like(state)
            sums_ref[...] = jnp.zeros_like(sums_ref)

    in_turns(*(backward_heads(ones, *group) for group in groups))

    @pl.when(pl.program_id(0) == pl.num_programs(0) - 1)
    def _():
        for *_, first_ref, state in groups:
            first_ref[...] = fold(state[...], ones)


def forward_heads(
    ones, r_ref, k_ref, v_ref, gate_ref, low_ref, up_ref, par_ref, first_ref, mixed_ref, wkv_ref, held_ref, state
):
    r, k, v = r_ref[...], k_ref[...], v_ref[...]
    _, run, before = decay_of(low_ref, up_ref, par_ref)
    yield
    held_ref[...] = fold(state[...], ones)
    score = jnp.zeros((CHUNK, PACK), jnp.float32)
    for to_row, to_prior, pairs in piece_factors(run, before):
        score = jnp.where(pairs, mxu(r * to_row, spread(k * to_prior, ones), NT), score)
        yield
    out = mxu(score, spread(v, ones), NN) + mxu(r * jnp.exp(before), state[...], NT)
    out = out + head_sum(r * par_ref[1:2] * k, ones) * v
    yield
    wkv_ref[...] = out
    last = row_of(run, CHUNK - 1)
    state[...] = jnp.exp(last) * state[...] + mxu(v, k * jnp.exp(last - run), TN) * ones
    yield
    unit, _ = unit_heads(out, ones)
    yield
    gate = gate_ref[...]
    mixed_ref[...] = ((unit * par_ref[2:3] + par_ref[3:4]) * gate * jax.nn.sigmoid(gate)).astype(jnp.bfloat16)


def wkv_forward(r, k, v, gate, low, up, par, first):
    rows, columns = r.shape
    chunks = rows // CHUNK
    block = pl.BlockSpec((CHUNK, columns), lambda c: (c, 0))
    whole = lambda a: pl.BlockSpec(a.shape, lambda c: (0, 0))
    return pl.pallas_call(
        wkv_forward_kernel,
        grid=(chunks,),
        in_specs=[block] * 4
        + [
            pl.BlockSpec((CHUNK, low.shape[1]), lambda c: (c, 0)),
            whole(up),
            whole(par),
            whole(first),
        ],
        out_specs=[block, block, block],
        out_shape=[
            jax.ShapeDtypeStruct((rows, columns), jnp.bfloat16),
            jax.ShapeDtypeStruct((rows, columns), jnp.float32),
            jax.ShapeDtypeStruct((rows, columns), jnp.float32),
        ],
        scratch_shapes=[pltpu.VMEM((columns // PACK, PACK, PACK), jnp.float32)],
        compiler_params=pltpu.CompilerParams(
            dimension_semantics=("arbitrary",), vmem_limit_bytes=32 * 2**20
        ),
        cost_estimate=SOON,
        name="wkv_forward",
    )(*[pltpu.with_memory_space_constraint(x, pltpu.HBM) for x in (r, k, v, gate)], low, up, par, first)


def backward_heads(
    ones, r_ref, k_ref, v_ref, gate_ref, low_ref, up_ref, par_ref, wkv_ref, held_ref, gm_ref,
    gr_ref, gk_ref, gv_ref, gg_ref, gw_ref, sums_ref, first_ref, state,
):
    r, k, v, gate = r_ref[...], k_ref[...], v_ref[...], gate_ref[...]
    bonus, gain = par_ref[1:2], par_ref[2:3]

    def add_to(row, values):
        sums_ref[row : row + 1] = sums_ref[row : row + 1] + jnp.sum(values, axis=0, keepdims=True)

    unit, rstd = unit_heads(wkv_ref[...], ones)
    yield
    sig = jax.nn.sigmoid(gate)
    g_mixed = gm_ref[...].astype(jnp.float32)
    g_grouped = g_mixed * gate * sig
    grouped = unit * gain + par_ref[3:4]
    gg_ref[...] = (g_mixed * grouped * sig * (1.0 + gate * (1.0 - sig))).astype(jnp.bfloat16)
    add_to(2, g_grouped * unit)
    add_to(3, g_grouped)
    g_unit = g_grouped * gain
    scale = 1.0 / GROUP_DIMENSION
    g_out = rstd * (
        g_unit - head_sum(g_unit, ones) * scale - unit * (head_sum(g_unit * unit, ones) * scale)
    )

    yield
    log_decay, run, before = decay_of(low_ref, up_ref, par_ref)
    yield
    last = row_of(run, CHUNK - 1)
    start = spread(held_ref[...], ones)
    end_grad = state[...]
    yield
    v_wide = spread(v, ones)
    g_score = mxu(g_out, v_wide, NT)
    score = jnp.zeros((CHUNK, PACK), jnp.float32)
    from_start = jnp.exp(before)
    g_r = from_start * mxu(g_out, start, NN)
    g_before = r * g_r
    to_end = jnp.exp(last - run)
    g_end = to_end * mxu(v, end_grad, NN)
    g_k = g_end
    g_after = k * g_end
    for to_row, to_prior, pairs in piece_factors(run, before):
        r_level = (r * to_row).astype(jnp.bfloat16)
        k_rows = (k * to_prior).astype(jnp.bfloat16)
        k_level = spread(k_rows.astype(jnp.float32), ones).astype(jnp.bfloat16)
        score = jnp.where(pairs, mxu(r_level, k_level, NT), score)
        yield
        g_level = jnp.where(pairs, g_score, 0.0).astype(jnp.bfloat16)
        g_rows = mxu(g_level, k_level, NN)
        yield
        g_prior = fold(mxu(g_level, r_level, TN), ones)
        g_r = g_r + to_row * g_rows
        g_k = g_k + to_prior * g_prior
        g_before = g_before + r_level.astype(jnp.float32) * g_rows
        g_after = g_after + k_rows.astype(jnp.float32) * g_prior
        yield
    g_v = fold(mxu(score, g_out, TN), ones) + mxu(k * to_end, end_grad, NT)
    g_run = g_before - g_after
    g_last = jnp.sum(k * g_end, axis=0, keepdims=True) + jnp.exp(last) * jnp.sum(
        start * end_grad, axis=0, keepdims=True
    )
    upper = jnp.where(iota2((CHUNK, CHUNK), 0) <= iota2((CHUNK, CHUNK), 1), 1.0, 0.0).astype(jnp.float32)
    g_decay = run_sum(upper, g_run) - g_before + g_last
    yield
    g_expo = g_decay * log_decay
    gw_ref[...] = g_expo.astype(jnp.bfloat16)
    add_to(0, g_expo)
    yield
    g_diag = head_sum(g_out * v, ones)
    add_to(1, r * k * g_diag)
    gr_ref[...] = (g_r + bonus * k * g_diag).astype(jnp.bfloat16)
    gk_ref[...] = (g_k + bonus * r * g_diag).astype(jnp.bfloat16)
    gv_ref[...] = (g_v + head_sum(r * bonus * k, ones) * g_out).astype(jnp.bfloat16)
    state[...] = jnp.exp(last) * end_grad + mxu(g_out, r * from_start, TN) * ones


def wkv_backward(r, k, v, gate, low, up, par, wkv, held, g_mixed):
    rows, columns = r.shape
    chunks = rows // CHUNK
    block = pl.BlockSpec((CHUNK, columns), lambda c: (chunks - 1 - c, 0))
    whole = lambda a: pl.BlockSpec(a.shape, lambda c: (0, 0))
    of_all = lambda n: pl.BlockSpec((n, columns), lambda c: (0, 0))
    low_type = jax.ShapeDtypeStruct((rows, columns), jnp.bfloat16)
    return pl.pallas_call(
        wkv_backward_kernel,
        grid=(chunks,),
        in_specs=[block] * 4
        + [
            pl.BlockSpec((CHUNK, low.shape[1]), lambda c: (chunks - 1 - c, 0)),
            whole(up),
            whole(par),
            block,
            block,
            block,
        ],
        out_specs=[block] * 5 + [of_all(8), of_all(GROUP_DIMENSION)],
        out_shape=[low_type] * 5
        + [
            jax.ShapeDtypeStruct((8, columns), jnp.float32),
            jax.ShapeDtypeStruct((GROUP_DIMENSION, columns), jnp.float32),
        ],
        scratch_shapes=[pltpu.VMEM((columns // PACK, PACK, PACK), jnp.float32)],
        compiler_params=pltpu.CompilerParams(
            dimension_semantics=("arbitrary",), vmem_limit_bytes=32 * 2**20
        ),
        cost_estimate=SOON,
        name="wkv_backward",
    )(r, k, v, gate, low, up, par, wkv, held, g_mixed)


GRAD_ROWS, GRAD_COLUMNS = 512, 256


def grad_kernel(left_ref, right_ref, *rest):
    out_ref = rest[-1]
    turned = left_ref[...].T
    for at in range(0, out_ref.shape[1], GRAD_COLUMNS):
        columns = slice(at, at + GRAD_COLUMNS)
        out_ref[:, columns] = mxu(turned, right_ref[:, columns], NN).astype(jnp.bfloat16)


def grad_into(left, right, total, at, into=None):
    rows, width = left.shape
    columns = right.shape[1]
    shift = at // columns
    specs = [
        pl.BlockSpec((rows, GRAD_ROWS), lambda i: (0, i)),
        pl.BlockSpec((rows, columns), lambda i: (0, 0)),
    ]
    operands = [left, right]
    alias = {}
    if into is not None:
        specs.append(pl.BlockSpec(memory_space=pltpu.HBM))
        operands.append(into)
        alias = {2: 0}
    return pl.pallas_call(
        grad_kernel,
        grid=(width // GRAD_ROWS,),
        in_specs=specs,
        out_specs=pl.BlockSpec((GRAD_ROWS, columns), lambda i: (i, shift)),
        out_shape=pltpu.HBM((width, total), jnp.bfloat16),
        input_output_aliases=alias,
        compiler_params=pltpu.CompilerParams(
            dimension_semantics=("arbitrary",), vmem_limit_bytes=32 * 2**20
        ),
        cost_estimate=SOON,
        name="weight_grad",
    )(*operands)


def grads_kernel(*refs):
    count = len(refs) // 2
    out_ref = refs[-1]
    for n in range(count):

        @pl.when(pl.program_id(0) == n)
        def _(left_ref=refs[n], right_ref=refs[count + n]):
            turned = left_ref[...].T
            for at in range(0, out_ref.shape[1], GRAD_COLUMNS):
                columns = slice(at, at + GRAD_COLUMNS)
                out_ref[:, columns] = mxu(turned, right_ref[:, columns], NN).astype(jnp.bfloat16)


def grads_side_by_side(lefts, rights, total):
    rows, width = lefts[0].shape
    columns = rights[0].shape[1]
    blocks = width // GRAD_ROWS

    def left_spec(n):
        return pl.BlockSpec(
            (rows, GRAD_ROWS),
            lambda p, i: (0, jnp.where(p == n, i, jnp.where(p < n, 0, blocks - 1))),
        )

    return pl.pallas_call(
        grads_kernel,
        grid=(len(lefts), blocks),
        in_specs=[left_spec(n) for n in range(len(lefts))]
        + [pl.BlockSpec((rows, columns), lambda p, i: (0, 0))] * len(rights),
        out_specs=pl.BlockSpec((GRAD_ROWS, columns), lambda p, i: (i, p)),
        out_shape=pltpu.HBM((width, total), jnp.bfloat16),
        compiler_params=pltpu.CompilerParams(
            dimension_semantics=("arbitrary", "arbitrary"), vmem_limit_bytes=32 * 2**20
        ),
        cost_estimate=SOON,
        name="time_mix_grads",
    )(*lefts, *rights)


LOW = 256
SHIFT_LANES = 5 * SHIFT_RANK
LANES = SHIFT_LANES + 64

TILE = 512


def vectors_kernel(up_ref, out_ref):
    turned = up_ref[...].astype(jnp.float32).T
    out_ref[...] = turned[LANES : LANES + 16]


def turn_vectors(first, up_at):
    width = first.shape[0]
    return pl.pallas_call(
        vectors_kernel,
        grid=(width // TILE,),
        in_specs=[pl.BlockSpec((TILE, LOW), lambda n: (n, up_at // LOW))],
        out_specs=pl.BlockSpec((16, TILE), lambda n: (0, n)),
        out_shape=jax.ShapeDtypeStruct((16, width), jnp.float32),
        compiler_params=pltpu.CompilerParams(dimension_semantics=("arbitrary",)),
        cost_estimate=SOON,
        name="turn_vectors",
    )(first)


def lane_group(shape):
    return lax.shift_right_logical(iota2(shape, 1), 5)


def mixes_forward_kernel(
    unit_ref, w_ref, down_ref, up_ref, vec_ref,
    m0_ref, m1_ref, m2_ref, m3_ref, m4_ref, normed_ref, squash_ref, r_ref, k_ref, v_ref, g_ref,
    hidden, grouped,
):
    phase, tile = pl.program_id(0), pl.program_id(1)
    rows = unit_ref.shape[0]
    own = r_ref.shape[1]
    vec = vec_ref[...]
    normed = unit_ref[...] * vec[0:1] + vec[1:2]
    row = iota2(normed.shape, 0)
    shifted = jnp.where(row == 0, 0.0, pltpu.roll(normed, 1, 0)) - normed
    down = down_ref[...]
    of_shift = iota2(down.shape, 1) < SHIFT_LANES

    @pl.when((phase == 0) & (tile == 0))
    def _():
        hidden[...] = jnp.zeros_like(hidden)

    @pl.when(phase == 0)
    def _():
        hidden[...] = hidden[...] + mxu(normed + shifted * vec[2:3], jnp.where(of_shift, down, 0), NN)

    @pl.when((phase == 1) & (tile == 0))
    def _():
        squash = jnp.tanh(hidden[...])
        squash_ref[...] = squash
        group = lane_group(squash.shape)
        for g in range(5):
            grouped[g] = jnp.where(group == g, squash, 0.0).astype(jnp.bfloat16)
        hidden[...] = jnp.zeros_like(hidden)
        for ref in (r_ref, k_ref, v_ref, g_ref):
            ref[...] = jnp.zeros_like(ref)

    @pl.when(phase == 1)
    def _():
        normed_ref[...] = normed
        up = up_ref[...]
        for g, mix_ref in enumerate((m0_ref, m1_ref, m2_ref, m3_ref, m4_ref)):
            mix = (normed + shifted * (vec[3 + g : 4 + g] + mxu(grouped[g], up, NT))).astype(jnp.bfloat16)
            mix_ref[...] = mix
            if g == 0:
                hidden[...] = hidden[...] + mxu(mix, jnp.where(of_shift, 0, down), NN)
            else:
                column = (None, 1, 2, 0, 3)[g] * own
                out = (None, k_ref, v_ref, r_ref, g_ref)[g]
                out[...] = out[...] + mxu(mix, w_ref[:, column : column + own], NN)

    @pl.when((phase == 1) & (tile == pl.num_programs(1) - 1))
    def _():
        squash_ref[...] = squash_ref[...] + jnp.tanh(hidden[...])


def mixes_forward(unit, first, low_at, vec, own):
    rows, width = unit.shape
    tiles = width // TILE
    block = low_at // LOW
    across = lambda r: pl.BlockSpec((r, TILE), lambda p, n: (0, n))
    late = pl.BlockSpec((rows, TILE), lambda p, n: (0, n * p))
    whole = lambda columns: pl.BlockSpec((rows, columns), lambda p, n: (0, 0))
    kept = lambda columns, dtype: jax.ShapeDtypeStruct((rows, columns), dtype)
    return pl.pallas_call(
        mixes_forward_kernel,
        grid=(2, tiles),
        in_specs=[
            across(rows),
            pl.BlockSpec((TILE, 4 * own), lambda p, n: (n * p, 0)),
            pl.BlockSpec((TILE, LOW), lambda p, n: (n, block)),
            pl.BlockSpec((TILE, LOW), lambda p, n: (n, block + 1)),
            across(vec.shape[0]),
        ],
        out_specs=[late] * 6 + [whole(LOW)] + [whole(own)] * 4,
        out_shape=[kept(width, jnp.bfloat16)] * 5
        + [kept(width, jnp.float32), kept(LOW, jnp.float32)]
        + [pltpu.HBM((rows, own), jnp.float32)] * 4,
        scratch_shapes=[pltpu.VMEM((rows, LOW), jnp.float32), pltpu.VMEM((5, rows, LOW), jnp.bfloat16)],
        compiler_params=pltpu.CompilerParams(
            dimension_semantics=("arbitrary", "arbitrary"), vmem_limit_bytes=54 * 2**20
        ),
        cost_estimate=SOON,
        name="mixes_forward",
    )(unit, first, first, first, vec)


def mixes_back_kernel(
    gk_ref, gv_ref, gr_ref, gg_ref, gd_ref, w_ref, down_ref, up_ref, vec_ref, squash_ref, normed_ref,
    mix_ref, sums_ref, out_ref, small_ref,
    g_shift, g_norm, g_squash, g_hidden, g_up, g_sums, grouped, turned,
):
    phase, tile = pl.program_id(0), pl.program_id(1)
    rows = squash_ref.shape[0]
    own = gk_ref.shape[1]
    normed = normed_ref[...]
    row = iota2(normed.shape, 0)
    shifted = jnp.where(row == 0, 0.0, pltpu.roll(normed, 1, 0)) - normed
    squash = squash_ref[...]
    vec = vec_ref[...]

    @pl.when((phase == 0) & (tile == 0))
    def _():
        g_squash[...] = jnp.zeros_like(g_squash)
        group = lane_group(squash.shape)
        for g in range(5):
            grouped[g] = jnp.where(group == g, squash, 0.0).astype(jnp.bfloat16)
        turned[...] = squash.astype(jnp.bfloat16).T

    @pl.when(phase == 0)
    def _():
        up = up_ref[...]
        group_wide = lane_group(up.shape)
        total_shift = jnp.zeros((rows, TILE), jnp.float32)
        total_norm = jnp.zeros((rows, TILE), jnp.float32)
        add_squash = jnp.zeros((rows, LOW), jnp.float32)
        sums = []
        for g in range(5):
            if g == 0:
                part = mxu(gd_ref[...], down_ref[...], NT)
            else:
                column = (None, 1, 2, 0, 3)[g] * own
                grad = (None, gk_ref, gv_ref, gr_ref, gg_ref)[g]
                part = mxu(grad[...], w_ref[:, column : column + own], NT)
            coeff = vec[3 + g : 4 + g] + mxu(grouped[g], up, NT)
            times = part * shifted
            times_low = times.astype(jnp.bfloat16)
            sums.append(jnp.sum(times, axis=0, keepdims=True))
            total_shift = total_shift + part * coeff
            total_norm = total_norm + part
            add_squash = add_squash + mxu(times_low, jnp.where(group_wide == g, up, 0), NN)
            lanes = slice(g * SHIFT_RANK, (g + 1) * SHIFT_RANK)
            g_up[tile, lanes] = mxu(turned[lanes], times_low, NN)
        g_shift[tile] = total_shift
        g_norm[tile] = total_norm
        g_squash[...] = g_squash[...] + add_squash
        g_sums[tile] = jnp.concatenate(sums + [jnp.zeros((3, TILE), jnp.float32)], axis=0)

    @pl.when((phase == 1) & (tile == 0))
    def _():
        g_hidden[...] = (g_squash[...] * (1.0 - squash * squash)).astype(jnp.bfloat16)

    @pl.when(phase == 1)
    def _():
        blend = vec[2:3]
        part = mxu(g_hidden[...], down_ref[...], NT)
        total_shift = g_shift[tile] + part * blend
        total = g_norm[tile] + part - total_shift
        total = total + jnp.where(row == rows - 1, 0.0, pltpu.roll(total_shift, rows - 1, 0))
        out_ref[...] = total.astype(jnp.bfloat16)
        unit = (normed - vec[1:2]) / vec[0:1]
        head = [
            jnp.sum(total * unit, axis=0, keepdims=True),
            jnp.sum(total, axis=0, keepdims=True),
            jnp.sum(part * shifted, axis=0, keepdims=True),
        ]
        sums = jnp.concatenate(head + [g_sums[tile][:5], sums_ref[...]], axis=0)
        shape = (sums.shape[0], LOW)
        behind = jnp.where(iota2(shape, 1) == LANES + iota2(shape, 0), 1.0, 0.0)
        small_ref[:, :LOW] = (
            mxu(normed + shifted * blend, g_hidden[...], TN) + mxu(mix_ref[...], gd_ref[...], TN)
        ).astype(jnp.bfloat16)
        small_ref[:, LOW:] = mxu(sums, behind, TN).astype(jnp.bfloat16)
        small_ref[:, LOW : LOW + SHIFT_LANES] = g_up[tile].T.astype(jnp.bfloat16)


def mixes_back(g_key, g_val, g_recept, g_gate, g_decay, first, low_at, vec, squash, normed, mix, sums):
    rows, width = normed.shape
    own = g_key.shape[1]
    tiles = width // TILE
    block = low_at // LOW
    whole = lambda a: pl.BlockSpec(a.shape, lambda p, n: (0, 0))
    across = lambda r: pl.BlockSpec((r, TILE), lambda p, n: (0, n))
    late = lambda r: pl.BlockSpec((r, TILE), lambda p, n: (0, n * p))
    early = lambda p, n: n * (1 - p) + (tiles - 1) * p
    return pl.pallas_call(
        mixes_back_kernel,
        grid=(2, tiles),
        in_specs=[whole(g_key)] * 4
        + [
            whole(g_decay),
            pl.BlockSpec((TILE, 4 * own), lambda p, n: (early(p, n), 0)),
            pl.BlockSpec((TILE, LOW), lambda p, n: (n, block)),
            pl.BlockSpec((TILE, LOW), lambda p, n: (early(p, n), block + 1)),
            across(vec.shape[0]),
            whole(squash),
            across(rows),
            late(rows),
            late(sums.shape[0]),
        ],
        out_specs=[late(rows), pl.BlockSpec((TILE, 2 * LOW), lambda p, n: (n * p, 0))],
        out_shape=[
            jax.ShapeDtypeStruct((rows, width), jnp.bfloat16),
            jax.ShapeDtypeStruct((width, 2 * LOW), jnp.bfloat16),
        ],
        scratch_shapes=[
            pltpu.VMEM((tiles, rows, TILE), jnp.float32),
            pltpu.VMEM((tiles, rows, TILE), jnp.float32),
            pltpu.VMEM((rows, LOW), jnp.float32),
            pltpu.VMEM((rows, LOW), jnp.bfloat16),
            pltpu.VMEM((tiles, SHIFT_LANES, TILE), jnp.float32),
            pltpu.VMEM((tiles, 8, TILE), jnp.float32),
            pltpu.VMEM((5, rows, LOW), jnp.bfloat16),
            pltpu.VMEM((LOW, rows), jnp.bfloat16),
        ],
        compiler_params=pltpu.CompilerParams(
            dimension_semantics=("arbitrary", "arbitrary"), vmem_limit_bytes=56 * 2**20
        ),
        cost_estimate=SOON,
        name="mixes_back",
    )(g_key, g_val, g_recept, g_gate, g_decay, first, first, first, vec, squash, normed, mix, sums)


def shards(
    inputs,
    cotangent,
    states,
    vectors,
    time_mix_weight,
    output_weight,
    channel_receptance_weight,
    rank_down_weight,
    rank_up_weight,
    channel_key_weight,
    channel_value_weight,
):
    token_rows, width = inputs.shape
    seg_count = lax.axis_size("seg")
    own_width = time_mix_weight.shape[2]
    hidden = channel_key_weight.shape[1]
    local_heads = own_width // GROUP_DIMENSION
    col_start = lax.axis_index("span") * own_width
    position = lax.axis_index("span") * token_rows

    x_seg = span_gather(inputs).astype(jnp.float32)
    grad_columns = split_columns(cotangent).astype(jnp.float32)
    def blank(count):
        return jnp.zeros((token_rows // 8, count), jnp.bfloat16)

    small_rows = jnp.concatenate(
        [rank_down_weight, blank(LOW - LANES), rank_up_weight.T, vectors.T, blank(LOW - LANES - 16)], axis=1
    )
    span_rows = gather_and_split(small_rows, channel_receptance_weight)
    weights = both_planes(lambda proj: [proj[g] for g in range(4)], time_mix_weight)
    small_pair = both_planes(lambda rows: [rows], span_rows[:, own_width:])
    late_pairs = [fill_pair(rows[None])[0] for rows in (output_weight.T, span_rows[:, :own_width])]
    first = plane_gather(jnp.concatenate([weights, small_pair] + late_pairs, axis=1))
    _, unit_seg, _ = norm_rows(x_seg, 1.0, 0.0)
    second_pair = both_planes(lambda key, value: [key, value.T], channel_key_weight, channel_value_weight)
    second_pair, unit_seg, grad_columns = lax.optimization_barrier((second_pair, unit_seg, grad_columns))
    second = plane_gather(second_pair)
    low_at = 4 * own_width
    late_at = low_at + 2 * LOW

    def late_rows(at):
        pairs = first[:, at : at + own_width // 2].reshape(-1, 2 * (width // seg_count), own_width // 2)
        return from_pair(pairs)

    out_half, recept_half = late_rows(late_at), late_rows(late_at + own_width // 2)
    late_got = swap_high(jnp.concatenate([out_half, recept_half], axis=2))
    out_got, recept_got = late_got[:, :, :own_width], late_got[:, :, own_width:]
    up_at = low_at + LOW
    vec = first[:, up_at + LANES : up_at + LANES + 16].T.astype(jnp.float32)

    def own_cols(line):
        return lax.dynamic_slice_in_dim(line, col_start, own_width, line.ndim - 1)

    def own_rows(values):
        return lax.dynamic_slice_in_dim(values, position, token_rows, 0)

    x_in = inputs.astype(jnp.float32)
    *mixes, normed, squash, recept, key_proj, val_proj, gate_pre = mixes_forward(
        unit_seg, first, low_at, vec, own_width
    )
    lane = lax.broadcasted_iota(jnp.int32, squash.shape, 1)
    of_decay = (lane >= SHIFT_LANES) & (lane < LANES)
    decay_low = jnp.where(of_decay, squash, 0.0).astype(jnp.bfloat16)
    up_own = lax.dynamic_slice(first, (col_start, up_at), (own_width, LOW))
    head_vec = jnp.concatenate([own_cols(vec[8:12]), jnp.zeros((4, own_width), jnp.float32)], axis=0)
    first_state = jnp.transpose(states[0], (2, 0, 1)).reshape(GROUP_DIMENSION, own_width)
    out_w = other_plane(out_half, out_got)
    heads_in = (recept, key_proj, val_proj, gate_pre, decay_low, up_own, head_vec)
    mixed, wkv, held = wkv_forward(*heads_in, first_state)
    recept_w = other_plane(recept_half, recept_got)
    resid = x_in + span_reduce(backward_product(mixed, out_w).astype(jnp.bfloat16))

    normed_two, unit_two, rstd_two = norm_rows(resid, vec[12], vec[13])
    n2 = span_gather(normed_two.astype(jnp.bfloat16)).astype(jnp.float32)
    shifted_two = prior_rows(n2) - n2
    key_in = (n2 + shifted_two * vec[14]).astype(jnp.bfloat16)
    rec_in = (n2 + shifted_two * vec[15]).astype(jnp.bfloat16)
    rec_gate = jax.nn.sigmoid(product_lower(rec_in, recept_w))
    g_value = (grad_columns * rec_gate).astype(jnp.bfloat16)
    g_value, second = lax.optimization_barrier((g_value, second))
    g_value_all = span_gather(g_value, 1)
    key_w, value_w = second[:, :hidden], second[:, hidden:]
    hidden_two = product_lower(key_in, key_w)
    active = jax.nn.relu(hidden_two)
    squared = (active * active).astype(jnp.bfloat16)
    active = active.astype(jnp.bfloat16)

    low = lax.axis_index("span") // 2

    def value_columns(which):
        weights = lax.dynamic_slice(second, (which * (width // 2), hidden), (width // 2, hidden))
        return core_reduce(backward_product(squared, weights).astype(jnp.bfloat16))

    far, near = value_columns(1 - low), value_columns(low)
    far, g_value_all = lax.optimization_barrier((far.astype(jnp.bfloat16), g_value_all))
    far = swap_low(far)
    cm_total = 2 * hidden
    g_hid = (product_lower(g_value_all, value_w) * 2.0 * active.astype(jnp.float32)).astype(jnp.bfloat16)
    g_value_all, g_hid = lax.optimization_barrier((g_value_all, g_hid))
    cm_part = grad_into(g_value_all, squared, cm_total, hidden)
    far, near, cm_part = lax.optimization_barrier((far, near, cm_part))
    cm_part = grad_into(key_in, g_hid, cm_total, 0, cm_part)
    cm_part, g_hid = lax.optimization_barrier((cm_part, g_hid))
    cm_pair = plane_scatter(cm_part)
    value_out = near + far.astype(jnp.float32)
    gated = (rec_gate * value_out).astype(jnp.bfloat16)
    g_rec = (grad_columns * value_out * rec_gate * (1.0 - rec_gate)).astype(jnp.bfloat16)
    g_key_in = backward_product(g_hid, key_w)
    g_rec_in = backward_product(g_rec, recept_w)
    vec_fourteen = jnp.sum(g_key_in * shifted_two, axis=0)
    vec_fifteen = jnp.sum(g_rec_in * shifted_two, axis=0)
    g_shift_two = g_key_in * vec[14] + g_rec_in * vec[15]
    g_n2_part = g_key_in + g_rec_in - g_shift_two + next_rows(g_shift_two)
    g_n2 = span_reduce(g_n2_part.astype(jnp.bfloat16))
    rec_part = grad_into(rec_in, g_rec, own_width, 0)
    g_n2, rec_part = lax.optimization_barrier((g_n2, rec_part))
    vec_twelve = jnp.sum(g_n2 * unit_two, axis=0)
    vec_thirteen = jnp.sum(g_n2, axis=0)
    g_resid = cotangent.astype(jnp.float32) + norm_back(g_n2, unit_two, rstd_two, vec[12])

    g_att = span_gather(g_resid.astype(jnp.bfloat16))
    rec_part = rec_part.reshape(seg_count // 2, 2, width // seg_count, own_width)
    rec_mine, rec_send = in_order(rec_part[:, 0], rec_part[:, 1], lax.axis_index("seg") % 2 == 1)
    g_att, gated, rec_send = lax.optimization_barrier((g_att, gated, rec_send))
    rec_got = swap_high(rec_send)
    gated_rows = join_columns(gated)
    g_mixed = product_lower(g_att, out_w)
    g_recept, g_key, g_val, g_gate, g_ww, head_sums, g_first = wkv_backward(
        *heads_in, wkv, held, g_mixed
    )
    state_grad = jnp.transpose(
        g_first.reshape(GROUP_DIMENSION, local_heads, GROUP_DIMENSION), (1, 2, 0)
    )[None]
    tm_total = 5 * own_width + own_width // 2
    tm_part = grads_side_by_side(
        (g_att, mixes[3], mixes[1], mixes[2], mixes[4]), (mixed, g_recept, g_key, g_val, g_gate), tm_total
    )
    rec_got, g_ww = lax.optimization_barrier((rec_got, g_ww))
    rec_sum = (rec_mine.astype(jnp.float32) + rec_got.astype(jnp.float32)).astype(jnp.bfloat16)
    tm_part = lax.dynamic_update_slice(
        tm_part, fill_pair(rec_sum).reshape(width, own_width // 2), (0, 5 * own_width)
    )
    tm_part, cm_pair, gated_rows = lax.optimization_barrier((tm_part, cm_pair, gated_rows))
    output = (resid + gated_rows.astype(jnp.float32)).astype(jnp.bfloat16)
    tm_pair = plane_scatter(tm_part)
    g_key, g_ww, cm_pair = lax.optimization_barrier((g_key, g_ww, cm_pair))

    g_decay_hidden = jnp.where(
        of_decay, product_lower(g_ww, up_own) * (1.0 - squash * squash), 0.0
    ).astype(jnp.bfloat16)
    up_decay_grad = outer_sum(g_ww, decay_low)
    other_sums = jnp.concatenate(
        [
            lax.dynamic_update_slice_in_dim(jnp.zeros((4, width), jnp.float32), head_sums[:4], col_start, 1),
            jnp.stack([vec_twelve, vec_thirteen, vec_fourteen, vec_fifteen]),
        ],
        axis=0,
    )
    g_normed, small_part = mixes_back(
        g_key, g_val, g_recept, g_gate, g_decay_hidden, first, low_at, vec, squash, normed, mixes[0], other_sums
    )
    own_part = lax.dynamic_slice(small_part, (col_start, LOW), (own_width, LOW))
    small_part = lax.dynamic_update_slice(
        small_part, (own_part.astype(jnp.float32) + up_decay_grad).astype(jnp.bfloat16), (col_start, LOW)
    )
    small, g_n1, cm_grad = reduce_small(small_part, over_cores(g_normed), cm_pair)
    rec_own = from_pair(tm_pair[None, :, 5 * own_width :])[0]
    tm_grad = finish_scatter(*plane_halves(tm_pair[:, : 5 * own_width]))
    _, unit_own, rstd_own = norm_rows(x_in, vec[0], vec[1])
    x_grad = g_resid + norm_back(g_n1, unit_own, rstd_own, vec[0])
    down_grad = small[:, :LANES]
    up_grad = small[:, LOW : LOW + LANES].T
    vec_grad = small[:, LOW + LANES : LOW + LANES + 16].T
    rec_grad = join_columns(rec_own).astype(jnp.float32)
    value_grad = cm_grad[:, hidden:].T
    key_grad = cm_grad[:, :hidden]
    out_grad = tm_grad[:, :own_width].T
    proj_grad = jnp.moveaxis(tm_grad[:, own_width : 5 * own_width].reshape(-1, 4, own_width), 1, 0)
    return (
        output,
        x_grad,
        state_grad,
        vec_grad,
        proj_grad,
        out_grad,
        rec_grad,
        down_grad,
        up_grad,
        key_grad,
        value_grad,
    )


def solution(mesh):
    rows, columns = P(ALL, None), P(None, ALL)
    state = P("seg", "span", None, None)
    time_mix = P(None, "seg", "span")
    turned, straight = P("span", "seg"), P("seg", "span")
    return jax.shard_map(
        shards,
        mesh=mesh,
        in_specs=(
            rows, rows, state, columns, time_mix, turned, rows, rows, columns, straight, turned
        ),
        out_specs=(
            rows, rows, state, columns, time_mix, turned, rows, rows, columns, straight, turned
        ),
        check_vma=False,
    )
```
